32 devices in a mesh: dp: 4 (over z), seq: 2 (over x), fsdp: 4 (over y, core).
Axes of the slice: x: 2, y: 2, z: 4, core: 2. Of those that a mesh axis runs over, the one named last changes fastest.
Arguments:
- fields: bfloat16 [3, 16, 2048, 276], P(None, ('dp', 'fsdp'), 'seq'), may hold values from -6 to 6
- targets: bfloat16 [3, 16, 2048, 276], P(None, ('dp', 'fsdp'), 'seq'), may hold values from -6 to 6
- interval: int32 [3, 16], replicated, may hold values from 0 to 2
- storm_index: int32 [3, 16], replicated, may hold values from 0 to 3
- valid_count: int32 [3, 16], replicated, may hold values from 1024 to 2048, as said below
- latitude: float32 [2048], replicated, may hold values from 0.5 to 5
- storm_scale: float32 [4], replicated, may hold values from 1 to 4
- embedding: float32 [276, 1024], P(None, ('dp', 'seq', 'fsdp')), may hold values from -0.375 to 0.375
- intervals: float32 [3, 1024], P(None, ('dp', 'seq', 'fsdp')), may hold values from -6 to 6
- modulator: float32 [1024, 6144], P(('dp', 'seq', 'fsdp')), may hold values from -0.1875 to 0.1875
- projector: float32 [1024, 3072], P(('dp', 'seq', 'fsdp')), may hold values from -0.1875 to 0.1875
- combiner: float32 [1024, 1024], P(('dp', 'seq', 'fsdp')), may hold values from -1 to 1
- feedforward: float32 [2, 1024, 4096], P(None, ('dp', 'seq', 'fsdp')), may hold values from -0.125 to 0.125
- readout: float32 [1024, 276], P(('dp', 'seq', 'fsdp')), may hold values from -0.1875 to 0.1875
- vectors: float32 [7, 1024], P(None, ('dp', 'seq', 'fsdp')), may hold values from 0.1 to 1.9
- first_embedding: float32 [276, 1024], P(None, ('dp', 'seq', 'fsdp')), may hold values from -1.9073486e-06 to 1.9073486e-06
- first_intervals: float32 [3, 1024], P(None, ('dp', 'seq', 'fsdp')), may hold values from -1.9073486e-06 to 1.9073486e-06
- first_modulator: float32 [1024, 6144], P(('dp', 'seq', 'fsdp')), may hold values from -1.9073486e-06 to 1.9073486e-06
- first_projector: float32 [1024, 3072], P(('dp', 'seq', 'fsdp')), may hold values from -1.9073486e-06 to 1.9073486e-06
- first_combiner: float32 [1024, 1024], P(('dp', 'seq', 'fsdp')), may hold values from -1.9073486e-06 to 1.9073486e-06
- first_feedforward: float32 [2, 1024, 4096], P(None, ('dp', 'seq', 'fsdp')), may hold values from -1.9073486e-06 to 1.9073486e-06
- first_readout: float32 [1024, 276], P(('dp', 'seq', 'fsdp')), may hold values from -1.9073486e-06 to 1.9073486e-06
- first_vectors: float32 [7, 1024], P(None, ('dp', 'seq', 'fsdp')), may hold values from -1.9073486e-06 to 1.9073486e-06
- second_embedding: float32 [276, 1024], P(None, ('dp', 'seq', 'fsdp')), may hold values from 1.2853565e-15 to 5.141426e-15
- second_intervals: float32 [3, 1024], P(None, ('dp', 'seq', 'fsdp')), may hold values from 1.2853565e-15 to 5.141426e-15
- second_modulator: float32 [1024, 6144], P(('dp', 'seq', 'fsdp')), may hold values from 1.2853565e-15 to 5.141426e-15
- second_projector: float32 [1024, 3072], P(('dp', 'seq', 'fsdp')), may hold values from 1.2853565e-15 to 5.141426e-15
- second_combiner: float32 [1024, 1024], P(('dp', 'seq', 'fsdp')), may hold values from 1.2853565e-15 to 5.141426e-15
- second_feedforward: float32 [2, 1024, 4096], P(None, ('dp', 'seq', 'fsdp')), may hold values from 1.2853565e-15 to 5.141426e-15
- second_readout: float32 [1024, 276], P(('dp', 'seq', 'fsdp')), may hold values from 1.2853565e-15 to 5.141426e-15
- second_vectors: float32 [7, 1024], P(None, ('dp', 'seq', 'fsdp')), may hold values from 1.2853565e-15 to 5.141426e-15
Outputs:
- updated_embedding: float32 [276, 1024], P(None, ('dp', 'seq', 'fsdp'))
- updated_intervals: float32 [3, 1024], P(None, ('dp', 'seq', 'fsdp'))
- updated_modulator: float32 [1024, 6144], P(('dp', 'seq', 'fsdp'))
- updated_projector: float32 [1024, 3072], P(('dp', 'seq', 'fsdp'))
- updated_combiner: float32 [1024, 1024], P(('dp', 'seq', 'fsdp'))
- updated_feedforward: float32 [2, 1024, 4096], P(None, ('dp', 'seq', 'fsdp'))
- updated_readout: float32 [1024, 276], P(('dp', 'seq', 'fsdp'))
- updated_vectors: float32 [7, 1024], P(None, ('dp', 'seq', 'fsdp'))
- momentum_embedding: float32 [276, 1024], P(None, ('dp', 'seq', 'fsdp'))
- momentum_intervals: float32 [3, 1024], P(None, ('dp', 'seq', 'fsdp'))
- momentum_modulator: float32 [1024, 6144], P(('dp', 'seq', 'fsdp'))
- momentum_projector: float32 [1024, 3072], P(('dp', 'seq', 'fsdp'))
- momentum_combiner: float32 [1024, 1024], P(('dp', 'seq', 'fsdp'))
- momentum_feedforward: float32 [2, 1024, 4096], P(None, ('dp', 'seq', 'fsdp'))
- momentum_readout: float32 [1024, 276], P(('dp', 'seq', 'fsdp'))
- momentum_vectors: float32 [7, 1024], P(None, ('dp', 'seq', 'fsdp'))
- variance_embedding: float32 [276, 1024], P(None, ('dp', 'seq', 'fsdp'))
- variance_intervals: float32 [3, 1024], P(None, ('dp', 'seq', 'fsdp'))
- variance_modulator: float32 [1024, 6144], P(('dp', 'seq', 'fsdp'))
- variance_projector: float32 [1024, 3072], P(('dp', 'seq', 'fsdp'))
- variance_combiner: float32 [1024, 1024], P(('dp', 'seq', 'fsdp'))
- variance_feedforward: float32 [2, 1024, 4096], P(None, ('dp', 'seq', 'fsdp'))
- variance_readout: float32 [1024, 276], P(('dp', 'seq', 'fsdp'))
- variance_vectors: float32 [7, 1024], P(None, ('dp', 'seq', 'fsdp'))
- loss_total: float32 [], replicated
- loss_weight: float32 [], replicated
- gradient_norm: float32 [], replicated
The draws below stay inside these ranges and needn't reach their ends.
Inputs may be any that keep to these rules, and one draw needn't show every extreme that they name: `valid_count`: in every interval some sample counts all 2048 patches.
All inputs are finite; a program needn't handle non-finite values.
Results may differ from the reference program's by a relative error of at most 0.013.
Values may be sent and summed in bfloat16 or wider, within the bound.
A program may use at most 1.1875 GiB of HBM per device.

```python
import math
import jax
import jax.numpy as jnp
from jax import lax

D = 1024
HEADS = 16
HD = 64
FF = 4096
PIN = 276
DTK = 3
STORMS = 4
MICRO = 3
STEP = 10
PATCHES = 2048
SAMPLES = 16
NPARAM = 19449856


def draw_valid_count(key, part):
    key = jax.random.fold_in(key, 11)
    key_counts, key_rows, key_short = jax.random.split(key, 3)
    counts = jax.random.randint(key_counts, (MICRO, SAMPLES), PATCHES // 2, PATCHES + 1)
    fullest = jax.random.randint(key_rows, (MICRO,), 0, SAMPLES)
    counts = counts.at[jnp.arange(MICRO), fullest].set(PATCHES)
    offset = jax.random.randint(key_short, (), 1, max(SAMPLES, 2))
    shortest = (fullest[0] + offset) % SAMPLES
    return counts.at[0, shortest].set(PATCHES // 2).astype(jnp.int32)


def draw_latitude(key, part):
    key = jax.random.fold_in(key, 12)
    place = jnp.arange(PATCHES, dtype=jnp.float32) / max(PATCHES - 1, 1)
    rising = 1.0 + 2.0 * place
    factor = jax.random.uniform(key, (PATCHES,), jnp.float32, 0.5, 1.0)
    return rising * factor


def with_ends(drawn, rng, smallest, top_value):
    longest = drawn.shape.index(max(drawn.shape))
    spots = []
    for shift in (0, 1):
        where = [jax.random.randint(jax.random.fold_in(rng, axis), (), 0, length) for axis, length in enumerate(drawn.shape)]
        where[longest] = (where[longest] + shift) % drawn.shape[longest]
        spots.append(tuple(where))
    return drawn.at[spots[0]].set(smallest).at[spots[1]].set(top_value)


def levels(stream_key, shape, pieces, low, largest):
    def one(position, shards_of):
        draws = jax.random.uniform(jax.random.fold_in(jax.random.fold_in(stream_key, 6), position), (shards_of,), jnp.float32, low / len(pieces), largest / len(pieces))
        return jnp.repeat(jnp.exp(draws), shape[position] // shards_of).reshape((-1,) + (1,) * (len(shape) - position - 1))

    factor_of = one(*pieces[0])
    for cut in pieces[1:]:
        factor_of = factor_of * one(*cut)
    return factor_of


def scatter_about(rng, dims, scale, reach, shards=(), kind=jnp.bfloat16):
    values = jax.random.normal(rng, dims, jnp.float32) * scale
    if len(shards) > 0:
        values = levels(rng, dims, shards, -0.22, 0.18) * values
    return jnp.clip(values, min=-reach, max=reach).astype(kind)


def setup_inputs(seed: int = 0) -> dict:
    keys = jax.random.split(jax.random.key(seed), 32)
    return {
        "fields": scatter_about(keys[0], (MICRO, SAMPLES, PATCHES, PIN), 1.0, 6.0, ((1, 16), (2, 2))),
        "targets": scatter_about(keys[1], (MICRO, SAMPLES, PATCHES, PIN), 1.0, 6.0, ((1, 16), (2, 2))),
        "interval": with_ends(jax.random.randint(keys[2], (MICRO, SAMPLES), 0, DTK), jax.random.fold_in(keys[2], 1), 0, DTK - 1).astype(jnp.int32),
        "storm_index": with_ends(jax.random.randint(keys[3], (MICRO, SAMPLES), 0, STORMS), jax.random.fold_in(keys[3], 1), 0, STORMS - 1).astype(jnp.int32),
        "valid_count": draw_valid_count(jax.random.fold_in(keys[31], 71), 0),
        "latitude": draw_latitude(jax.random.fold_in(keys[31], 71), 0),
        "storm_scale": jnp.clip(jnp.exp(jax.random.uniform(keys[6], (STORMS,), jnp.float32, math.log(1.0), math.log(4.0))), 1.0, 4.0),
        "embedding": scatter_about(keys[7], (PIN, D), PIN ** -0.5, 0.375, ((1, 32),), jnp.float32),
        "intervals": scatter_about(keys[8], (DTK, D), 1.0, 6.0, ((1, 32),), jnp.float32),
        "modulator": scatter_about(keys[9], (D, 6 * D), D ** -0.5, 0.1875, ((0, 32),), jnp.float32),
        "projector": scatter_about(keys[10], (D, 3 * D), D ** -0.5, 0.1875, ((0, 32),), jnp.float32),
        "combiner": scatter_about(keys[11], (D, D), (max(D * 64 // PATCHES, 16)) ** -0.5, 1.0, ((0, 32),), jnp.float32),
        "feedforward": scatter_about(keys[12], (2, D, FF), (2 * D) ** -0.5, 0.125, ((1, 32),), jnp.float32),
        "readout": scatter_about(keys[13], (D, PIN), D ** -0.5, 0.1875, ((0, 32),), jnp.float32),
        "vectors": jnp.clip(1.0 + 0.18 * jax.random.normal(keys[14], (7, D), jnp.float32), 0.1, 1.9),
        "first_embedding": scatter_about(keys[15], (PIN, D), (0.000556 / NPARAM ** 0.5), 1.9073486328125e-06, ((1, 32),), jnp.float32),
        "first_intervals": scatter_about(keys[16], (DTK, D), (0.000556 / NPARAM ** 0.5), 1.9073486328125e-06, ((1, 32),), jnp.float32),
        "first_modulator": scatter_about(keys[17], (D, 6 * D), (0.000556 / NPARAM ** 0.5), 1.9073486328125e-06, ((0, 32),), jnp.float32),
        "first_projector": scatter_about(keys[18], (D, 3 * D), (0.000556 / NPARAM ** 0.5), 1.9073486328125e-06, ((0, 32),), jnp.float32),
        "first_combiner": scatter_about(keys[19], (D, D), (0.000556 / NPARAM ** 0.5), 1.9073486328125e-06, ((0, 32),), jnp.float32),
        "first_feedforward": scatter_about(keys[20], (2, D, FF), (0.000556 / NPARAM ** 0.5), 1.9073486328125e-06, ((1, 32),), jnp.float32),
        "first_readout": scatter_about(keys[21], (D, PIN), (0.000556 / NPARAM ** 0.5), 1.9073486328125e-06, ((0, 32),), jnp.float32),
        "first_vectors": scatter_about(keys[22], (7, D), (0.000556 / NPARAM ** 0.5), 1.9073486328125e-06, ((1, 32),), jnp.float32),
        "second_embedding": jnp.clip(1.2853565097115213e-15 + 3.856069529134564e-15 * jax.random.uniform(keys[23], (PIN, D), jnp.float32) ** levels(keys[23], (PIN, D), ((1, 32),), -0.2, 0.2), 1.2853565097115213e-15, 5.141426038846085e-15),
        "second_intervals": jnp.clip(1.2853565097115213e-15 + 3.856069529134564e-15 * jax.random.uniform(keys[24], (DTK, D), jnp.float32) ** levels(keys[24], (DTK, D), ((1, 32),), -0.2, 0.2), 1.2853565097115213e-15, 5.141426038846085e-15),
        "second_modulator": jnp.clip(1.2853565097115213e-15 + 3.856069529134564e-15 * jax.random.uniform(keys[25], (D, 6 * D), jnp.float32) ** levels(keys[25], (D, 6 * D), ((0, 32),), -0.2, 0.2), 1.2853565097115213e-15, 5.141426038846085e-15),
        "second_projector": jnp.clip(1.2853565097115213e-15 + 3.856069529134564e-15 * jax.random.uniform(keys[26], (D, 3 * D), jnp.float32) ** levels(keys[26], (D, 3 * D), ((0, 32),), -0.2, 0.2), 1.2853565097115213e-15, 5.141426038846085e-15),
        "second_combiner": jnp.clip(1.2853565097115213e-15 + 3.856069529134564e-15 * jax.random.uniform(keys[27], (D, D), jnp.float32) ** levels(keys[27], (D, D), ((0, 32),), -0.2, 0.2), 1.2853565097115213e-15, 5.141426038846085e-15),
        "second_feedforward": jnp.clip(1.2853565097115213e-15 + 3.856069529134564e-15 * jax.random.uniform(keys[28], (2, D, FF), jnp.float32) ** levels(keys[28], (2, D, FF), ((1, 32),), -0.2, 0.2), 1.2853565097115213e-15, 5.141426038846085e-15),
        "second_readout": jnp.clip(1.2853565097115213e-15 + 3.856069529134564e-15 * jax.random.uniform(keys[29], (D, PIN), jnp.float32) ** levels(keys[29], (D, PIN), ((0, 32),), -0.2, 0.2), 1.2853565097115213e-15, 5.141426038846085e-15),
        "second_vectors": jnp.clip(1.2853565097115213e-15 + 3.856069529134564e-15 * jax.random.uniform(keys[30], (7, D), jnp.float32) ** levels(keys[30], (7, D), ((1, 32),), -0.2, 0.2), 1.2853565097115213e-15, 5.141426038846085e-15),
    }


@jax.custom_vjp
def low(v):
    return lax.optimization_barrier(v.astype(jnp.bfloat16)).astype(jnp.float32)

@jax.custom_vjp
def low_back(v):
    return v

def low_keep(v):
    return (low(v), None)

def low_pass(kept, grad):
    return (grad,)

def back_keep(v):
    return (v, None)

def back_low(kept, grad):
    return (low(grad),)
low.defvjp(low_keep, low_pass)
low_back.defvjp(back_keep, back_low)
beta_one = 0.9
beta_two = 0.999
decay = 0.01
epsilon = 1e-08
clip_norm = 0.005
norm_eps = 1e-06
highest = lax.Precision.HIGHEST

def step_rates():
    factor = 1.5
    return (factor / PIN ** 0.5, factor, factor / D ** 0.5, factor / D ** 0.5, factor / max(64 * D // PATCHES, 16) ** 0.5, factor / (2 * D) ** 0.5, factor / D ** 0.5, factor)

def product(left, right):
    return jnp.dot(left, right, precision=highest)

def layer_norm(values):
    center = values - lax.optimization_barrier(jnp.mean(values, -1, keepdims=True))
    return center * lax.rsqrt(lax.optimization_barrier(jnp.mean(center * center, -1, keepdims=True)) + norm_eps)

def rounded(values):
    return low_back(low(values))

def one_head(block):
    query, keyset, valueset = block
    scores = low_back(product(query, keyset.T) * 0.125)
    probs = jax.nn.softmax(scores, axis=-1)
    return product(low(probs), valueset)

def split_heads(values):
    return values.reshape(PATCHES, HEADS, HD).transpose(1, 0, 2)

def sample_loss(params, field, target, onehot, rowweight):
    embedding, intervals, modulator, projector, combiner, feedforward, readout, vectors = params
    active = jax.nn.silu(product(onehot, intervals))
    parts = low_back(product(low(active), modulator) + vectors[:6].reshape(-1)).reshape(6, D)
    stream = low_back(product(field, embedding))
    hidden = low(layer_norm(stream) * (1.0 + parts[1]) + parts[0])
    mixed = product(hidden, projector)
    heads = (split_heads(rounded(mixed[:, :D])), split_heads(rounded(mixed[:, D:2 * D])), split_heads(rounded(mixed[:, 2 * D:])))
    attended = lax.map(jax.checkpoint(one_head), heads)
    attended = rounded(attended.transpose(1, 0, 2).reshape(PATCHES, D))
    stream = stream + parts[2] * low_back(product(attended, combiner))
    hidden = low(layer_norm(stream) * (1.0 + parts[4]) + parts[3])
    inner = low_back(product(hidden, feedforward[0]))
    activated = low(jax.nn.gelu(inner, approximate=False))
    stream = stream + parts[5] * low_back(product(activated, feedforward[1].T))
    final = low(layer_norm(stream) * vectors[6])
    predicted = low_back(product(final, readout))
    diff = predicted - target
    return jnp.sum(rowweight[:, None] * diff * diff)

def adam(master, first, second, grad, factor, step_rate):
    grad = grad * factor
    first_new = beta_one * first + (1.0 - beta_one) * grad
    second_new = beta_two * second + (1.0 - beta_two) * grad * grad
    corrected = first_new / (1.0 - beta_one ** STEP) / (jnp.sqrt(second_new / (1.0 - beta_two ** STEP)) + epsilon)
    return (master - step_rate * (corrected + decay * master), first_new, second_new)

def reference(fields, targets, interval, storm_index, valid_count, latitude, storm_scale, embedding, intervals, modulator, projector, combiner, feedforward, readout, vectors, first_embedding, first_intervals, first_modulator, first_projector, first_combiner, first_feedforward, first_readout, first_vectors, second_embedding, second_intervals, second_modulator, second_projector, second_combiner, second_feedforward, second_readout, second_vectors):
    masters = (embedding, intervals, modulator, projector, combiner, feedforward, readout, vectors)
    firsts = (first_embedding, first_intervals, first_modulator, first_projector, first_combiner, first_feedforward, first_readout, first_vectors)
    seconds = (second_embedding, second_intervals, second_modulator, second_projector, second_combiner, second_feedforward, second_readout, second_vectors)
    place = jnp.arange(PATCHES, dtype=jnp.int32)
    mask = (place[None, None, :] >= PATCHES - valid_count[:, :, None]).astype(jnp.float32)
    rowweights = latitude[None, None, :] * storm_scale[storm_index][:, :, None] * mask
    total_weight = PIN * jnp.sum(rowweights)
    onehots = (interval[:, :, None] == jnp.arange(DTK, dtype=jnp.int32)).astype(jnp.float32)
    data = (fields.astype(jnp.float32).reshape(MICRO * SAMPLES, PATCHES, PIN), targets.astype(jnp.float32).reshape(MICRO * SAMPLES, PATCHES, PIN), onehots.reshape(MICRO * SAMPLES, DTK), rowweights.reshape(MICRO * SAMPLES, PATCHES))

    def objective(*weights):
        params = tuple((low(w) for w in weights))

        def accumulate(total, item):
            return (total + jax.checkpoint(sample_loss)(params, *item), None)
        total, unused = lax.scan(accumulate, jnp.zeros((), jnp.float32), data)
        return (total / total_weight, total)
    value, pullback, loss_total = jax.vjp(objective, *masters, has_aux=True)
    grads = pullback(jnp.ones((), jnp.float32))
    squares = sum((jnp.sum(g * g) for g in grads))
    norm = jnp.sqrt(squares)
    factor = clip_norm / jnp.maximum(norm, clip_norm)
    results = [adam(w, m, v, g, factor, r) for w, m, v, g, r in zip(masters, firsts, seconds, grads, step_rates())]
    news = tuple((r[0] for r in results))
    moms = tuple((r[1] for r in results))
    varis = tuple((r[2] for r in results))
    return (news[0], news[1], news[2], news[3], news[4], news[5], news[6], news[7], moms[0], moms[1], moms[2], moms[3], moms[4], moms[5], moms[6], moms[7], varis[0], varis[1], varis[2], varis[3], varis[4], varis[5], varis[6], varis[7], loss_total, total_weight, norm)
```

```python
import functools

import jax
import jax.numpy as jnp
from jax import lax
from jax.experimental import pallas as pl
from jax.experimental.pallas import tpu as pltpu
from jax.sharding import PartitionSpec as P

D = 1024
HD = 64
PIN = 276
WIDE = 384
DTK = 3
STEP = 10
PATCHES = 2048
ALL = ("dp", "seq", "fsdp")

beta_one = 0.9
beta_two = 0.999
decay = 0.01
epsilon = 1e-08
clip_norm = 0.005
norm_eps = 1e-06
bf16 = jnp.bfloat16
f32 = jnp.float32
LN2 = 0.6931471805599453
QUERY_SCALE = 0.125 / LN2
VMEM_BYTES = 60 * 2**20
ERF = (
    0.7978822138768258,
    0.03634467259297056,
    -4.4877727054425946e-05,
    -5.036405881894902e-05,
    3.0986869577148946e-06,
    -6.638614747540505e-08,
)
ERF_END = 21.16


def step_rates():
    factor = 1.5
    return (
        factor / PIN**0.5,
        factor,
        factor / D**0.5,
        factor / D**0.5,
        factor / max(64 * D // PATCHES, 16) ** 0.5,
        factor / (2 * D) ** 0.5,
        factor / D**0.5,
        factor,
    )


def contract(left, right, left_dim, right_dim):
    return lax.dot_general(
        left, right, (((left_dim,), (right_dim,)), ((), ())), preferred_element_type=f32
    )


def layer_norm(values):
    center = values - jnp.mean(values, -1, keepdims=True)
    inverse = lax.rsqrt(jnp.mean(center * center, -1, keepdims=True) + norm_eps)
    return (center * inverse, inverse)


def norm_back(upstream, normed, inverse):
    return inverse * (
        upstream
        - jnp.mean(upstream, -1, keepdims=True)
        - normed * jnp.mean(upstream * normed, -1, keepdims=True)
    )


def column_sum(values):
    return jnp.sum(values, 0, keepdims=True)


def gelu_pair(inner):
    square = inner * inner
    bounded = jnp.minimum(square, ERF_END)
    series = jnp.full_like(inner, ERF[-1])
    for coefficient in ERF[-2::-1]:
        series = series * bounded + coefficient
    normal = 0.5 + 0.5 * jnp.tanh(inner * series)
    density = jnp.exp2(square * (-0.5 / LN2)) * 0.3989422804014327
    return (inner * normal, normal + inner * density)


def resident(shape):
    return pl.BlockSpec(shape, lambda *place: (0,) * len(shape), pipeline_mode=pl.Buffered(1))


def entry_kernel(query_blocks, field, embed, weight, mod, stream, hidden, mixed):
    width = embed.shape[0]
    stream_zero = contract(field[...], embed[...], 1, 1)
    stream[...] = stream_zero
    normed, unused = layer_norm(stream_zero)
    low = (normed * (1.0 + mod[1:2, :]) + mod[0:1, :]).astype(bf16)
    hidden[...] = low
    for part in (1, 2):
        columns = pl.ds(part * width, width)
        mixed[:, columns] = contract(low, weight[:, columns], 1, 0).astype(bf16)

    @pl.when(pl.program_id(0) < query_blocks)
    def _():
        queries = contract(low, weight[:, 0:width], 1, 0)
        mixed[:, 0:width] = (queries * QUERY_SCALE).astype(bf16)


def entry(fields, embed, weight, mod, block, query_rows, unit_of):
    rows, pieces = fields.shape
    width = embed.shape[0]
    by_row = lambda columns: pl.BlockSpec((block, columns), lambda i: (i, 0))
    return pl.pallas_call(
        functools.partial(entry_kernel, query_rows // block),
        grid=(rows // block,),
        in_specs=[
            by_row(pieces),
            resident(embed.shape),
            resident(weight.shape),
            pl.BlockSpec((None,) + mod.shape[1:], lambda i: (unit_of(i), 0, 0)),
        ],
        out_specs=[by_row(width), by_row(width), by_row(3 * width)],
        out_shape=[
            jax.ShapeDtypeStruct((rows, width), f32),
            jax.ShapeDtypeStruct((rows, width), bf16),
            jax.ShapeDtypeStruct((rows, 3 * width), bf16),
        ],
        compiler_params=pltpu.CompilerParams(vmem_limit_bytes=VMEM_BYTES),
        name="entry",
    )(fields, embed, weight, mod)


def attend_kernel(sub, query, key, value, out, kept, inverse, value_t, key_one, stats):
    block, keys = query.shape[0], key.shape[0]
    zero, one = jnp.zeros((), bf16), jnp.ones((), bf16)

    @pl.when(pl.program_id(1) == 0)
    def _():
        turned = jnp.transpose(value[...])
        first_rows = lax.broadcasted_iota(jnp.int32, (2 * HD, keys), 0) < HD
        value_t[0] = jnp.where(first_rows, turned, one)
        value_t[1] = jnp.where(first_rows, one, turned)
        first_lanes = lax.broadcasted_iota(jnp.int32, (keys, 2 * HD), 1) < HD
        both = key[...]
        key_one[0] = jnp.where(first_lanes, both, one)
        key_one[1] = jnp.where(first_lanes, one, both)
        wide = both.astype(f32)
        mean = jnp.mean(wide, 0, keepdims=True)
        spread = (wide - mean) * (wide - mean)
        stats[0:1] = mean
        for head in range(2):
            mine = first_lanes if head == 0 else jnp.logical_not(first_lanes)
            size = jnp.sum(jnp.where(mine, spread, 0.0), 1, keepdims=True)
            far = jnp.max(size, 0, keepdims=True)
            stats[1 + head : 2 + head] = jnp.broadcast_to(0.5 * jnp.sqrt(far), (1, 2 * HD))

    lanes = lax.broadcasted_iota(jnp.int32, (block, 2 * HD), 1)
    wide = query[...].astype(f32)
    level = wide * stats[0:1]
    shifts, reaches = [], []
    for head in range(2):
        mine = (lanes < HD) if head == 0 else (lanes >= HD)
        length = jnp.sqrt(jnp.sum(jnp.where(mine, wide * wide, 0.0), 1, keepdims=True))
        reach = length * stats[1 + head : 2 + head, 0:1]
        shifts.append(jnp.sum(jnp.where(mine, level, 0.0), 1, keepdims=True) + reach)
        reaches.append(jnp.max(reach))
    near = jnp.maximum(reaches[0], reaches[1]) <= 60.0
    upper = lax.broadcasted_iota(jnp.int32, (2 * HD, sub), 0) < HD

    def run(exact):
        for part in range(block // sub):
            rows = pl.ds(part * sub, sub)
            results = []
            for head in range(2):
                spot = lanes[0:sub]
                mine = (spot < HD) if head == 0 else (spot >= HD)
                if exact:
                    moved = jnp.where(mine, query[rows, :], zero)
                    scores = contract(key_one[head], moved, 1, 1)
                    scores = scores - jnp.max(scores, 0, keepdims=True)
                else:
                    shift = (-shifts[head][part * sub : part * sub + sub]).astype(bf16)
                    free = HD if head == 0 else 0
                    rest = jnp.where(spot == free, shift, zero)
                    moved = jnp.where(mine, query[rows, :], rest)
                    scores = contract(key_one[head], moved, 1, 1)
                weights = jnp.exp2(scores).astype(bf16)
                kept[head, :, rows] = weights
                results.append(contract(value_t[head], weights, 1, 0))
            total = jnp.where(
                upper, pltpu.roll(results[0], HD, 0), pltpu.roll(results[1], HD, 0)
            )
            above = 1.0 / total
            mean = jnp.where(upper, results[0], results[1]) * above
            out[rows, :] = jnp.transpose(mean).astype(bf16)
            inverse[0:1, rows] = above[0:1]
            inverse[1:2, rows] = above[HD : HD + 1]

    @pl.when(near)
    def _():
        run(False)

    @pl.when(jnp.logical_not(near))
    def _():
        run(True)


def attend(queries, memory, places, block, sub, count, keys, width):
    pairs = width // (2 * HD)
    query_at, key_at, key_column, value_column = places
    return pl.pallas_call(
        functools.partial(attend_kernel, sub),
        grid=(pairs, count // block),
        in_specs=[
            pl.BlockSpec((block, 2 * HD), lambda h, i: (query_at // block + i, h)),
            pl.BlockSpec((keys, 2 * HD), lambda h, i: (key_at // keys, key_column * pairs + h)),
            pl.BlockSpec((keys, 2 * HD), lambda h, i: (key_at // keys, value_column * pairs + h)),
        ],
        out_specs=[
            pl.BlockSpec((block, 2 * HD), lambda h, i: (i, h)),
            pl.BlockSpec((None, None, 2, keys, block), lambda h, i: (h, i, 0, 0, 0)),
            pl.BlockSpec((None, 2, block), lambda h, i: (h, 0, i)),
        ],
        out_shape=[
            jax.ShapeDtypeStruct((count, width), bf16),
            jax.ShapeDtypeStruct((pairs, count // block, 2, keys, block), bf16),
            jax.ShapeDtypeStruct((pairs, 2, count), f32),
        ],
        scratch_shapes=[
            pltpu.VMEM((2, 2 * HD, keys), bf16),
            pltpu.VMEM((2, keys, 2 * HD), bf16),
            pltpu.VMEM((8, 2 * HD), f32),
        ],
        compiler_params=pltpu.CompilerParams(vmem_limit_bytes=VMEM_BYTES),
        name="attend",
    )(queries, memory, memory)


def attend_back_kernel(
    sub, query, key, value, grad, out, kept, inverse,
    grad_query, grad_key, grad_value, key_t, value_one, key_sum, value_sum,
):
    block, keys = query.shape[0], key.shape[0]
    step, steps = pl.program_id(1), pl.num_programs(1)
    zero = jnp.zeros((), bf16)

    @pl.when(step == 0)
    def _():
        first_rows = lax.broadcasted_iota(jnp.int32, (2 * HD, keys), 0) < HD
        turned = jnp.transpose(key[...])
        key_t[0] = jnp.where(first_rows, turned, zero)
        key_t[1] = jnp.where(first_rows, zero, turned)
        first_lanes = lax.broadcasted_iota(jnp.int32, (keys, 2 * HD), 1) < HD
        minus = jnp.full((), -1.0, bf16)
        value_one[0] = jnp.where(first_lanes, value[...], minus)
        value_one[1] = jnp.where(first_lanes, minus, value[...])
        key_sum[...] = jnp.zeros_like(key_sum)
        value_sum[...] = jnp.zeros_like(value_sum)

    lanes = lax.broadcasted_iota(jnp.int32, (sub, 2 * HD), 1)
    places = lax.broadcasted_iota(jnp.int32, (2 * HD, sub), 0)
    upper = places < HD
    for part in range(block // sub):
        rows = pl.ds(part * sub, sub)
        above = jnp.where(upper, inverse[0:1, rows], inverse[1:2, rows])
        scaled = (jnp.transpose(grad[rows, :].astype(f32)) * above).astype(bf16)
        product = scaled.astype(f32) * jnp.transpose(out[rows, :].astype(f32))
        natural = jnp.transpose(scaled)
        queries = query[rows, :]
        turned = None
        for head in range(2):
            delta = jnp.sum(product[HD * head : HD * head + HD], 0, keepdims=True)
            high = delta.astype(bf16)
            rest = (delta - high.astype(f32)).astype(bf16)
            free = HD if head == 0 else 0
            mine = upper if head == 0 else jnp.logical_not(upper)
            extra = jnp.where(places == free, high, jnp.where(places == free + 1, rest, zero))
            grad_probs = contract(value_one[head], jnp.where(mine, scaled, extra), 1, 0)
            weights = kept[head, :, rows]
            grad_scores = grad_probs.astype(bf16) * weights
            own = (lanes < HD) if head == 0 else (lanes >= HD)
            value_sum[...] += contract(weights, jnp.where(own, natural, zero), 1, 0)
            key_sum[...] += contract(grad_scores, jnp.where(own, queries, zero), 1, 0)
            term = contract(key_t[head], grad_scores, 1, 0)
            turned = term if turned is None else turned + term
        grad_query[rows, :] = (jnp.transpose(turned) * 0.125).astype(bf16)

    @pl.when(step == steps - 1)
    def _():
        grad_key[...] = (key_sum[...] * LN2).astype(bf16)
        grad_value[...] = value_sum[...].astype(bf16)


def attend_back(queries, memory, grads, out, kept, inverse, places, block, sub, count, keys, width):
    pairs = width // (2 * HD)
    query_at, key_at, key_column, value_column = places
    return pl.pallas_call(
        functools.partial(attend_back_kernel, sub),
        grid=(pairs, count // block),
        in_specs=[
            pl.BlockSpec((block, 2 * HD), lambda h, i: (query_at // block + i, h)),
            pl.BlockSpec((keys, 2 * HD), lambda h, i: (key_at // keys, key_column * pairs + h)),
            pl.BlockSpec((keys, 2 * HD), lambda h, i: (key_at // keys, value_column * pairs + h)),
            pl.BlockSpec((block, 2 * HD), lambda h, i: (query_at // block + i, h)),
            pl.BlockSpec((block, 2 * HD), lambda h, i: (i, h)),
            pl.BlockSpec((None, None, 2, keys, block), lambda h, i: (h, i, 0, 0, 0)),
            pl.BlockSpec((None, 2, block), lambda h, i: (h, 0, i)),
        ],
        out_specs=[
            pl.BlockSpec((block, 2 * HD), lambda h, i: (i, h)),
            pl.BlockSpec((keys, 2 * HD), lambda h, i: (0, h)),
            pl.BlockSpec((keys, 2 * HD), lambda h, i: (0, h)),
        ],
        out_shape=[
            jax.ShapeDtypeStruct((count, width), bf16),
            jax.ShapeDtypeStruct((keys, width), bf16),
            jax.ShapeDtypeStruct((keys, width), bf16),
        ],
        scratch_shapes=[
            pltpu.VMEM((2, 2 * HD, keys), bf16),
            pltpu.VMEM((2, keys, 2 * HD), bf16),
            pltpu.VMEM((keys, 2 * HD), f32),
            pltpu.VMEM((keys, 2 * HD), f32),
        ],
        compiler_params=pltpu.CompilerParams(vmem_limit_bytes=VMEM_BYTES),
        name="attend_back",
    )(queries, memory, memory, grads, out, kept, inverse)


def middle_kernel(
    attended, stream, target, weight_rows, mod, combine, first, second, read,
    hidden, active, grad_two, grad_inner, final, grad_read, grad_one, grad_attended, grad_stream,
    sums, losses, slopes,
):
    width, spread = first.shape
    tiles = [pl.ds(start, width) for start in range(0, spread, width)]
    gate_a, shift_b, scale_b = mod[2:3, :], mod[3:4, :], mod[4:5, :]
    gate_b, gain = mod[5:6, :], mod[6:7, :]
    branch_a = contract(attended[...], combine[...], 1, 0)
    stream_one = stream[...] + gate_a * branch_a
    norm_b, inverse_b = layer_norm(stream_one)
    low = (norm_b * (1.0 + scale_b) + shift_b).astype(bf16)
    hidden[...] = low
    branch_b = None
    for tile in tiles:
        value, slope = gelu_pair(contract(low, first[:, tile], 1, 0))
        value = value.astype(bf16)
        active[:, tile] = value
        slopes[:, tile] = slope.astype(bf16)
        term = contract(value, second[:, tile], 1, 1)
        branch_b = term if branch_b is None else branch_b + term
    norm_c, inverse_c = layer_norm(stream_one + gate_b * branch_b)
    last = (norm_c * gain).astype(bf16)
    final[...] = last
    diff = contract(last, read[...], 1, 0) - target[...].astype(f32)
    losses[...] = jnp.broadcast_to(column_sum(weight_rows[:, 0:1] * diff * diff), losses.shape)
    grad_low = (weight_rows[:, 1:2] * diff).astype(bf16)
    grad_read[...] = grad_low
    grad_final = contract(grad_low, read[...], 1, 1)
    sums[6:7, :] = column_sum(grad_final * norm_c)
    grad = norm_back(grad_final * gain, norm_c, inverse_c)
    sums[5:6, :] = column_sum(grad * branch_b)
    back = (grad * gate_b).astype(bf16)
    grad_two[...] = back
    grad_hidden = None
    for tile in tiles:
        inner = contract(back, second[:, tile], 1, 0)
        inner = (inner * slopes[:, tile].astype(f32)).astype(bf16)
        grad_inner[:, tile] = inner
        term = contract(inner, first[:, tile], 1, 1)
        grad_hidden = term if grad_hidden is None else grad_hidden + term
    sums[3:4, :] = column_sum(grad_hidden)
    sums[4:5, :] = column_sum(grad_hidden * norm_b)
    grad = grad + norm_back(grad_hidden * (1.0 + scale_b), norm_b, inverse_b)
    grad_stream[...] = grad
    sums[2:3, :] = column_sum(grad * branch_a)
    back = (grad * gate_a).astype(bf16)
    grad_one[...] = back
    grad_attended[...] = contract(back, combine[...], 1, 1).astype(bf16)
    sums[0:2, :] = jnp.zeros((2, width), f32)
    sums[7:8, :] = jnp.zeros((1, width), f32)


def middle(attended, stream, target, weight_rows, mod, combine, first, second, read, block, unit_of):
    rows, width = attended.shape
    spread, pieces = first.shape[1], read.shape[1]
    blocks = rows // block
    by_row = lambda columns: pl.BlockSpec((block, columns), lambda i: (i, 0))
    shape = lambda columns, kind: jax.ShapeDtypeStruct((rows, columns), kind)
    outs = (
        (width, bf16), (spread, bf16), (width, bf16), (spread, bf16), (width, bf16), (pieces, bf16),
        (width, bf16), (width, bf16), (width, f32),
    )
    return pl.pallas_call(
        middle_kernel,
        grid=(blocks,),
        in_specs=[
            by_row(width),
            by_row(width),
            by_row(pieces),
            by_row(2),
            pl.BlockSpec((None,) + mod.shape[1:], lambda i: (unit_of(i), 0, 0)),
            resident(combine.shape),
            resident(first.shape),
            resident(second.shape),
            resident(read.shape),
        ],
        out_specs=[by_row(columns) for columns, kind in outs]
        + [
            pl.BlockSpec((None, 8, width), lambda i: (i, 0, 0)),
            pl.BlockSpec((None, 8, pieces), lambda i: (i, 0, 0)),
        ],
        out_shape=[shape(columns, kind) for columns, kind in outs]
        + [
            jax.ShapeDtypeStruct((blocks, 8, width), f32),
            jax.ShapeDtypeStruct((blocks, 8, pieces), f32),
        ],
        scratch_shapes=[pltpu.VMEM((block, spread), bf16)],
        compiler_params=pltpu.CompilerParams(vmem_limit_bytes=VMEM_BYTES),
        name="middle",
    )(attended, stream, target, weight_rows, mod, combine, first, second, read)


def leave_kernel(query_blocks, grad_query, grad_memory, stream, grad_stream, weight, mod, out, sums, held):
    width = stream.shape[1]
    asks = pl.program_id(0) < query_blocks
    grad_hidden = contract(grad_memory[...], weight[:, width:], 1, 1)
    held[...] = grad_hidden

    @pl.when(asks)
    def _():
        held[...] += contract(grad_query[...], weight[:, 0:width], 1, 1)

    normed, inverse = layer_norm(stream[...])
    grad_hidden = held[...]
    sums[0:1, :] = column_sum(grad_hidden)
    sums[1:2, :] = column_sum(grad_hidden * normed)
    sums[2:8, :] = jnp.zeros((6, width), f32)
    grad = norm_back(grad_hidden * (1.0 + mod[1:2, :]), normed, inverse)
    grad = grad + jnp.where(asks, grad_stream[...], 0.0)
    out[...] = grad.astype(bf16)


def leave(grad_query, grad_memory, stream, grad_stream, weight, mod, block, unit_of):
    rows, width = stream.shape
    asking = grad_query.shape[0] // block
    blocks = rows // block
    by_row = lambda columns: pl.BlockSpec((block, columns), lambda i: (i, 0))
    asked = pl.BlockSpec((block, width), lambda i: (jnp.minimum(i, asking - 1), 0))
    return pl.pallas_call(
        functools.partial(leave_kernel, asking),
        grid=(blocks,),
        in_specs=[
            asked,
            by_row(2 * width),
            by_row(width),
            asked,
            resident(weight.shape),
            pl.BlockSpec((None,) + mod.shape[1:], lambda i: (unit_of(i), 0, 0)),
        ],
        out_specs=[by_row(width), pl.BlockSpec((None, 8, width), lambda i: (i, 0, 0))],
        out_shape=[
            jax.ShapeDtypeStruct((rows, width), bf16),
            jax.ShapeDtypeStruct((blocks, 8, width), f32),
        ],
        scratch_shapes=[pltpu.VMEM((block, width), f32)],
        compiler_params=pltpu.CompilerParams(vmem_limit_bytes=VMEM_BYTES),
        name="leave",
    )(grad_query, grad_memory, stream, grad_stream, weight, mod)


def adam(master, first, second, grad, factor, step_rate):
    grad = grad * factor
    first_new = beta_one * first + (1.0 - beta_one) * grad
    second_new = beta_two * second + (1.0 - beta_two) * grad * grad
    corrected = (
        first_new
        / (1.0 - beta_one**STEP)
        / (jnp.sqrt(second_new / (1.0 - beta_two**STEP)) + epsilon)
    )
    return (master - step_rate * (corrected + decay * master), first_new, second_new)


def largest(limit, *sizes):
    block = limit
    while any(size % block for size in sizes):
        block //= 2
    return block


def body(ways, *args):
    fields, targets, interval, storm_index, valid_count, latitude, storm_scale = args[:7]
    masters, firsts, seconds = args[7:15], args[15:23], args[23:31]
    embedding, intervals, modulator, projector, combiner, feedforward, readout, vectors = masters
    micros, samples_dev, part, pieces = fields.shape
    patches = latitude.shape[0]
    units = micros * samples_dev
    share, width = projector.shape[0], projector.shape[1] // 3
    place = lax.axis_index("seq")
    device = lax.axis_index(ALL)
    sample_start = lax.axis_index(("dp", "fsdp")) * samples_dev
    ring = [(index, 1 - index) for index in range(2)]
    alone = units // 2 if ways == 2 else 0
    shared = units - ways * alone
    have = alone + shared

    everywhere = jnp.arange(patches, dtype=jnp.int32)
    mask = (everywhere[None, None, :] >= patches - valid_count[:, :, None]).astype(f32)
    levels = jnp.arange(storm_scale.shape[0], dtype=jnp.int32)
    storms = jnp.sum(jnp.where(storm_index[:, :, None] == levels, storm_scale, 0.0), -1)
    row_weights = latitude[None, None, :] * storms[:, :, None] * mask
    total_weight = pieces * jnp.sum(row_weights)

    def local(values):
        cut = lax.dynamic_slice_in_dim(values, sample_start, samples_dev, 1)
        cut = cut.reshape((units,) + values.shape[2:])
        mine = [lax.dynamic_slice_in_dim(cut, place * alone, alone, 0)] if alone else []
        return jnp.concatenate(mine + [cut[ways * alone :]], 0)

    kinds = local(interval)
    weights_unit = jnp.roll(local(row_weights), -place * part, 1)
    weights_rows = jnp.concatenate(
        [weights_unit[:alone].reshape(-1), weights_unit[alone:, :part].reshape(-1)]
    )
    weight_rows = jnp.stack([weights_rows, weights_rows * (2.0 / total_weight)], 1)

    def widen(values):
        flat = values.reshape(units, part, pieces)
        return jnp.pad(flat, ((0, 0), (0, 0), (0, WIDE - pieces)))

    own, goal = widen(fields), widen(targets)
    if alone:
        away = (1 - place) * alone
        cut = lambda values, start: lax.dynamic_slice_in_dim(values, start, alone, 0)
        sent = jnp.concatenate([cut(own, away), own[2 * alone :]], 0)
        came = lax.ppermute(sent, "seq", ring)
        goal_came = lax.ppermute(cut(goal, away), "seq", ring)
        whole = jnp.concatenate([cut(own, place * alone), came[:alone]], 1)
        goal_whole = jnp.concatenate([cut(goal, place * alone), goal_came], 1)
        rows = [whole, own[2 * alone :], came[alone:]]
        goals = [goal_whole, goal[2 * alone :]]
    elif ways == 1:
        rows, goals = [own], [goal]
    else:
        everyone = lax.all_gather(own, "seq", axis=1, tiled=True)
        rows = [own, jnp.roll(everyone, -place * part, 1)[:, part:]]
        goals = [goal]
    flatten = lambda parts: jnp.concatenate([piece.reshape(-1, WIDE) for piece in parts], 0)
    all_rows, goal_rows = flatten(rows), flatten(goals)
    asking = (alone * ways + shared) * part

    def unit_of(block):
        whole_blocks = alone * patches // block
        own_blocks = shared * part // block
        other = max((patches - part) // block, 1)

        def at(i):
            late = alone + (i - whole_blocks) // (part // block)
            later = alone + (i - whole_blocks - own_blocks) // other
            late = jnp.where(i < whole_blocks + own_blocks, late, later)
            return jnp.where(i < whole_blocks, i // (patches // block), late)

        return at

    low = [master.astype(bf16) for master in masters]
    step_vec = low[1].astype(f32)
    active = jax.nn.silu(step_vec)
    active_low = active.astype(bf16)
    table = contract(active_low, low[2], 1, 0)
    spread_vectors = lax.dynamic_update_slice(
        jnp.zeros((7, width), f32), low[7].astype(f32), (0, device * share)
    )
    carried = lax.psum(jnp.concatenate([table.reshape(-1), spread_vectors.reshape(-1)]), ALL)
    table = carried[: table.size].reshape(DTK, 6, width)
    all_vectors = carried[table.size :].reshape(7, width)
    table = table + all_vectors[None, :6]
    chosen = sum(jnp.where(kinds[:, None, None] == kind, table[kind], 0.0) for kind in range(DTK))
    gain = jnp.broadcast_to(all_vectors[6], (have, 1, width))
    mod = jnp.concatenate([chosen, gain, jnp.zeros((have, 1, width), f32)], 1)

    gather = lambda values: lax.all_gather(values, ALL, axis=0, tiled=True)
    wide_readout = jnp.pad(low[6], ((0, 0), (0, WIDE - pieces)))
    embed = gather(jnp.pad(low[0].T, ((0, 0), (0, WIDE - pieces))))
    project = gather(low[3])
    combine = gather(low[4])
    first = gather(low[5][0])
    second = gather(low[5][1])
    read = gather(wide_readout)

    block = largest(512, part)
    stream, hidden_a, mixed = entry(all_rows, embed, project, mod, block, asking, unit_of(block))

    calls = []
    for unit in range(have):
        if unit < alone:
            calls.append((unit * patches, patches, mixed, unit * patches, 1, 2))
        else:
            start = alone * patches + (unit - alone) * part
            behind = asking + (unit - alone) * (patches - part)
            if shared == 1 and start % patches == 0:
                calls.append((start, part, mixed, start, 1, 2))
            else:
                pieces_of = [mixed[start : start + part, width:]]
                pieces_of.append(mixed[behind : behind + patches - part, width:])
                calls.append((start, part, jnp.concatenate(pieces_of, 0), 0, 0, 1))
    attended, saved = [], []
    for start, count, memory, key_at, key_column, value_column in calls:
        block = largest(2048, count, start if start else count)
        where = (start, key_at, key_column, value_column)
        sub = min(block, 1024)
        out, kept, inverse = attend(mixed, memory, where, block, sub, count, patches, width)
        attended.append(out)
        saved.append((out, kept, inverse, where, block))
    attended_rows = jnp.concatenate(attended, 0)

    block = largest(256, part)
    (
        hidden_b, activated, grad_two, grad_inner, final, grad_read, grad_one, grad_attended,
        grad_stream, sums, losses,
    ) = middle(
        attended_rows, stream[:asking], goal_rows, weight_rows, mod, combine, first, second, read, block,
        unit_of(block),
    )
    units_mid = [unit_of(block)(jnp.int32(i)) for i in range(sums.shape[0])]
    loss_local = jnp.sum(losses[:, 0, :])

    scatter = lambda values: lax.psum_scatter(values, ALL, scatter_dimension=0, tiled=True)
    summed = lambda left, right: contract(left, right, 0, 0).astype(bf16)
    shard_first = scatter(summed(hidden_b, grad_inner)).astype(f32)
    shard_second = scatter(summed(grad_two, activated)).astype(f32)
    shard_combine = scatter(summed(attended_rows, grad_one)).astype(f32)
    shard_read = scatter(summed(final, grad_read)).astype(f32)

    grad_queries, grad_memories = [], []
    for (start, count, memory, unused_a, unused_b, unused_c), (out, kept, inverse, where, block) in zip(
        calls, saved
    ):
        grad_query, grad_key, grad_value = attend_back(
            mixed, memory, grad_attended, out, kept, inverse, where, block, min(block, 256), count,
            patches, width,
        )
        grad_queries.append(grad_query)
        grad_memories.append(jnp.concatenate([grad_key, grad_value], 1))
    grad_query_rows = jnp.concatenate(grad_queries, 0)
    grad_memory_rows = jnp.concatenate(
        grad_memories[:alone]
        + [values[:part] for values in grad_memories[alone:]]
        + [values[part:] for values in grad_memories[alone:]],
        0,
    )
    shard_project = scatter(
        jnp.concatenate(
            [
                summed(hidden_a[:asking], grad_query_rows),
                summed(hidden_a, grad_memory_rows),
            ],
            1,
        )
    ).astype(f32)
    block = largest(512, part)
    grad_zero, sums_a = leave(
        grad_query_rows, grad_memory_rows, stream, grad_stream, project, mod, block, unit_of(block)
    )
    units_out = [unit_of(block)(jnp.int32(i)) for i in range(sums_a.shape[0])]
    shard_embed = scatter(summed(grad_zero, all_rows)).astype(f32)

    by_block = jnp.concatenate([sums, sums_a], 0)
    kind_block = kinds[jnp.stack(units_mid + units_out)]
    grad_table = jnp.stack(
        [
            jnp.sum(jnp.where((kind_block == kind)[:, None, None], by_block, 0.0), 0)
            for kind in range(DTK)
        ]
    )
    carried = lax.psum(
        jnp.concatenate([grad_table[:, :7].reshape(-1), loss_local.reshape(1)]), ALL
    )
    loss_total = carried[-1]
    grad_table = carried[:-1].reshape(DTK, 7, width)
    grad_mod = grad_table[:, :6].reshape(DTK, 6 * width)
    shard_vectors = lax.dynamic_slice_in_dim(jnp.sum(grad_table, 0), device * share, share, 1)
    active_wide = active_low.astype(f32)
    shard_modulator = sum(
        active_wide[kind][:, None] * grad_mod[kind][None, :] for kind in range(DTK)
    )
    grad_active = jnp.stack(
        [jnp.sum(low[2].astype(f32) * grad_mod[kind][None, :], 1) for kind in range(DTK)]
    )
    unused, silu_back = jax.vjp(jax.nn.silu, step_vec)
    shard_intervals = silu_back(grad_active)[0]

    shards = (
        shard_embed[:, :pieces].T,
        shard_intervals,
        shard_modulator,
        shard_project,
        shard_combine,
        jnp.stack([shard_first, shard_second]),
        shard_read[:, :pieces],
        shard_vectors,
    )
    squares = lax.psum(sum(jnp.sum(grad * grad) for grad in shards), ALL)
    norm = jnp.sqrt(squares)
    factor = clip_norm / jnp.maximum(norm, clip_norm)
    results = [
        adam(master, first_moment, second_moment, grad, factor, rate)
        for master, first_moment, second_moment, grad, rate in zip(
            masters, firsts, seconds, shards, step_rates()
        )
    ]
    return tuple(result[index] for index in range(3) for result in results) + (
        loss_total,
        total_weight,
        norm,
    )


def solution(mesh):
    data = P(None, ("dp", "fsdp"), "seq", None)
    columns, rows = P(None, ALL), P(ALL, None)
    weights = (columns, columns, rows, rows, rows, P(None, ALL, None), rows, columns)
    return jax.shard_map(
        functools.partial(body, mesh.shape["seq"]),
        mesh=mesh,
        in_specs=(data, data) + (P(),) * 5 + weights * 3,
        out_specs=weights * 3 + (P(),) * 3,
        check_vma=False,
    )
```

```python
import functools

import jax
import jax.numpy as jnp
from jax import lax
from jax.experimental import pallas as pl
from jax.experimental.pallas import tpu as pltpu
from jax.sharding import PartitionSpec as P

D = 1024
HD = 64
PIN = 276
WIDE = 384
DTK = 3
STEP = 10
PATCHES = 2048
ALL = ("dp", "seq", "fsdp")

beta_one = 0.9
beta_two = 0.999
decay = 0.01
epsilon = 1e-08
clip_norm = 0.005
norm_eps = 1e-06
bf16 = jnp.bfloat16
f32 = jnp.float32
LN2 = 0.6931471805599453
QUERY_SCALE = 0.125 / LN2
VMEM_BYTES = 60 * 2**20
ERF = (
    0.7978822138768258,
    0.03634467259297056,
    -4.4877727054425946e-05,
    -5.036405881894902e-05,
    3.0986869577148946e-06,
    -6.638614747540505e-08,
)
ERF_END = 21.16


def step_rates():
    factor = 1.5
    return (
        factor / PIN**0.5,
        factor,
        factor / D**0.5,
        factor / D**0.5,
        factor / max(64 * D // PATCHES, 16) ** 0.5,
        factor / (2 * D) ** 0.5,
        factor / D**0.5,
        factor,
    )


def contract(left, right, left_dim, right_dim):
    return lax.dot_general(
        left, right, (((left_dim,), (right_dim,)), ((), ())), preferred_element_type=f32
    )


def layer_norm(values):
    center = values - jnp.mean(values, -1, keepdims=True)
    inverse = lax.rsqrt(jnp.mean(center * center, -1, keepdims=True) + norm_eps)
    return (center * inverse, inverse)


def norm_back(upstream, normed, inverse):
    return inverse * (
        upstream
        - jnp.mean(upstream, -1, keepdims=True)
        - normed * jnp.mean(upstream * normed, -1, keepdims=True)
    )


def column_sum(values):
    return jnp.sum(values, 0, keepdims=True)


def gelu_pair(inner):
    square = inner * inner
    bounded = jnp.minimum(square, ERF_END)
    series = jnp.full_like(inner, ERF[-1])
    for coefficient in ERF[-2::-1]:
        series = series * bounded + coefficient
    normal = 0.5 + 0.5 * jnp.tanh(inner * series)
    density = jnp.exp2(square * (-0.5 / LN2)) * 0.3989422804014327
    return (inner * normal, normal + inner * density)


def resident(shape):
    return pl.BlockSpec(shape, lambda *place: (0,) * len(shape), pipeline_mode=pl.Buffered(1))


def entry_kernel(query_blocks, field, embed, weight, mod, stream, hidden, mixed):
    width = embed.shape[0]
    stream_zero = contract(field[...], embed[...], 1, 1)
    stream[...] = stream_zero
    normed, unused = layer_norm(stream_zero)
    low = (normed * (1.0 + mod[1:2, :]) + mod[0:1, :]).astype(bf16)
    hidden[...] = low
    for part in (1, 2):
        columns = pl.ds(part * width, width)
        mixed[:, columns] = contract(low, weight[:, columns], 1, 0).astype(bf16)

    @pl.when(pl.program_id(0) < query_blocks)
    def _():
        queries = contract(low, weight[:, 0:width], 1, 0)
        mixed[:, 0:width] = (queries * QUERY_SCALE).astype(bf16)


def entry(fields, embed, weight, mod, block, query_rows, unit_of):
    rows, pieces = fields.shape
    width = embed.shape[0]
    by_row = lambda columns: pl.BlockSpec((block, columns), lambda i: (i, 0))
    return pl.pallas_call(
        functools.partial(entry_kernel, query_rows // block),
        grid=(rows // block,),
        in_specs=[
            by_row(pieces),
            resident(embed.shape),
            resident(weight.shape),
            pl.BlockSpec((None,) + mod.shape[1:], lambda i: (unit_of(i), 0, 0)),
        ],
        out_specs=[by_row(width), by_row(width), by_row(3 * width)],
        out_shape=[
            jax.ShapeDtypeStruct((rows, width), f32),
            jax.ShapeDtypeStruct((rows, width), bf16),
            jax.ShapeDtypeStruct((rows, 3 * width), bf16),
        ],
        cost_estimate=pl.CostEstimate(
            flops=8 * rows * width * width, bytes_accessed=12 * rows * width, transcendentals=0
        ),
        compiler_params=pltpu.CompilerParams(vmem_limit_bytes=VMEM_BYTES),
        name="entry",
    )(fields, embed, weight, mod)


def attend_kernel(sub, query, key, value, out, kept, inverse, value_t, key_one, stats):
    block, keys = query.shape[0], key.shape[0]
    zero, one = jnp.zeros((), bf16), jnp.ones((), bf16)

    @pl.when(pl.program_id(1) == 0)
    def _():
        turned = jnp.transpose(value[...])
        first_rows = lax.broadcasted_iota(jnp.int32, (2 * HD, keys), 0) < HD
        value_t[0] = jnp.where(first_rows, turned, one)
        value_t[1] = jnp.where(first_rows, one, turned)
        first_lanes = lax.broadcasted_iota(jnp.int32, (keys, 2 * HD), 1) < HD
        both = key[...]
        key_one[0] = jnp.where(first_lanes, both, one)
        key_one[1] = jnp.where(first_lanes, one, both)
        wide = both.astype(f32)
        mean = jnp.mean(wide, 0, keepdims=True)
        spread = (wide - mean) * (wide - mean)
        stats[0:1] = mean
        for head in range(2):
            mine = first_lanes if head == 0 else jnp.logical_not(first_lanes)
            size = jnp.sum(jnp.where(mine, spread, 0.0), 1, keepdims=True)
            far = jnp.max(size, 0, keepdims=True)
            stats[1 + head : 2 + head] = jnp.broadcast_to(0.5 * jnp.sqrt(far), (1, 2 * HD))

    lanes = lax.broadcasted_iota(jnp.int32, (block, 2 * HD), 1)
    wide = query[...].astype(f32)
    level = wide * stats[0:1]
    shifts, reaches = [], []
    for head in range(2):
        mine = (lanes < HD) if head == 0 else (lanes >= HD)
        length = jnp.sqrt(jnp.sum(jnp.where(mine, wide * wide, 0.0), 1, keepdims=True))
        reach = length * stats[1 + head : 2 + head, 0:1]
        shifts.append(jnp.sum(jnp.where(mine, level, 0.0), 1, keepdims=True) + reach)
        reaches.append(jnp.max(reach))
    near = jnp.maximum(reaches[0], reaches[1]) <= 60.0
    upper = lax.broadcasted_iota(jnp.int32, (2 * HD, sub), 0) < HD

    def run(exact):
        for part in range(block // sub):
            rows = pl.ds(part * sub, sub)
            results = []
            for head in range(2):
                spot = lanes[0:sub]
                mine = (spot < HD) if head == 0 else (spot >= HD)
                if exact:
                    moved = jnp.where(mine, query[rows, :], zero)
                    scores = contract(key_one[head], moved, 1, 1)
                    scores = scores - jnp.max(scores, 0, keepdims=True)
                else:
                    shift = (-shifts[head][part * sub : part * sub + sub]).astype(bf16)
                    free = HD if head == 0 else 0
                    rest = jnp.where(spot == free, shift, zero)
                    moved = jnp.where(mine, query[rows, :], rest)
                    scores = contract(key_one[head], moved, 1, 1)
                weights = jnp.exp2(scores).astype(bf16)
                kept[head, :, rows] = weights
                results.append(contract(value_t[head], weights, 1, 0))
            total = jnp.where(
                upper, pltpu.roll(results[0], HD, 0), pltpu.roll(results[1], HD, 0)
            )
            above = 1.0 / total
            mean = jnp.where(upper, results[0], results[1]) * above
            out[rows, :] = jnp.transpose(mean).astype(bf16)
            inverse[0:1, rows] = above[0:1]
            inverse[1:2, rows] = above[HD : HD + 1]

    @pl.when(near)
    def _():
        run(False)

    @pl.when(jnp.logical_not(near))
    def _():
        run(True)


def attend(queries, memory, places, block, sub, count, keys, width):
    pairs = width // (2 * HD)
    query_at, key_at, key_column, value_column = places
    return pl.pallas_call(
        functools.partial(attend_kernel, sub),
        grid=(pairs, count // block),
        in_specs=[
            pl.BlockSpec((block, 2 * HD), lambda h, i: (query_at // block + i, h)),
            pl.BlockSpec((keys, 2 * HD), lambda h, i: (key_at // keys, key_column * pairs + h)),
            pl.BlockSpec((keys, 2 * HD), lambda h, i: (key_at // keys, value_column * pairs + h)),
        ],
        out_specs=[
            pl.BlockSpec((block, 2 * HD), lambda h, i: (i, h)),
            pl.BlockSpec((None, None, 2, keys, block), lambda h, i: (h, i, 0, 0, 0)),
            pl.BlockSpec((None, 2, block), lambda h, i: (h, 0, i)),
        ],
        out_shape=[
            jax.ShapeDtypeStruct((count, width), bf16),
            jax.ShapeDtypeStruct((pairs, count // block, 2, keys, block), bf16),
            jax.ShapeDtypeStruct((pairs, 2, count), f32),
        ],
        scratch_shapes=[
            pltpu.VMEM((2, 2 * HD, keys), bf16),
            pltpu.VMEM((2, keys, 2 * HD), bf16),
            pltpu.VMEM((8, 2 * HD), f32),
        ],
        cost_estimate=pl.CostEstimate(
            flops=20 * count * keys * width, bytes_accessed=2 * count * keys, transcendentals=0
        ),
        compiler_params=pltpu.CompilerParams(vmem_limit_bytes=VMEM_BYTES),
        name="attend",
    )(queries, memory, memory)


def attend_back_kernel(
    sub, query, key, value, grad, out, kept, inverse,
    grad_query, grad_key, grad_value, key_t, value_one, key_sum, value_sum,
):
    block, keys = query.shape[0], key.shape[0]
    step, steps = pl.program_id(1), pl.num_programs(1)
    zero = jnp.zeros((), bf16)

    @pl.when(step == 0)
    def _():
        first_rows = lax.broadcasted_iota(jnp.int32, (2 * HD, keys), 0) < HD
        turned = jnp.transpose(key[...])
        key_t[0] = jnp.where(first_rows, turned, zero)
        key_t[1] = jnp.where(first_rows, zero, turned)
        first_lanes = lax.broadcasted_iota(jnp.int32, (keys, 2 * HD), 1) < HD
        minus = jnp.full((), -1.0, bf16)
        value_one[0] = jnp.where(first_lanes, value[...], minus)
        value_one[1] = jnp.where(first_lanes, minus, value[...])
        key_sum[...] = jnp.zeros_like(key_sum)
        value_sum[...] = jnp.zeros_like(value_sum)

    lanes = lax.broadcasted_iota(jnp.int32, (sub, 2 * HD), 1)
    places = lax.broadcasted_iota(jnp.int32, (2 * HD, sub), 0)
    upper = places < HD
    for part in range(block // sub):
        rows = pl.ds(part * sub, sub)
        above = jnp.where(upper, inverse[0:1, rows], inverse[1:2, rows])
        scaled = (jnp.transpose(grad[rows, :].astype(f32)) * above).astype(bf16)
        product = scaled.astype(f32) * jnp.transpose(out[rows, :].astype(f32))
        natural = jnp.transpose(scaled)
        queries = query[rows, :]
        turned = None
        for head in range(2):
            delta = jnp.sum(product[HD * head : HD * head + HD], 0, keepdims=True)
            high = delta.astype(bf16)
            rest = (delta - high.astype(f32)).astype(bf16)
            free = HD if head == 0 else 0
            mine = upper if head == 0 else jnp.logical_not(upper)
            extra = jnp.where(places == free, high, jnp.where(places == free + 1, rest, zero))
            grad_probs = contract(value_one[head], jnp.where(mine, scaled, extra), 1, 0)
            weights = kept[head, :, rows]
            grad_scores = grad_probs.astype(bf16) * weights
            own = (lanes < HD) if head == 0 else (lanes >= HD)
            value_sum[...] += contract(weights, jnp.where(own, natural, zero), 1, 0)
            key_sum[...] += contract(grad_scores, jnp.where(own, queries, zero), 1, 0)
            term = contract(key_t[head], grad_scores, 1, 0)
            turned = term if turned is None else turned + term
        grad_query[rows, :] = (jnp.transpose(turned) * 0.125).astype(bf16)

    @pl.when(step == steps - 1)
    def _():
        grad_key[...] = (key_sum[...] * LN2).astype(bf16)
        grad_value[...] = value_sum[...].astype(bf16)


def attend_back(queries, memory, grads, out, kept, inverse, places, block, sub, pairs, into, shapes):
    query_at, key_at, key_column, value_column, grad_query_at, grad_key_at = places
    count, keys = out.shape[0], kept.shape[3]
    every = out.shape[1] // (2 * HD)
    first, last = pairs
    two = 2 * HD
    any_place = [pl.BlockSpec(memory_space=pl.ANY)] * len(into)
    kernel = functools.partial(attend_back_kernel, sub)
    if into:
        kernel = lambda *refs: attend_back_kernel(sub, *(refs[:7] + refs[10:]))
    work = (last - first) * count * keys * two
    return pl.pallas_call(
        kernel,
        grid=(last - first, count // block),
        in_specs=[
            pl.BlockSpec((block, two), lambda h, i: (query_at // block + i, first + h)),
            pl.BlockSpec((keys, two), lambda h, i: (key_at // keys, key_column * every + first + h)),
            pl.BlockSpec((keys, two), lambda h, i: (key_at // keys, value_column * every + first + h)),
            pl.BlockSpec((block, two), lambda h, i: (query_at // block + i, first + h)),
            pl.BlockSpec((block, two), lambda h, i: (i, first + h)),
            pl.BlockSpec((None, None, 2, keys, block), lambda h, i: (first + h, i, 0, 0, 0)),
            pl.BlockSpec((None, 2, block), lambda h, i: (first + h, 0, i)),
        ]
        + any_place,
        out_specs=[
            pl.BlockSpec((block, two), lambda h, i: (grad_query_at // block + i, h)),
            pl.BlockSpec((keys, two), lambda h, i: (grad_key_at // keys, h)),
            pl.BlockSpec((keys, two), lambda h, i: (grad_key_at // keys, h)),
        ],
        out_shape=[jax.ShapeDtypeStruct(shape, bf16) for shape in shapes],
        scratch_shapes=[
            pltpu.VMEM((2, two, keys), bf16),
            pltpu.VMEM((2, keys, two), bf16),
            pltpu.VMEM((keys, two), f32),
            pltpu.VMEM((keys, two), f32),
        ],
        input_output_aliases={7 + index: index for index in range(len(into))},
        cost_estimate=pl.CostEstimate(flops=32 * work, bytes_accessed=4 * work // HD, transcendentals=0),
        compiler_params=pltpu.CompilerParams(vmem_limit_bytes=VMEM_BYTES),
        name="attend_back",
    )(queries, memory, memory, grads, out, kept, inverse, *into)


def middle_kernel(
    attended, stream, target, weight_rows, mod, combine, first, second, read,
    hidden, active, grad_two, grad_inner, final, grad_read, grad_one, grad_attended, grad_stream,
    sums, losses, slopes,
):
    width, spread = first.shape
    tiles = [pl.ds(start, width) for start in range(0, spread, width)]
    gate_a, shift_b, scale_b = mod[2:3, :], mod[3:4, :], mod[4:5, :]
    gate_b, gain = mod[5:6, :], mod[6:7, :]
    branch_a = contract(attended[...], combine[...], 1, 0)
    stream_one = stream[...] + gate_a * branch_a
    norm_b, inverse_b = layer_norm(stream_one)
    low = (norm_b * (1.0 + scale_b) + shift_b).astype(bf16)
    hidden[...] = low
    branch_b = None
    for tile in tiles:
        value, slope = gelu_pair(contract(low, first[:, tile], 1, 0))
        value = value.astype(bf16)
        active[:, tile] = value
        slopes[:, tile] = slope.astype(bf16)
        term = contract(value, second[:, tile], 1, 1)
        branch_b = term if branch_b is None else branch_b + term
    norm_c, inverse_c = layer_norm(stream_one + gate_b * branch_b)
    last = (norm_c * gain).astype(bf16)
    final[...] = last
    diff = contract(last, read[...], 1, 0) - target[...].astype(f32)
    losses[...] = jnp.broadcast_to(column_sum(weight_rows[:, 0:1] * diff * diff), losses.shape)
    grad_low = (weight_rows[:, 1:2] * diff).astype(bf16)
    grad_read[...] = grad_low
    grad_final = contract(grad_low, read[...], 1, 1)
    sums[6:7, :] = column_sum(grad_final * norm_c)
    grad = norm_back(grad_final * gain, norm_c, inverse_c)
    sums[5:6, :] = column_sum(grad * branch_b)
    back = (grad * gate_b).astype(bf16)
    grad_two[...] = back
    grad_hidden = None
    for tile in tiles:
        inner = contract(back, second[:, tile], 1, 0)
        inner = (inner * slopes[:, tile].astype(f32)).astype(bf16)
        grad_inner[:, tile] = inner
        term = contract(inner, first[:, tile], 1, 1)
        grad_hidden = term if grad_hidden is None else grad_hidden + term
    sums[3:4, :] = column_sum(grad_hidden)
    sums[4:5, :] = column_sum(grad_hidden * norm_b)
    grad = grad + norm_back(grad_hidden * (1.0 + scale_b), norm_b, inverse_b)
    grad_stream[...] = grad
    sums[2:3, :] = column_sum(grad * branch_a)
    back = (grad * gate_a).astype(bf16)
    grad_one[...] = back
    grad_attended[...] = contract(back, combine[...], 1, 1).astype(bf16)
    sums[0:2, :] = jnp.zeros((2, width), f32)
    sums[7:8, :] = jnp.zeros((1, width), f32)


def middle(attended, stream, target, weight_rows, mod, combine, first, second, read, block, unit_of):
    rows, width = attended.shape
    spread, pieces = first.shape[1], read.shape[1]
    blocks = rows // block
    by_row = lambda columns: pl.BlockSpec((block, columns), lambda i: (i, 0))
    shape = lambda columns, kind: jax.ShapeDtypeStruct((rows, columns), kind)
    outs = (
        (width, bf16), (spread, bf16), (width, bf16), (spread, bf16), (width, bf16), (pieces, bf16),
        (width, bf16), (width, bf16), (width, f32),
    )
    return pl.pallas_call(
        middle_kernel,
        grid=(blocks,),
        in_specs=[
            by_row(width),
            by_row(width),
            by_row(pieces),
            by_row(2),
            pl.BlockSpec((None,) + mod.shape[1:], lambda i: (unit_of(i), 0, 0)),
            resident(combine.shape),
            resident(first.shape),
            resident(second.shape),
            resident(read.shape),
        ],
        out_specs=[by_row(columns) for columns, kind in outs]
        + [
            pl.BlockSpec((None, 8, width), lambda i: (i, 0, 0)),
            pl.BlockSpec((None, 8, pieces), lambda i: (i, 0, 0)),
        ],
        out_shape=[shape(columns, kind) for columns, kind in outs]
        + [
            jax.ShapeDtypeStruct((blocks, 8, width), f32),
            jax.ShapeDtypeStruct((blocks, 8, pieces), f32),
        ],
        scratch_shapes=[pltpu.VMEM((block, spread), bf16)],
        cost_estimate=pl.CostEstimate(
            flops=60 * rows * width * width, bytes_accessed=40 * rows * width, transcendentals=0
        ),
        compiler_params=pltpu.CompilerParams(vmem_limit_bytes=VMEM_BYTES),
        name="middle",
    )(attended, stream, target, weight_rows, mod, combine, first, second, read)


def leave_kernel(query_blocks, parts, *refs):
    grads, (stream, grad_stream, weight, mod, out, sums, held) = refs[: 3 * parts], refs[3 * parts :]
    width = stream.shape[1]
    piece = width // parts
    asks = pl.program_id(0) < query_blocks
    columns = lambda kind, part: pl.ds(kind * width + part * piece, piece)
    total = None
    for part in range(parts):
        for kind in (1, 2):
            term = contract(grads[3 * part + kind][...], weight[:, columns(kind, part)], 1, 1)
            total = term if total is None else total + term
    held[...] = total

    @pl.when(asks)
    def _():
        for part in range(parts):
            held[...] += contract(grads[3 * part][...], weight[:, columns(0, part)], 1, 1)

    normed, inverse = layer_norm(stream[...])
    grad_hidden = held[...]
    sums[0:1, :] = column_sum(grad_hidden)
    sums[1:2, :] = column_sum(grad_hidden * normed)
    sums[2:8, :] = jnp.zeros((6, width), f32)
    grad = norm_back(grad_hidden * (1.0 + mod[1:2, :]), normed, inverse)
    grad = grad + jnp.where(asks, grad_stream[...], 0.0)
    out[...] = grad.astype(bf16)


def leave(grads, stream, grad_stream, weight, mod, block, unit_of, start, count, query_count):
    width = stream.shape[1]
    parts = len(grads) // 3
    asking = query_count // block
    blocks, offset = count // block, start // block
    by_row = lambda columns: pl.BlockSpec((block, columns), lambda i: (offset + i, 0))
    asked = lambda columns: pl.BlockSpec(
        (block, columns), lambda i: (jnp.minimum(offset + i, asking - 1), 0)
    )
    piece = width // parts
    return pl.pallas_call(
        functools.partial(leave_kernel, asking - offset, parts),
        grid=(blocks,),
        in_specs=[asked(piece), by_row(piece), by_row(piece)] * parts
        + [
            by_row(width),
            asked(width),
            resident(weight.shape),
            pl.BlockSpec((None,) + mod.shape[1:], lambda i: (unit_of(offset + i), 0, 0)),
        ],
        out_specs=[
            pl.BlockSpec((block, width), lambda i: (i, 0)),
            pl.BlockSpec((None, 8, width), lambda i: (i, 0, 0)),
        ],
        out_shape=[
            jax.ShapeDtypeStruct((count, width), bf16),
            jax.ShapeDtypeStruct((blocks, 8, width), f32),
        ],
        scratch_shapes=[pltpu.VMEM((block, width), f32)],
        cost_estimate=pl.CostEstimate(
            flops=7 * count * width * width, bytes_accessed=16 * count * width, transcendentals=0
        ),
        compiler_params=pltpu.CompilerParams(vmem_limit_bytes=VMEM_BYTES),
        name="leave",
    )(*grads, stream, grad_stream, weight, mod)


MESH = pl.DeviceIdType.MESH


def where_am_i():
    both = lax.axis_index("fsdp")
    return (lax.axis_index("dp"), lax.axis_index("seq"), both // 2, both % 2)


def neighbour(digit, away=1):
    z, x, y, core = where_am_i()
    if digit == 0:
        return {"dp": (z + away) % 4}
    if digit == 1:
        return {"seq": 1 - x}
    return {"fsdp": (1 - y) * 2 + core if digit == 2 else y * 2 + 1 - core}


def greet():
    barrier = pltpu.get_barrier_semaphore()
    partners = [neighbour(1), neighbour(2), neighbour(3)] + [neighbour(0, d) for d in (1, 2, 3)]
    for partner in partners:
        pl.semaphore_signal(barrier, inc=1, device_id=partner, device_id_type=MESH)
    pl.semaphore_wait(barrier, len(partners))


class Summing:
    steps = ((3, 1), (1, 1), (2, 1), (0, 1), (0, 2))

    def __init__(self, running, came, sent, got):
        self.running, self.came, self.sent, self.got = running, came, sent, got
        self.copies = []

    def start(self):
        index = len(self.copies)
        digit, bit = self.steps[index]
        if digit == 0:
            z = where_am_i()[0]
            partner = {"dp": z + bit - 2 * bit * ((z // bit) % 2)}
        else:
            partner = neighbour(digit)
        copy = pltpu.make_async_remote_copy(
            src_ref=self.running.at[index],
            dst_ref=self.came.at[index],
            send_sem=self.sent.at[index],
            recv_sem=self.got.at[index],
            device_id=partner,
            device_id_type=MESH,
        )
        copy.start()
        self.copies.append(copy)

    def end(self):
        index = len(self.copies) - 1
        self.copies[index].wait()
        self.running[index + 1] = self.running[index] + self.came[index]


def summing_scratch(shape):
    return [
        pltpu.VMEM((6,) + shape, f32),
        pltpu.VMEM((5,) + shape, f32),
        pltpu.SemaphoreType.DMA((5,)),
        pltpu.SemaphoreType.DMA((5,)),
    ]


def small_sum_kernel(values, out, running, came, sent, got):
    running[0] = values[...]
    greet()
    total = Summing(running, came, sent, got)
    for step in range(5):
        total.start()
        total.end()
    out[...] = running[5]


def small_sum(values):
    return pl.pallas_call(
        small_sum_kernel,
        out_shape=jax.ShapeDtypeStruct(values.shape, f32),
        in_specs=[pl.BlockSpec(memory_space=pltpu.VMEM)],
        out_specs=pl.BlockSpec(memory_space=pltpu.VMEM),
        scratch_shapes=summing_scratch(values.shape),
        compiler_params=pltpu.CompilerParams(collective_id=2, has_side_effects=True),
        name="small_sum",
    )(values)


def spread_kernel(chunks, arrays, *refs):
    sources, values, targets, out = refs[:arrays], refs[arrays], refs[arrays + 1 : -10], refs[-10]
    running, came, sent, got, own_sem, z_sent, z_got, far_sent, far_got = refs[-9:]
    z, x, y, core = where_am_i()
    running[0] = values[...]
    greet()
    total = Summing(running, came, sent, got)
    total.start()
    own = []
    for index in range(arrays):
        copy = pltpu.make_async_copy(
            sources[index], targets[index].at[z, x, y, core], own_sem.at[index]
        )
        copy.start()
        own.append(copy)
    along = {}
    for chunk, (which, start, size, order) in enumerate(chunks):
        columns = pl.ds(start, size)
        for away in (1, 2, 3):
            copy = pltpu.make_async_remote_copy(
                src_ref=sources[which].at[:, columns],
                dst_ref=targets[which].at[z, x, y, core, :, columns],
                send_sem=z_sent.at[chunk, away - 1],
                recv_sem=z_got.at[chunk, away - 1],
                device_id=neighbour(0, away),
                device_id_type=MESH,
            )
            copy.start()
            along[chunk, away] = copy
    for copy in own:
        copy.wait()
    far = {}
    every = slice(None)
    for time in range(len(chunks) + 2):
        for stage in range(3):
            chunk = time - stage
            if not 0 <= chunk < len(chunks):
                continue
            which, start, size, order = chunks[chunk]
            if stage == 0:
                for away in (1, 2, 3):
                    along[chunk, away].wait_recv()
            else:
                far[chunk, stage - 1].wait_recv()
            at = [every, x, y, core]
            for digit in order[:stage]:
                at[digit] = every
            block = targets[which].at[(*at, every, pl.ds(start, size))]
            copy = pltpu.make_async_remote_copy(
                src_ref=block,
                dst_ref=block,
                send_sem=far_sent.at[chunk, stage],
                recv_sem=far_got.at[chunk, stage],
                device_id=neighbour(order[stage]),
                device_id_type=MESH,
            )
            copy.start()
            far[chunk, stage] = copy
        if time < 5:
            total.end()
            if time < 4:
                total.start()
    out[...] = running[5]
    for chunk in range(len(chunks)):
        far[chunk, 2].wait_recv()
        for away in (1, 2, 3):
            along[chunk, away].wait_send()
        for stage in range(3):
            far[chunk, stage].wait_send()


def spread_start(shards, values):
    share = shards[0].shape[0]
    orders = ((1, 2, 3), (2, 1, 3))
    chunks = []
    for which, shard in enumerate(shards):
        size = min(512, shard.shape[1])
        for start in range(0, shard.shape[1], size):
            chunks.append((which, start, size, orders[len(chunks) % 2]))
    count = len(chunks)
    grid = (4, 2, 2, 2, share)
    anywhere = pl.BlockSpec(memory_space=pl.ANY)
    near = pl.BlockSpec(memory_space=pltpu.VMEM)
    results = pl.pallas_call(
        functools.partial(spread_kernel, chunks, len(shards)),
        out_shape=[jax.ShapeDtypeStruct(grid + (shard.shape[1],), bf16) for shard in shards]
        + [jax.ShapeDtypeStruct(values.shape, f32)],
        in_specs=[anywhere] * len(shards) + [near],
        out_specs=[anywhere] * len(shards) + [near],
        scratch_shapes=summing_scratch(values.shape)
        + [pltpu.SemaphoreType.DMA((len(shards),))]
        + [pltpu.SemaphoreType.DMA((count, 3))] * 4,
        compiler_params=pltpu.CompilerParams(collective_id=0, has_side_effects=True),
        name="spread_start",
    )(*shards, values)
    return [whole.reshape(32 * share, whole.shape[-1]) for whole in results[:-1]], results[-1]


def fold_kernel(chunks, first, last, values, out_first, out_last, out, running, came, sent, got,
                part, part_one, part_two, got_core, got_one, got_two, got_z, sents, gots):
    place = where_am_i()
    z, core = place[0], place[3]
    sources, outs = (first, last), (out_first, out_last)
    running[0] = values[...]
    greet()
    total = Summing(running, came, sent, got)
    copies = {}
    every = slice(None)

    def send(chunk, stage, source, target, partner):
        copy = pltpu.make_async_remote_copy(
            src_ref=source,
            dst_ref=target,
            send_sem=sents.at[chunk, stage],
            recv_sem=gots.at[chunk, stage],
            device_id=partner,
            device_id_type=MESH,
        )
        copy.start()
        copies[chunk, stage] = copy

    def sum_of(left, right):
        return (left.astype(f32) + right.astype(f32)).astype(bf16)

    for chunk, (which, start, size, order) in enumerate(chunks):
        block = sources[which].at[:, :, :, 1 - core, :, pl.ds(start, size)]
        send(chunk, 0, block, got_core.at[chunk], neighbour(3))
    total.start()
    for time in range(len(chunks) + 3):
        for stage in range(1, 5):
            chunk = time - stage + 1
            if not 0 <= chunk < len(chunks):
                continue
            which, start, size, order = chunks[chunk]
            columns = pl.ds(start, size)
            near, far = order
            if stage == 1:
                copies[chunk, 0].wait_recv()
                part[chunk] = sum_of(sources[which][:, :, :, core, :, columns], got_core[chunk])
                at = [every, every, every]
                at[near] = 1 - place[near]
                send(chunk, 1, part.at[(chunk, *at)], got_one.at[chunk], neighbour(near))
            elif stage == 2:
                copies[chunk, 1].wait_recv()
                at = [every, every, every]
                at[near] = place[near]
                part_one[chunk] = sum_of(part[(chunk, *at)], got_one[chunk])
                send(
                    chunk, 2, part_one.at[chunk, :, 1 - place[far]], got_two.at[chunk], neighbour(far)
                )
            elif stage == 3:
                copies[chunk, 2].wait_recv()
                part_two[chunk] = sum_of(part_one[chunk, :, place[far]], got_two[chunk])
                for away in (1, 2, 3):
                    source = part_two.at[chunk, (z + away) % 4]
                    send(chunk, 2 + away, source, got_z.at[chunk, away - 1], neighbour(0, away))
            else:
                whole = part_two[chunk, z].astype(f32)
                for away in (1, 2, 3):
                    copies[chunk, 2 + away].wait_recv()
                    whole = whole + got_z[chunk, away - 1].astype(f32)
                outs[which][:, columns] = whole
        if time < 5:
            total.end()
            if time < 4:
                total.start()
    for step in range(len(chunks) + 3, 5):
        total.end()
        if step < 4:
            total.start()
    out[...] = running[5]
    for chunk in range(len(chunks)):
        for stage in range(6):
            copies[chunk, stage].wait_send()


def fold_end(first, last, values):
    rows, wide = first.shape
    thin = last.shape[1]
    share = rows // 32
    size = thin
    orders = ((1, 2), (2, 1))
    chunks = [(0, start, size, orders[(start // size) % 2]) for start in range(0, wide, size)]
    chunks.append((1, 0, thin, orders[len(chunks) % 2]))
    count = len(chunks)
    grid = (4, 2, 2, 2, share)
    near = pl.BlockSpec(memory_space=pltpu.VMEM)
    return pl.pallas_call(
        functools.partial(fold_kernel, chunks),
        out_shape=[
            jax.ShapeDtypeStruct((share, wide), f32),
            jax.ShapeDtypeStruct((share, thin), f32),
            jax.ShapeDtypeStruct(values.shape, f32),
        ],
        in_specs=[near, near, near],
        out_specs=[near, near, near],
        scratch_shapes=summing_scratch(values.shape)
        + [
            pltpu.VMEM((count, 4, 2, 2, share, size), bf16),
            pltpu.VMEM((count, 4, 2, share, size), bf16),
            pltpu.VMEM((count, 4, share, size), bf16),
            pltpu.VMEM((count, 4, 2, 2, share, size), bf16),
            pltpu.VMEM((count, 4, 2, share, size), bf16),
            pltpu.VMEM((count, 4, share, size), bf16),
            pltpu.VMEM((count, 3, share, size), bf16),
            pltpu.SemaphoreType.DMA((count, 6)),
            pltpu.SemaphoreType.DMA((count, 6)),
        ],
        compiler_params=pltpu.CompilerParams(
            collective_id=1, has_side_effects=True, vmem_limit_bytes=VMEM_BYTES
        ),
        name="fold_end",
    )(first.reshape(grid + (wide,)), last.reshape(grid + (thin,)), values)


class Links:
    def __init__(self, sizes):
        self.plain = sizes != (4, 2, 4)
        swap = lambda bit, size: [(index, index ^ bit) for index in range(size)]
        self.pairs = {
            1: ("seq", swap(1, 2)),
            2: ("fsdp", swap(2, 4)),
            3: ("fsdp", swap(1, 4)),
        }

    def places(self):
        both = lax.axis_index("fsdp")
        return (lax.axis_index("dp"), lax.axis_index("seq"), both // 2, both % 2)

    def start(self, shards, values):
        if not self.plain:
            return spread_start(shards, values)
        gather = lambda shard: lax.all_gather(shard, ALL, axis=0, tiled=True)
        return [gather(shard) for shard in shards], lax.psum(values, ALL)

    def end(self, first, last, values):
        if not self.plain:
            return fold_end(first, last, values)
        scatter = lambda whole: lax.psum_scatter(whole, ALL, scatter_dimension=0, tiled=True)
        return scatter(first).astype(f32), scatter(last).astype(f32), lax.psum(values, ALL)

    def total(self, values):
        return lax.psum(values, ALL) if self.plain else small_sum(values)

    def scatter(self, values):
        if self.plain:
            yield lax.psum_scatter(values, ALL, scatter_dimension=0, tiled=True).astype(f32)
            return
        rows, columns = values.shape
        place = self.places()
        half = columns // 2
        blocks = values.reshape(4, 2, 2, 2, rows // 32, columns)
        lanes = [blocks[..., :half], blocks[..., half:]]
        for step in range(3):
            sums = []
            sent = []
            for lane, order in zip(lanes, ((3, 2, 1), (3, 1, 2))):
                digit = order[step]
                axis, swap = self.pairs[digit]
                pick = lambda which: lax.dynamic_slice_in_dim(lane, which, 1, digit)
                sent.append(lax.ppermute(pick(1 - place[digit]), axis, swap))
                sums.append(pick(place[digit]))
            yield sent
            lanes = [
                (mine.astype(f32) + came.astype(f32)).astype(bf16) for mine, came in zip(sums, sent)
            ]
        whole = jnp.concatenate(
            [lane.reshape(4, rows // 32, half) for lane in lanes], 2
        )
        came = []
        for away in (1, 2, 3):
            part = lax.dynamic_slice_in_dim(whole, (place[0] + away) % 4, 1, 0)
            came.append(lax.ppermute(part, "dp", [(i, (i + away) % 4) for i in range(4)]))
        yield came
        total = lax.dynamic_slice_in_dim(whole, place[0], 1, 0).astype(f32)
        for part in came:
            total = total + part.astype(f32)
        yield total[0]


class Flow:
    def __init__(self):
        self.active = []
        self.results = {}
        self.pending = []

    def add(self, name, chain):
        self.active.append((name, chain))
        self.step(only=name)

    def step(self, only=None):
        left = []
        for name, chain in self.active:
            if only is not None and name != only:
                left.append((name, chain))
                continue
            value = next(chain)
            if isinstance(value, list):
                self.pending.extend(value)
                left.append((name, chain))
            else:
                self.results[name] = value
        self.active = left

    def tie(self, values):
        if not self.pending:
            return values
        held, self.pending = lax.optimization_barrier((values, self.pending))[0], []
        return held

    def finish(self):
        while self.active:
            self.step()


def adam(master, first, second, grad, factor, step_rate):
    grad = grad * factor
    first_new = beta_one * first + (1.0 - beta_one) * grad
    second_new = beta_two * second + (1.0 - beta_two) * grad * grad
    corrected = (
        first_new
        / (1.0 - beta_one**STEP)
        / (jnp.sqrt(second_new / (1.0 - beta_two**STEP)) + epsilon)
    )
    return (master - step_rate * (corrected + decay * master), first_new, second_new)


def largest(limit, *sizes):
    block = limit
    while any(size % block for size in sizes):
        block //= 2
    return block


def body(sizes, *args):
    ways = sizes[1]
    links = Links(sizes)
    fields, targets, interval, storm_index, valid_count, latitude, storm_scale = args[:7]
    masters, firsts, seconds = args[7:15], args[15:23], args[23:31]
    embedding, intervals, modulator, projector, combiner, feedforward, readout, vectors = masters
    micros, samples_dev, part, pieces = fields.shape
    patches = latitude.shape[0]
    units = micros * samples_dev
    share, width = projector.shape[0], projector.shape[1] // 3
    place = lax.axis_index("seq")
    device = lax.axis_index(ALL)
    sample_start = lax.axis_index(("dp", "fsdp")) * samples_dev
    ring = [(index, 1 - index) for index in range(2)]
    alone = units // 2 if ways == 2 else 0
    shared = units - ways * alone
    have = alone + shared

    everywhere = jnp.arange(patches, dtype=jnp.int32)
    mask = (everywhere[None, None, :] >= patches - valid_count[:, :, None]).astype(f32)
    levels = jnp.arange(storm_scale.shape[0], dtype=jnp.int32)
    storms = jnp.sum(jnp.where(storm_index[:, :, None] == levels, storm_scale, 0.0), -1)
    row_weights = latitude[None, None, :] * storms[:, :, None] * mask
    total_weight = pieces * jnp.sum(row_weights)

    def local(values):
        cut = lax.dynamic_slice_in_dim(values, sample_start, samples_dev, 1)
        cut = cut.reshape((units,) + values.shape[2:])
        mine = [lax.dynamic_slice_in_dim(cut, place * alone, alone, 0)] if alone else []
        return jnp.concatenate(mine + [cut[ways * alone :]], 0)

    kinds = local(interval)
    weights_unit = jnp.roll(local(row_weights), -place * part, 1)
    weights_rows = jnp.concatenate(
        [weights_unit[:alone].reshape(-1), weights_unit[alone:, :part].reshape(-1)]
    )
    weight_rows = jnp.stack([weights_rows, weights_rows * (2.0 / total_weight)], 1)

    def widen(values):
        flat = values.reshape(units, part, pieces)
        return jnp.pad(flat, ((0, 0), (0, 0), (0, WIDE - pieces)))

    own, goal = widen(fields), widen(targets)
    if alone:
        away = (1 - place) * alone
        cut = lambda values, start: lax.dynamic_slice_in_dim(values, start, alone, 0)
        sent = jnp.concatenate([cut(own, away), own[2 * alone :]], 0)
        came = lax.ppermute(sent, "seq", ring)
        goal_came = lax.ppermute(cut(goal, away), "seq", ring)
        whole = jnp.concatenate([cut(own, place * alone), came[:alone]], 1)
        goal_whole = jnp.concatenate([cut(goal, place * alone), goal_came], 1)
        rows = [whole, own[2 * alone :], came[alone:]]
        goals = [goal_whole, goal[2 * alone :]]
    elif ways == 1:
        rows, goals = [own], [goal]
    else:
        everyone = lax.all_gather(own, "seq", axis=1, tiled=True)
        rows = [own, jnp.roll(everyone, -place * part, 1)[:, part:]]
        goals = [goal]
    flatten = lambda parts: jnp.concatenate([piece.reshape(-1, WIDE) for piece in parts], 0)
    all_rows, goal_rows = flatten(rows), flatten(goals)
    asking = (alone * ways + shared) * part

    def unit_of(block):
        whole_blocks = alone * patches // block
        own_blocks = shared * part // block
        other = max((patches - part) // block, 1)

        def at(i):
            late = alone + (i - whole_blocks) // (part // block)
            later = alone + (i - whole_blocks - own_blocks) // other
            late = jnp.where(i < whole_blocks + own_blocks, late, later)
            return jnp.where(i < whole_blocks, i // (patches // block), late)

        return at

    low = [master.astype(bf16) for master in masters]
    step_vec = low[1].astype(f32)
    active = jax.nn.silu(step_vec)
    active_low = active.astype(bf16)
    table = contract(active_low, low[2], 1, 0)
    spread_vectors = lax.dynamic_update_slice(
        jnp.zeros((7, width), f32), low[7].astype(f32), (0, device * share)
    )
    to_wide = lambda values: jnp.pad(values, ((0, 0), (0, WIDE - pieces)))
    (embed, project, read), carried = links.start(
        (to_wide(low[0].T), low[3], to_wide(low[6])),
        jnp.concatenate([table.reshape(3 * 6 * width // 128, 128), spread_vectors.reshape(-1, 128)]),
    )
    nothing = carried[0, 0] * 0.0
    carried = carried.reshape(-1)
    table = carried[: table.size].reshape(DTK, 6, width)
    all_vectors = carried[table.size :].reshape(7, width)
    table = table + all_vectors[None, :6]
    chosen = sum(jnp.where(kinds[:, None, None] == kind, table[kind], 0.0) for kind in range(DTK))
    gain = jnp.broadcast_to(all_vectors[6], (have, 1, width))
    mod = jnp.concatenate([chosen, gain, jnp.zeros((have, 1, width), f32)], 1)

    gather = lambda values: lax.all_gather(values, ALL, axis=0, tiled=True)
    late = (combiner, feedforward[0], feedforward[1])
    combine, first, second = [gather((shard + nothing).astype(bf16)) for shard in late]

    block = largest(512, part)
    stream, hidden_a, mixed = entry(all_rows, embed, project, mod, block, asking, unit_of(block))

    calls = []
    for unit in range(have):
        if unit < alone:
            start = unit * patches
            calls.append((patches, mixed, (start, start, 1, 2)))
        else:
            start = alone * patches + (unit - alone) * part
            behind = asking + (unit - alone) * (patches - part)
            if shared == 1 and start % patches == 0:
                calls.append((part, mixed, (start, start, 1, 2)))
            else:
                joined = jnp.concatenate(
                    [
                        mixed[start : start + part, width:],
                        mixed[behind : behind + patches - part, width:],
                    ],
                    0,
                )
                calls.append((part, joined, (start, 0, 0, 1)))
    saved = []
    for count, memory, where in calls:
        block = largest(1024, count, where[0] if where[0] else count)
        saved.append(attend(mixed, memory, where, block, block, count, patches, width))
    attended_rows = jnp.concatenate([out for out, kept, inverse in saved], 0)

    block = largest(256, part)
    (
        hidden_b, activated, grad_two, grad_inner, final, grad_read, grad_one, grad_attended,
        grad_stream, sums, losses,
    ) = middle(
        attended_rows, stream, goal_rows, weight_rows, mod, combine, first, second, read, block,
        unit_of(block),
    )
    units_mid = [unit_of(block)(jnp.int32(i)) for i in range(sums.shape[0])]
    loss_local = jnp.sum(losses[:, 0, :])

    flow = Flow()
    summed = lambda left, right: contract(left, right, 0, 0).astype(bf16)
    flow.add("first", links.scatter(summed(hidden_b, grad_inner)))
    grad_two = flow.tie(grad_two)
    flow.step()
    flow.add("second", links.scatter(summed(grad_two, activated)))
    rest = jnp.concatenate([summed(attended_rows, grad_one), summed(final, grad_read)], 1)
    grad_attended = flow.tie((grad_attended, rest))[0]
    flow.step()
    flow.add("rest", links.scatter(rest))

    pairs = width // (2 * HD)
    halves = 2
    grads = []
    for half in range(halves):
        reach = (half * pairs // halves, (half + 1) * pairs // halves)
        piece = width // halves
        shapes = ((asking, piece), (have * patches, piece), (have * patches, piece))
        into = ()
        for unit, ((count, memory, where), (out, kept, inverse)) in enumerate(zip(calls, saved)):
            block = kept.shape[4]
            into = attend_back(
                mixed, memory, grad_attended, out, kept, inverse,
                where + (where[0], unit * patches), block, min(block, 256), reach, into, shapes,
            )
            grad_attended, into = flow.tie((grad_attended, into))
            flow.step()
        if not (alone and shared <= 1):
            own_part = lambda values, unit, low_row, high_row: values[
                unit * patches + low_row : unit * patches + high_row
            ]
            into = (into[0],) + tuple(
                jnp.concatenate(
                    [values[: alone * patches]]
                    + [own_part(values, unit, 0, part) for unit in range(alone, have)]
                    + [own_part(values, unit, part, patches) for unit in range(alone, have)],
                    0,
                )
                for values in into[1:]
            )
        grads.extend(into)
        pieces_of = [summed(hidden_a[:asking], into[0])]
        pieces_of += [summed(hidden_a, values) for values in into[1:]]
        last_part = jnp.concatenate(pieces_of, 1)
        if half < halves - 1:
            flow.add("project" + str(half), links.scatter(last_part))
    block = largest(512, part)
    grad_zero, sums_a, units_out = [], [], []
    for start, count in ((0, alone * patches), (alone * patches, (have - alone) * patches)):
        if count == 0:
            continue
        held = flow.tie(tuple(grads))
        flow.step()
        value, by_block = leave(
            held, stream, grad_stream, project, mod, block, unit_of(block), start, count, asking
        )
        grad_zero.append(value)
        sums_a.append(by_block)
        units_out += [unit_of(block)(jnp.int32(start // block + i)) for i in range(count // block)]
    grad_embed = summed(jnp.concatenate(grad_zero, 0), all_rows)
    flow.finish()
    shard_first, shard_second = flow.results["first"], flow.results["second"]
    shard_combine, shard_read = flow.results["rest"][:, :width], flow.results["rest"][:, width:]
    sums_a = jnp.concatenate(sums_a, 0)

    by_block = jnp.concatenate([sums, sums_a], 0)
    kind_block = kinds[jnp.stack(units_mid + units_out)]
    grad_table = jnp.stack(
        [
            jnp.sum(jnp.where((kind_block == kind)[:, None, None], by_block, 0.0), 0)
            for kind in range(DTK)
        ]
    )
    loss_row = jnp.full((1, 128), loss_local)
    small = jnp.concatenate([grad_table[:, :7].reshape(-1, 128), loss_row])
    shard_last, shard_embed, carried = links.end(last_part, grad_embed, small)
    by_half = [flow.results["project" + str(half)] for half in range(halves - 1)] + [shard_last]
    by_half = jnp.stack(by_half, 1).reshape(share, halves, 3, width // halves)
    shard_project = by_half.transpose(0, 2, 1, 3).reshape(share, 3 * width)
    loss_total = carried[-1, 0]
    grad_table = carried[:-1].reshape(DTK, 7, width)
    grad_mod = grad_table[:, :6].reshape(DTK, 6 * width)
    shard_vectors = lax.dynamic_slice_in_dim(jnp.sum(grad_table, 0), device * share, share, 1)
    active_wide = active_low.astype(f32)
    shard_modulator = sum(
        active_wide[kind][:, None] * grad_mod[kind][None, :] for kind in range(DTK)
    )
    grad_active = jnp.stack(
        [jnp.sum(low[2].astype(f32) * grad_mod[kind][None, :], 1) for kind in range(DTK)]
    )
    unused, silu_back = jax.vjp(jax.nn.silu, step_vec)
    shard_intervals = silu_back(grad_active)[0]

    shards = (
        shard_embed[:, :pieces].T,
        shard_intervals,
        shard_modulator,
        shard_project,
        shard_combine,
        jnp.stack([shard_first, shard_second]),
        shard_read[:, :pieces],
        shard_vectors,
    )
    squares = sum(jnp.sum(grad * grad) for grad in shards)
    squares = links.total(jnp.full((8, 128), squares))[0, 0]
    norm = jnp.sqrt(squares)
    factor = clip_norm / jnp.maximum(norm, clip_norm)
    results = [
        adam(master, first_moment, second_moment, grad, factor, rate)
        for master, first_moment, second_moment, grad, rate in zip(
            masters, firsts, seconds, shards, step_rates()
        )
    ]
    return tuple(result[index] for index in range(3) for result in results) + (
        loss_total,
        total_weight,
        norm,
    )


def solution(mesh):
    data = P(None, ("dp", "fsdp"), "seq", None)
    columns, rows = P(None, ALL), P(ALL, None)
    weights = (columns, columns, rows, rows, rows, P(None, ALL, None), rows, columns)
    return jax.shard_map(
        functools.partial(body, tuple(mesh.shape[axis] for axis in ALL)),
        mesh=mesh,
        in_specs=(data, data) + (P(),) * 5 + weights * 3,
        out_specs=weights * 3 + (P(),) * 3,
        check_vma=False,
    )
```

```python
import functools

import jax
import jax.numpy as jnp
from jax import lax
from jax.experimental import pallas as pl
from jax.experimental.pallas import tpu as pltpu
from jax.sharding import PartitionSpec as P

D = 1024
HD = 64
PIN = 276
WIDE = 384
DTK = 3
STEP = 10
PATCHES = 2048
ALL = ("dp", "seq", "fsdp")

beta_one = 0.9
beta_two = 0.999
decay = 0.01
epsilon = 1e-08
clip_norm = 0.005
norm_eps = 1e-06
bf16 = jnp.bfloat16
f32 = jnp.float32
LN2 = 0.6931471805599453
QUERY_SCALE = 0.125 / LN2
VMEM_BYTES = 60 * 2**20
ERF = (
    0.7978822138768258,
    0.03634467259297056,
    -4.4877727054425946e-05,
    -5.036405881894902e-05,
    3.0986869577148946e-06,
    -6.638614747540505e-08,
)
ERF_END = 21.16
TILE = 1024


def step_rates():
    factor = 1.5
    return (
        factor / PIN**0.5,
        factor,
        factor / D**0.5,
        factor / D**0.5,
        factor / max(64 * D // PATCHES, 16) ** 0.5,
        factor / (2 * D) ** 0.5,
        factor / D**0.5,
        factor,
    )


def contract(left, right, left_dim, right_dim):
    return lax.dot_general(
        left, right, (((left_dim,), (right_dim,)), ((), ())), preferred_element_type=f32
    )


def layer_norm(values):
    center = values - jnp.mean(values, -1, keepdims=True)
    inverse = lax.rsqrt(jnp.mean(center * center, -1, keepdims=True) + norm_eps)
    return (center * inverse, inverse)


def norm_back(upstream, normed, inverse):
    return inverse * (
        upstream
        - jnp.mean(upstream, -1, keepdims=True)
        - normed * jnp.mean(upstream * normed, -1, keepdims=True)
    )


def column_sum(values):
    return jnp.sum(values, 0, keepdims=True)


def gelu_pair(inner):
    square = inner * inner
    bounded = jnp.minimum(square, ERF_END)
    series = jnp.full_like(inner, ERF[-1])
    for coefficient in ERF[-2::-1]:
        series = series * bounded + coefficient
    normal = 0.5 + 0.5 * jnp.tanh(inner * series)
    density = jnp.exp2(square * (-0.5 / LN2)) * 0.3989422804014327
    return (inner * normal, normal + inner * density)


def resident(shape):
    return pl.BlockSpec(shape, lambda *place: (0,) * len(shape), pipeline_mode=pl.Buffered(1))


MESH = pl.DeviceIdType.MESH


def where_am_i():
    both = lax.axis_index("fsdp")
    return (lax.axis_index("dp"), lax.axis_index("seq"), both // 2, both % 2)


def neighbour(digit, away=1):
    z, x, y, core = where_am_i()
    if digit == 0:
        return {"dp": (z + away) % 4}
    if digit == 1:
        return {"seq": 1 - x}
    return {"fsdp": (1 - y) * 2 + core if digit == 2 else y * 2 + 1 - core}


def greet():
    barrier = pltpu.get_barrier_semaphore()
    partners = [neighbour(1), neighbour(2), neighbour(3)] + [neighbour(0, d) for d in (1, 2, 3)]
    for partner in partners:
        pl.semaphore_signal(barrier, inc=1, device_id=partner, device_id_type=MESH)
    pl.semaphore_wait(barrier, len(partners))


class Summing:
    steps = ((3, 1), (1, 1), (2, 1), (0, 1), (0, 2))

    def __init__(self, running, came, sent, got):
        self.running, self.came, self.sent, self.got = running, came, sent, got
        self.copies = []

    def start(self):
        index = len(self.copies)
        digit, bit = self.steps[index]
        if digit == 0:
            z = where_am_i()[0]
            partner = {"dp": z + bit - 2 * bit * ((z // bit) % 2)}
        else:
            partner = neighbour(digit)
        copy = pltpu.make_async_remote_copy(
            src_ref=self.running.at[index],
            dst_ref=self.came.at[index],
            send_sem=self.sent.at[index],
            recv_sem=self.got.at[index],
            device_id=partner,
            device_id_type=MESH,
        )
        copy.start()
        self.copies.append(copy)

    def end(self):
        index = len(self.copies) - 1
        self.copies[index].wait()
        self.running[index + 1] = self.running[index] + self.came[index]


def summing_scratch(shape):
    return [
        pltpu.VMEM((6,) + shape, f32),
        pltpu.VMEM((5,) + shape, f32),
        pltpu.SemaphoreType.DMA((5,)),
        pltpu.SemaphoreType.DMA((5,)),
    ]


def small_sum_kernel(values, out, running, came, sent, got):
    running[0] = values[...]
    greet()
    total = Summing(running, came, sent, got)
    for step in range(5):
        total.start()
        total.end()
    out[...] = running[5]


def small_sum(values):
    return pl.pallas_call(
        small_sum_kernel,
        out_shape=jax.ShapeDtypeStruct(values.shape, f32),
        in_specs=[pl.BlockSpec(memory_space=pltpu.VMEM)],
        out_specs=pl.BlockSpec(memory_space=pltpu.VMEM),
        scratch_shapes=summing_scratch(values.shape),
        compiler_params=pltpu.CompilerParams(collective_id=2, has_side_effects=True),
        name="small_sum",
    )(values)


def spread_kernel(chunks, arrays, *refs):
    sources, values, targets, out = refs[:arrays], refs[arrays], refs[arrays + 1 : -10], refs[-10]
    running, came, sent, got, own_sem, z_sent, z_got, far_sent, far_got = refs[-9:]
    z, x, y, core = where_am_i()
    running[0] = values[...]
    greet()
    total = Summing(running, came, sent, got)
    total.start()
    own = []
    for index in range(arrays):
        copy = pltpu.make_async_copy(
            sources[index], targets[index].at[z, x, y, core], own_sem.at[index]
        )
        copy.start()
        own.append(copy)
    along = {}
    for chunk, (which, start, size, order) in enumerate(chunks):
        columns = pl.ds(start, size)
        for away in (1, 2, 3):
            copy = pltpu.make_async_remote_copy(
                src_ref=sources[which].at[:, columns],
                dst_ref=targets[which].at[z, x, y, core, :, columns],
                send_sem=z_sent.at[chunk, away - 1],
                recv_sem=z_got.at[chunk, away - 1],
                device_id=neighbour(0, away),
                device_id_type=MESH,
            )
            copy.start()
            along[chunk, away] = copy
    for copy in own:
        copy.wait()
    far = {}
    every = slice(None)
    for time in range(len(chunks) + 2):
        for stage in range(3):
            chunk = time - stage
            if not 0 <= chunk < len(chunks):
                continue
            which, start, size, order = chunks[chunk]
            if stage == 0:
                for away in (1, 2, 3):
                    along[chunk, away].wait_recv()
            else:
                far[chunk, stage - 1].wait_recv()
            at = [every, x, y, core]
            for digit in order[:stage]:
                at[digit] = every
            block = targets[which].at[(*at, every, pl.ds(start, size))]
            copy = pltpu.make_async_remote_copy(
                src_ref=block,
                dst_ref=block,
                send_sem=far_sent.at[chunk, stage],
                recv_sem=far_got.at[chunk, stage],
                device_id=neighbour(order[stage]),
                device_id_type=MESH,
            )
            copy.start()
            far[chunk, stage] = copy
        if time < 5:
            total.end()
            if time < 4:
                total.start()
    out[...] = running[5]
    for chunk in range(len(chunks)):
        far[chunk, 2].wait_recv()
        for away in (1, 2, 3):
            along[chunk, away].wait_send()
        for stage in range(3):
            far[chunk, stage].wait_send()


def spread_start(shards, values):
    share = shards[0].shape[0]
    orders = ((1, 2, 3), (2, 1, 3))
    chunks = []
    for which, shard in enumerate(shards):
        size = min(512, shard.shape[1])
        for start in range(0, shard.shape[1], size):
            chunks.append((which, start, size, orders[len(chunks) % 2]))
    count = len(chunks)
    grid = (4, 2, 2, 2, share)
    anywhere = pl.BlockSpec(memory_space=pl.ANY)
    near = pl.BlockSpec(memory_space=pltpu.VMEM)
    results = pl.pallas_call(
        functools.partial(spread_kernel, chunks, len(shards)),
        out_shape=[jax.ShapeDtypeStruct(grid + (shard.shape[1],), bf16) for shard in shards]
        + [jax.ShapeDtypeStruct(values.shape, f32)],
        in_specs=[anywhere] * len(shards) + [near],
        out_specs=[anywhere] * len(shards) + [near],
        scratch_shapes=summing_scratch(values.shape)
        + [pltpu.SemaphoreType.DMA((len(shards),))]
        + [pltpu.SemaphoreType.DMA((count, 3))] * 4,
        compiler_params=pltpu.CompilerParams(collective_id=0, has_side_effects=True),
        name="spread_start",
    )(*shards, values)
    return [whole.reshape(32 * share, whole.shape[-1]) for whole in results[:-1]], results[-1]


def fold_kernel(chunks, last, values, out_last, out, running, came, sent, got,
                part, part_one, part_two, got_core, got_one, got_two, got_z, sents, gots):
    place = where_am_i()
    z, core = place[0], place[3]
    running[0] = values[...]
    greet()
    total = Summing(running, came, sent, got)
    copies = {}
    every = slice(None)

    def send(chunk, stage, source, target, partner):
        copy = pltpu.make_async_remote_copy(
            src_ref=source,
            dst_ref=target,
            send_sem=sents.at[chunk, stage],
            recv_sem=gots.at[chunk, stage],
            device_id=partner,
            device_id_type=MESH,
        )
        copy.start()
        copies[chunk, stage] = copy

    def sum_of(left, right):
        return (left.astype(f32) + right.astype(f32)).astype(bf16)

    for chunk, (start, size, order) in enumerate(chunks):
        block = last.at[:, :, :, 1 - core, :, pl.ds(start, size)]
        send(chunk, 0, block, got_core.at[chunk], neighbour(3))
    total.start()
    for time in range(len(chunks) + 3):
        for stage in range(1, 5):
            chunk = time - stage + 1
            if not 0 <= chunk < len(chunks):
                continue
            start, size, order = chunks[chunk]
            columns = pl.ds(start, size)
            near, far = order
            if stage == 1:
                copies[chunk, 0].wait_recv()
                part[chunk] = sum_of(last[:, :, :, core, :, columns], got_core[chunk])
                at = [every, every, every]
                at[near] = 1 - place[near]
                send(chunk, 1, part.at[(chunk, *at)], got_one.at[chunk], neighbour(near))
            elif stage == 2:
                copies[chunk, 1].wait_recv()
                at = [every, every, every]
                at[near] = place[near]
                part_one[chunk] = sum_of(part[(chunk, *at)], got_one[chunk])
                send(
                    chunk, 2, part_one.at[chunk, :, 1 - place[far]], got_two.at[chunk], neighbour(far)
                )
            elif stage == 3:
                copies[chunk, 2].wait_recv()
                part_two[chunk] = sum_of(part_one[chunk, :, place[far]], got_two[chunk])
                for away in (1, 2, 3):
                    source = part_two.at[chunk, (z + away) % 4]
                    send(chunk, 2 + away, source, got_z.at[chunk, away - 1], neighbour(0, away))
            else:
                whole = part_two[chunk, z].astype(f32)
                for away in (1, 2, 3):
                    copies[chunk, 2 + away].wait_recv()
                    whole = whole + got_z[chunk, away - 1].astype(f32)
                out_last[:, columns] = whole
        if time < 5:
            total.end()
            if time < 4:
                total.start()
    for step in range(len(chunks) + 3, 5):
        total.end()
        if step < 4:
            total.start()
    out[...] = running[5]
    for chunk in range(len(chunks)):
        for stage in range(6):
            copies[chunk, stage].wait_send()


def fold_end(last, values):
    rows, wide = last.shape
    share = rows // 32
    size = 128
    orders = ((1, 2), (2, 1))
    chunks = [(start, size, orders[(start // size) % 2]) for start in range(0, wide, size)]
    count = len(chunks)
    near = pl.BlockSpec(memory_space=pltpu.VMEM)
    return pl.pallas_call(
        functools.partial(fold_kernel, chunks),
        out_shape=[
            jax.ShapeDtypeStruct((share, wide), f32),
            jax.ShapeDtypeStruct(values.shape, f32),
        ],
        in_specs=[near, near],
        out_specs=[near, near],
        scratch_shapes=summing_scratch(values.shape)
        + [
            pltpu.VMEM((count, 4, 2, 2, share, size), bf16),
            pltpu.VMEM((count, 4, 2, share, size), bf16),
            pltpu.VMEM((count, 4, share, size), bf16),
            pltpu.VMEM((count, 4, 2, 2, share, size), bf16),
            pltpu.VMEM((count, 4, 2, share, size), bf16),
            pltpu.VMEM((count, 4, share, size), bf16),
            pltpu.VMEM((count, 3, share, size), bf16),
            pltpu.SemaphoreType.DMA((count, 6)),
            pltpu.SemaphoreType.DMA((count, 6)),
        ],
        compiler_params=pltpu.CompilerParams(
            collective_id=1, has_side_effects=True, vmem_limit_bytes=VMEM_BYTES
        ),
        name="fold_end",
    )(last.reshape(4, 2, 2, 2, share, wide), values)


class Ride:
    def __init__(self, arrays, lanes, columns, steps, collective):
        rows = arrays[0].shape[0]
        self.share = rows // 32
        self.arrays = [array.reshape(4, 2, 2, 2, self.share, array.shape[1]) for array in arrays]
        self.lanes, self.columns, self.steps, self.collective = lanes, columns, steps, collective
        self.size = 128
        while columns % self.size or columns // self.size + 4 > steps:
            self.size += 128
        self.chunks = columns // self.size

    def in_specs(self):
        return [pl.BlockSpec(memory_space=pl.ANY)] * len(self.arrays)

    def out_specs(self):
        return [pl.BlockSpec((self.share, self.columns), lambda *place: (0, 0))] * 2

    def out_shape(self):
        return [jax.ShapeDtypeStruct((self.share, self.columns), f32)] * 2

    def scratch(self):
        tail = (self.share, self.size)
        whole, half, quarter = (4, 2, 2) + tail, (4, 2) + tail, (4,) + tail
        every = (2, self.chunks)
        return [
            pltpu.VMEM((2, 2) + whole, bf16),
            pltpu.VMEM(every + whole, bf16),
            pltpu.VMEM(every + half, bf16),
            pltpu.VMEM(every + quarter, bf16),
            pltpu.VMEM(every + (3,) + tail, bf16),
            pltpu.VMEM((2, 2) + whole, bf16),
            pltpu.VMEM((2, 2) + half, bf16),
            pltpu.VMEM((2, 2) + quarter, bf16),
            pltpu.SemaphoreType.DMA((2, 2)),
            pltpu.SemaphoreType.DMA(every + (6,)),
            pltpu.SemaphoreType.DMA(every + (6,)),
        ]

    def step(self, time, sources, outs, scratch):
        own, got_core, got_one, got_two, got_z, part, part_one, part_two, own_sem, sents, gots = scratch
        place = where_am_i()
        z, core = place[0], place[3]
        count, size = self.chunks, self.size
        every = slice(None)

        def sum_of(left, right):
            return (left.astype(f32) + right.astype(f32)).astype(bf16)

        def copy_of(lane, chunk, stage):
            array, base = self.lanes[lane]
            near, far = ((1, 2), (2, 1))[lane]
            slot = chunk % 2
            if stage == 0:
                columns = pl.ds(pl.multiple_of(base + chunk * size, 128), size)
                source = sources[array].at[:, :, :, 1 - core, :, columns]
                target, partner = got_core.at[lane, chunk], neighbour(3)
            elif stage == 1:
                at = [every, every, every]
                at[near] = 1 - place[near]
                source, target = part.at[(lane, slot, *at)], got_one.at[lane, chunk]
                partner = neighbour(near)
            elif stage == 2:
                source = part_one.at[lane, slot, :, 1 - place[far]]
                target, partner = got_two.at[lane, chunk], neighbour(far)
            else:
                away = stage - 2
                source = part_two.at[lane, slot, (z + away) % 4]
                target, partner = got_z.at[lane, chunk, away - 1], neighbour(0, away)
            return pltpu.make_async_remote_copy(
                src_ref=source,
                dst_ref=target,
                send_sem=sents.at[lane, chunk, stage],
                recv_sem=gots.at[lane, chunk, stage],
                device_id=partner,
                device_id_type=MESH,
            )

        def own_copy(lane, chunk):
            array, base = self.lanes[lane]
            columns = pl.ds(pl.multiple_of(base + chunk * size, 128), size)
            source = sources[array].at[:, :, :, core, :, columns]
            slot = chunk % 2
            return pltpu.make_async_copy(source, own.at[lane, slot], own_sem.at[lane, slot])

        @pl.when(time == 0)
        def _():
            greet()

        for lane in range(2):
            near, far = ((1, 2), (2, 1))[lane]

            @pl.when(time < count)
            def _():
                copy_of(lane, time, 0).start()
                own_copy(lane, time).start()

            @pl.when((time >= 1) & (time < count + 1))
            def _():
                chunk = time - 1
                own_copy(lane, chunk).wait()
                copy_of(lane, chunk, 0).wait()

                @pl.when(chunk >= 2)
                def _():
                    copy_of(lane, chunk - 2, 1).wait_send()

                part[lane, chunk % 2] = sum_of(own[lane, chunk % 2], got_core[lane, chunk])
                copy_of(lane, chunk, 1).start()

            @pl.when((time >= 2) & (time < count + 2))
            def _():
                chunk = time - 2
                copy_of(lane, chunk, 1).wait_recv()

                @pl.when(chunk >= 2)
                def _():
                    copy_of(lane, chunk - 2, 2).wait_send()

                at = [every, every, every]
                at[near] = place[near]
                mine = part[(lane, chunk % 2, *at)]
                part_one[lane, chunk % 2] = sum_of(mine, got_one[lane, chunk])
                copy_of(lane, chunk, 2).start()

            @pl.when((time >= 3) & (time < count + 3))
            def _():
                chunk = time - 3
                copy_of(lane, chunk, 2).wait_recv()

                @pl.when(chunk >= 2)
                def _():
                    for away in (1, 2, 3):
                        copy_of(lane, chunk - 2, 2 + away).wait_send()

                mine = part_one[lane, chunk % 2, :, place[far]]
                part_two[lane, chunk % 2] = sum_of(mine, got_two[lane, chunk])
                for away in (1, 2, 3):
                    copy_of(lane, chunk, 2 + away).start()

            @pl.when((time >= 4) & (time < count + 4))
            def _():
                chunk = time - 4
                whole = part_two[lane, chunk % 2, z].astype(f32)
                for away in (1, 2, 3):
                    copy_of(lane, chunk, 2 + away).wait_recv()
                    whole = whole + got_z[lane, chunk, away - 1].astype(f32)
                outs[lane][:, pl.ds(pl.multiple_of(chunk * size, 128), size)] = whole

        @pl.when(time == self.steps - 1)
        def _():
            for lane in range(2):
                for chunk in range(max(count - 2, 0), count):
                    for stage in range(1, 6):
                        copy_of(lane, chunk, stage).wait_send()


class NoRide:
    arrays = ()
    collective = None
    in_specs = out_specs = out_shape = scratch = lambda self: []

    def step(self, *unused):
        pass


class Links:
    def __init__(self, sizes):
        self.plain = sizes != (4, 2, 4)

    def start(self, shards, values):
        if not self.plain:
            return spread_start(shards, values)
        gather = lambda shard: lax.all_gather(shard, ALL, axis=0, tiled=True)
        return [gather(shard) for shard in shards], lax.psum(values, ALL)

    def ride(self, arrays, lanes, columns, steps, collective):
        return NoRide() if self.plain else Ride(arrays, lanes, columns, steps, collective)

    def scatter(self, values, done):
        if not self.plain:
            return jnp.concatenate(done, 1)
        return lax.psum_scatter(values, ALL, scatter_dimension=0, tiled=True).astype(f32)

    def end(self, last, values):
        if not self.plain:
            return fold_end(last, values)
        total = lax.psum_scatter(last, ALL, scatter_dimension=0, tiled=True).astype(f32)
        return total, lax.psum(values, ALL)

    def total(self, values):
        return lax.psum(values, ALL) if self.plain else small_sum(values)


def entry_kernel(query_blocks, field, embed, weight, mod, stream, hidden, mixed):
    width = embed.shape[0]
    stream_zero = contract(field[...], embed[...], 1, 1)
    stream[...] = stream_zero
    normed, unused = layer_norm(stream_zero)
    low = (normed * (1.0 + mod[1:2, :]) + mod[0:1, :]).astype(bf16)
    hidden[...] = low
    for part in (1, 2):
        columns = pl.ds(part * width, width)
        mixed[:, columns] = contract(low, weight[:, columns], 1, 0).astype(bf16)

    @pl.when(pl.program_id(0) < query_blocks)
    def _():
        queries = contract(low, weight[:, 0:width], 1, 0)
        mixed[:, 0:width] = (queries * QUERY_SCALE).astype(bf16)


def entry(fields, embed, weight, mod, block, query_rows, unit_of):
    rows, pieces = fields.shape
    width = embed.shape[0]
    by_row = lambda columns: pl.BlockSpec((block, columns), lambda i: (i, 0))
    return pl.pallas_call(
        functools.partial(entry_kernel, query_rows // block),
        grid=(rows // block,),
        in_specs=[
            by_row(pieces),
            resident(embed.shape),
            resident(weight.shape),
            pl.BlockSpec((None,) + mod.shape[1:], lambda i: (unit_of(i), 0, 0)),
        ],
        out_specs=[by_row(width), by_row(width), by_row(3 * width)],
        out_shape=[
            jax.ShapeDtypeStruct((rows, width), f32),
            jax.ShapeDtypeStruct((rows, width), bf16),
            jax.ShapeDtypeStruct((rows, 3 * width), bf16),
        ],
        cost_estimate=pl.CostEstimate(
            flops=8 * rows * width * width, bytes_accessed=12 * rows * width, transcendentals=0
        ),
        compiler_params=pltpu.CompilerParams(vmem_limit_bytes=VMEM_BYTES),
        name="entry",
    )(fields, embed, weight, mod)


def crossed():
    row = lax.broadcasted_iota(jnp.int32, (2 * HD, 2 * HD), 0) < HD
    column = lax.broadcasted_iota(jnp.int32, (2 * HD, 2 * HD), 1) < HD
    return jnp.where(row != column, 1.0, 0.0).astype(bf16)


def attend_kernel(sub, query, key, value, out, kept, inverse, value_t, key_one, stats):
    block, keys = query.shape[0], key.shape[0]
    zero, one = jnp.zeros((), bf16), jnp.ones((), bf16)

    @pl.when(pl.program_id(1) == 0)
    def _():
        turned = jnp.transpose(value[...])
        first_rows = lax.broadcasted_iota(jnp.int32, (2 * HD, keys), 0) < HD
        value_t[0] = jnp.where(first_rows, turned, one)
        value_t[1] = jnp.where(first_rows, one, turned)
        first_lanes = lax.broadcasted_iota(jnp.int32, (keys, 2 * HD), 1) < HD
        both = key[...]
        key_one[0] = jnp.where(first_lanes, both, one)
        key_one[1] = jnp.where(first_lanes, one, both)
        wide = both.astype(f32)
        mean = jnp.mean(wide, 0, keepdims=True)
        spread = ((wide - mean) * (wide - mean)).astype(bf16)
        stats[0:1] = mean
        far = jnp.max(contract(spread, crossed(), 1, 0), 0, keepdims=True)
        stats[1:2] = 0.5 * jnp.sqrt(far)

    lanes = lax.broadcasted_iota(jnp.int32, (sub, 2 * HD), 1)
    wide = query[...].astype(f32)
    length = jnp.sqrt(contract((wide * wide).astype(bf16), crossed(), 1, 0))
    reach = length * stats[1:2]
    shifts = (-contract((wide * stats[0:1]).astype(bf16), crossed(), 1, 0) - reach).astype(bf16)
    near = jnp.max(reach) <= 60.0
    upper = lax.broadcasted_iota(jnp.int32, (2 * HD, sub), 0) < HD

    def run(exact):
        for part in range(block // sub):
            rows = pl.ds(part * sub, sub)
            results = []
            for head in range(2):
                mine = (lanes < HD) if head == 0 else (lanes >= HD)
                if exact:
                    moved = jnp.where(mine, query[rows, :], zero)
                    scores = contract(key_one[head], moved, 1, 1)
                    scores = scores - jnp.max(scores, 0, keepdims=True)
                else:
                    free = HD if head == 0 else 0
                    rest = jnp.where(lanes == free, shifts[part * sub : part * sub + sub], zero)
                    moved = jnp.where(mine, query[rows, :], rest)
                    scores = contract(key_one[head], moved, 1, 1)
                weights = jnp.exp2(scores).astype(bf16)
                kept[head, :, rows] = weights
                results.append(contract(value_t[head], weights, 1, 0))
            total = jnp.where(
                upper, pltpu.roll(results[0], HD, 0), pltpu.roll(results[1], HD, 0)
            )
            above = 1.0 / total
            mean = jnp.where(upper, results[0], results[1]) * above
            out[rows, :] = jnp.transpose(mean).astype(bf16)
            inverse[0:1, rows] = above[0:1]
            inverse[1:2, rows] = above[HD : HD + 1]

    @pl.when(near)
    def _():
        run(False)

    @pl.when(jnp.logical_not(near))
    def _():
        run(True)


def attend(queries, memory, places, block, sub, count, keys, width):
    pairs = width // (2 * HD)
    query_at, key_at, key_column, value_column = places
    return pl.pallas_call(
        functools.partial(attend_kernel, sub),
        grid=(pairs, count // block),
        in_specs=[
            pl.BlockSpec((block, 2 * HD), lambda h, i: (query_at // block + i, h)),
            pl.BlockSpec((keys, 2 * HD), lambda h, i: (key_at // keys, key_column * pairs + h)),
            pl.BlockSpec((keys, 2 * HD), lambda h, i: (key_at // keys, value_column * pairs + h)),
        ],
        out_specs=[
            pl.BlockSpec((block, 2 * HD), lambda h, i: (i, h)),
            pl.BlockSpec((None, None, 2, keys, block), lambda h, i: (h, i, 0, 0, 0)),
            pl.BlockSpec((None, 2, block), lambda h, i: (h, 0, i)),
        ],
        out_shape=[
            jax.ShapeDtypeStruct((count, width), bf16),
            jax.ShapeDtypeStruct((pairs, count // block, 2, keys, block), bf16),
            jax.ShapeDtypeStruct((pairs, 2, count), f32),
        ],
        scratch_shapes=[
            pltpu.VMEM((2, 2 * HD, keys), bf16),
            pltpu.VMEM((2, keys, 2 * HD), bf16),
            pltpu.VMEM((8, 2 * HD), f32),
        ],
        cost_estimate=pl.CostEstimate(
            flops=20 * count * keys * width, bytes_accessed=2 * count * keys, transcendentals=0
        ),
        compiler_params=pltpu.CompilerParams(vmem_limit_bytes=VMEM_BYTES),
        name="attend",
    )(queries, memory, memory)


def attend_back_kernel(
    sub, query, key, value, grad, out, kept, inverse,
    grad_query, grad_key, grad_value, key_t, value_one, key_sum, value_sum,
):
    block, keys = query.shape[0], key.shape[0]
    step, steps = pl.program_id(1), pl.num_programs(1)
    zero = jnp.zeros((), bf16)

    @pl.when(step == 0)
    def _():
        first_rows = lax.broadcasted_iota(jnp.int32, (2 * HD, keys), 0) < HD
        turned = jnp.transpose(key[...])
        key_t[0] = jnp.where(first_rows, turned, zero)
        key_t[1] = jnp.where(first_rows, zero, turned)
        first_lanes = lax.broadcasted_iota(jnp.int32, (keys, 2 * HD), 1) < HD
        minus = jnp.full((), -1.0, bf16)
        value_one[0] = jnp.where(first_lanes, value[...], minus)
        value_one[1] = jnp.where(first_lanes, minus, value[...])
        key_sum[...] = jnp.zeros_like(key_sum)
        value_sum[...] = jnp.zeros_like(value_sum)

    lanes = lax.broadcasted_iota(jnp.int32, (sub, 2 * HD), 1)
    places = lax.broadcasted_iota(jnp.int32, (2 * HD, sub), 0)
    upper = places < HD
    for part in range(block // sub):
        rows = pl.ds(part * sub, sub)
        above = jnp.where(upper, inverse[0:1, rows], inverse[1:2, rows])
        scaled = (jnp.transpose(grad[rows, :].astype(f32)) * above).astype(bf16)
        product = scaled.astype(f32) * jnp.transpose(out[rows, :].astype(f32))
        natural = jnp.transpose(scaled)
        queries = query[rows, :]
        turned = None
        for head in range(2):
            delta = jnp.sum(product[HD * head : HD * head + HD], 0, keepdims=True)
            high = delta.astype(bf16)
            rest = (delta - high.astype(f32)).astype(bf16)
            free = HD if head == 0 else 0
            mine = upper if head == 0 else jnp.logical_not(upper)
            extra = jnp.where(places == free, high, jnp.where(places == free + 1, rest, zero))
            grad_probs = contract(value_one[head], jnp.where(mine, scaled, extra), 1, 0)
            weights = kept[head, :, rows]
            grad_scores = grad_probs.astype(bf16) * weights
            own = (lanes < HD) if head == 0 else (lanes >= HD)
            value_sum[...] += contract(weights, jnp.where(own, natural, zero), 1, 0)
            key_sum[...] += contract(grad_scores, jnp.where(own, queries, zero), 1, 0)
            term = contract(key_t[head], grad_scores, 1, 0)
            turned = term if turned is None else turned + term
        grad_query[rows, :] = (jnp.transpose(turned) * 0.125).astype(bf16)

    @pl.when(step == steps - 1)
    def _():
        grad_key[...] = (key_sum[...] * LN2).astype(bf16)
        grad_value[...] = value_sum[...].astype(bf16)


def attend_back(queries, memory, grads, out, kept, inverse, places, block, sub, into, shapes, ride):
    query_at, key_at, key_column, value_column, grad_query_at, grad_key_at = places
    count, keys = out.shape[0], kept.shape[3]
    pairs = out.shape[1] // (2 * HD)
    two = 2 * HD
    steps = count // block
    given, riding = len(into), len(ride.arrays)

    def kernel(*refs):
        ins, refs = refs[:7], refs[7 + given :]
        sources, refs = refs[:riding], refs[riding:]
        outs, refs = refs[:3], refs[3:]
        sums, refs = refs[: 2 * bool(riding)], refs[2 * bool(riding) :]
        ride.step(pl.program_id(0) * steps + pl.program_id(1), sources, sums, refs[4:])
        attend_back_kernel(sub, *ins, *outs, *refs[:4])

    work = pairs * count * keys * two
    results = pl.pallas_call(
        kernel,
        grid=(pairs, steps),
        in_specs=[
            pl.BlockSpec((block, two), lambda h, i: (query_at // block + i, h)),
            pl.BlockSpec((keys, two), lambda h, i: (key_at // keys, key_column * pairs + h)),
            pl.BlockSpec((keys, two), lambda h, i: (key_at // keys, value_column * pairs + h)),
            pl.BlockSpec((block, two), lambda h, i: (query_at // block + i, h)),
            pl.BlockSpec((block, two), lambda h, i: (i, h)),
            pl.BlockSpec((None, None, 2, keys, block), lambda h, i: (h, i, 0, 0, 0)),
            pl.BlockSpec((None, 2, block), lambda h, i: (h, 0, i)),
        ]
        + [pl.BlockSpec(memory_space=pl.ANY)] * given
        + ride.in_specs(),
        out_specs=[
            pl.BlockSpec((block, two), lambda h, i: (grad_query_at // block + i, h)),
            pl.BlockSpec((keys, two), lambda h, i: (grad_key_at // keys, h)),
            pl.BlockSpec((keys, two), lambda h, i: (grad_key_at // keys, h)),
        ]
        + ride.out_specs(),
        out_shape=[jax.ShapeDtypeStruct(shape, bf16) for shape in shapes] + ride.out_shape(),
        scratch_shapes=[
            pltpu.VMEM((2, two, keys), bf16),
            pltpu.VMEM((2, keys, two), bf16),
            pltpu.VMEM((keys, two), f32),
            pltpu.VMEM((keys, two), f32),
        ]
        + ride.scratch(),
        input_output_aliases={7 + index: index for index in range(given)},
        cost_estimate=pl.CostEstimate(flops=32 * work, bytes_accessed=4 * work // HD, transcendentals=0),
        compiler_params=pltpu.CompilerParams(
            vmem_limit_bytes=VMEM_BYTES,
            collective_id=ride.collective,
            has_side_effects=riding > 0,
        ),
        name="attend_back",
    )(queries, memory, memory, grads, out, kept, inverse, *into, *ride.arrays)
    return results[:3], results[3:]


def middle_kernel(
    parts, attended, stream, target, weight_rows, mod, combine, first, second, read,
    hidden, active, grad_two, grad_inner, final, grad_read, grad_one, grad_attended, grad_stream,
    sums, losses, slopes,
):
    block = attended.shape[0]
    width, spread = first.shape
    size_tile = min(TILE, spread)
    tiles = [pl.ds(start, size_tile) for start in range(0, spread, size_tile)]
    gate_a, shift_b, scale_b = mod[2:3, :], mod[3:4, :], mod[4:5, :]
    gate_b, gain = mod[5:6, :], mod[6:7, :]

    def run(rows, found):
        branch_a = contract(attended[rows, :], combine[...], 1, 0)
        yield
        stream_one = stream[rows, :] + gate_a * branch_a
        norm_b, inverse_b = layer_norm(stream_one)
        low = (norm_b * (1.0 + scale_b) + shift_b).astype(bf16)
        hidden[rows, :] = low
        yield
        branch_b = None
        ahead = contract(low, first[:, tiles[0]], 1, 0)
        for index, tile in enumerate(tiles):
            inner = ahead
            if index + 1 < len(tiles):
                ahead = contract(low, first[:, tiles[index + 1]], 1, 0)
            yield
            value, slope = gelu_pair(inner)
            value = value.astype(bf16)
            active[rows, tile] = value
            slopes[rows, tile] = slope.astype(bf16)
            term = contract(value, second[:, tile], 1, 1)
            branch_b = term if branch_b is None else branch_b + term
            yield
        norm_c, inverse_c = layer_norm(stream_one + gate_b * branch_b)
        last = (norm_c * gain).astype(bf16)
        final[rows, :] = last
        yield
        diff = contract(last, read[...], 1, 0) - target[rows, :].astype(f32)
        found[0] = column_sum(weight_rows[rows, 0:1] * diff * diff)
        grad_low = (weight_rows[rows, 1:2] * diff).astype(bf16)
        grad_read[rows, :] = grad_low
        grad_final = contract(grad_low, read[...], 1, 1)
        yield
        found[6] = column_sum(grad_final * norm_c)
        grad = norm_back(grad_final * gain, norm_c, inverse_c)
        found[5] = column_sum(grad * branch_b)
        back = (grad * gate_b).astype(bf16)
        grad_two[rows, :] = back
        yield
        grad_hidden = None
        ahead = contract(back, second[:, tiles[0]], 1, 0)
        for index, tile in enumerate(tiles):
            inner = ahead
            if index + 1 < len(tiles):
                ahead = contract(back, second[:, tiles[index + 1]], 1, 0)
            yield
            inner = (inner * slopes[rows, tile].astype(f32)).astype(bf16)
            grad_inner[rows, tile] = inner
            term = contract(inner, first[:, tile], 1, 1)
            grad_hidden = term if grad_hidden is None else grad_hidden + term
            yield
        found[3] = column_sum(grad_hidden)
        found[4] = column_sum(grad_hidden * norm_b)
        grad = grad + norm_back(grad_hidden * (1.0 + scale_b), norm_b, inverse_b)
        grad_stream[rows, :] = grad
        found[2] = column_sum(grad * branch_a)
        back = (grad * gate_a).astype(bf16)
        grad_one[rows, :] = back
        yield
        grad_attended[rows, :] = contract(back, combine[...], 1, 1).astype(bf16)

    size = block // parts
    found = [{} for part in range(parts)]
    runs = [run(pl.ds(part * size, size), found[part]) for part in range(parts)]
    while runs:
        runs = [one for one in runs if next(one, runs) is not runs]
    losses[...] = jnp.broadcast_to(sum(one[0] for one in found), losses.shape)
    for row in (2, 3, 4, 5, 6):
        sums[row : row + 1, :] = sum(one[row] for one in found)
    sums[0:2, :] = jnp.zeros((2, width), f32)
    sums[7:8, :] = jnp.zeros((1, width), f32)


def middle(attended, stream, target, weight_rows, mod, combine, first, second, read, block, unit_of):
    rows, width = attended.shape
    spread, pieces = first.shape[1], read.shape[1]
    blocks = rows // block
    by_row = lambda columns: pl.BlockSpec((block, columns), lambda i: (i, 0))
    shape = lambda columns, kind: jax.ShapeDtypeStruct((rows, columns), kind)
    outs = (
        (width, bf16), (spread, bf16), (width, bf16), (spread, bf16), (width, bf16), (pieces, bf16),
        (width, bf16), (width, bf16), (width, f32),
    )
    return pl.pallas_call(
        functools.partial(middle_kernel, 1),
        grid=(blocks,),
        in_specs=[
            by_row(width),
            by_row(width),
            by_row(pieces),
            by_row(2),
            pl.BlockSpec((None,) + mod.shape[1:], lambda i: (unit_of(i), 0, 0)),
            resident(combine.shape),
            resident(first.shape),
            resident(second.shape),
            resident(read.shape),
        ],
        out_specs=[by_row(columns) for columns, kind in outs]
        + [
            pl.BlockSpec((None, 8, width), lambda i: (i, 0, 0)),
            pl.BlockSpec((None, 8, pieces), lambda i: (i, 0, 0)),
        ],
        out_shape=[shape(columns, kind) for columns, kind in outs]
        + [
            jax.ShapeDtypeStruct((blocks, 8, width), f32),
            jax.ShapeDtypeStruct((blocks, 8, pieces), f32),
        ],
        scratch_shapes=[pltpu.VMEM((block, spread), bf16)],
        cost_estimate=pl.CostEstimate(
            flops=60 * rows * width * width, bytes_accessed=40 * rows * width, transcendentals=0
        ),
        compiler_params=pltpu.CompilerParams(vmem_limit_bytes=VMEM_BYTES),
        name="middle",
    )(attended, stream, target, weight_rows, mod, combine, first, second, read)


def leave_kernel(query_blocks, grad_query, grad_key, grad_value, stream, grad_stream, weight, mod, out, sums, held):
    width = stream.shape[1]
    asks = pl.program_id(0) < query_blocks
    columns = lambda kind: pl.ds(kind * width, width)
    held[...] = contract(grad_key[...], weight[:, columns(1)], 1, 1)
    held[...] += contract(grad_value[...], weight[:, columns(2)], 1, 1)

    @pl.when(asks)
    def _():
        held[...] += contract(grad_query[...], weight[:, columns(0)], 1, 1)

    normed, inverse = layer_norm(stream[...])
    grad_hidden = held[...]
    sums[0:1, :] = column_sum(grad_hidden)
    sums[1:2, :] = column_sum(grad_hidden * normed)
    sums[2:8, :] = jnp.zeros((6, width), f32)
    grad = norm_back(grad_hidden * (1.0 + mod[1:2, :]), normed, inverse)
    grad = grad + jnp.where(asks, grad_stream[...], 0.0)
    out[...] = grad.astype(bf16)


def leave(grads, stream, grad_stream, weight, mod, block, unit_of, ride):
    rows, width = stream.shape
    asking = grads[0].shape[0] // block
    blocks, riding = rows // block, len(ride.arrays)
    by_row = pl.BlockSpec((block, width), lambda i: (i, 0))
    asked = pl.BlockSpec((block, width), lambda i: (jnp.minimum(i, asking - 1), 0))

    def kernel(*refs):
        ins, refs = refs[:7], refs[7:]
        sources, refs = refs[:riding], refs[riding:]
        outs, refs = refs[:2], refs[2:]
        shards, refs = refs[: 2 * bool(riding)], refs[2 * bool(riding) :]
        ride.step(pl.program_id(0), sources, shards, refs[1:])
        leave_kernel(asking, *ins, *outs, refs[0])

    results = pl.pallas_call(
        kernel,
        grid=(blocks,),
        in_specs=[
            asked,
            by_row,
            by_row,
            by_row,
            asked,
            resident(weight.shape),
            pl.BlockSpec((None,) + mod.shape[1:], lambda i: (unit_of(i), 0, 0)),
        ]
        + ride.in_specs(),
        out_specs=[by_row, pl.BlockSpec((None, 8, width), lambda i: (i, 0, 0))] + ride.out_specs(),
        out_shape=[
            jax.ShapeDtypeStruct((rows, width), bf16),
            jax.ShapeDtypeStruct((blocks, 8, width), f32),
        ]
        + ride.out_shape(),
        scratch_shapes=[pltpu.VMEM((block, width), f32)] + ride.scratch(),
        cost_estimate=pl.CostEstimate(
            flops=7 * rows * width * width, bytes_accessed=16 * rows * width, transcendentals=0
        ),
        compiler_params=pltpu.CompilerParams(
            vmem_limit_bytes=VMEM_BYTES,
            collective_id=ride.collective,
            has_side_effects=riding > 0,
        ),
        name="leave",
    )(*grads, stream, grad_stream, weight, mod, *ride.arrays)
    return results[:2], results[2:]


def adam(master, first, second, grad, factor, step_rate):
    grad = grad * factor
    first_new = beta_one * first + (1.0 - beta_one) * grad
    second_new = beta_two * second + (1.0 - beta_two) * grad * grad
    corrected = (
        first_new
        / (1.0 - beta_one**STEP)
        / (jnp.sqrt(second_new / (1.0 - beta_two**STEP)) + epsilon)
    )
    return (master - step_rate * (corrected + decay * master), first_new, second_new)


def largest(limit, *sizes):
    block = limit
    while any(size % block for size in sizes):
        block //= 2
    return block


def body(sizes, *args):
    ways = sizes[1]
    links = Links(sizes)
    fields, targets, interval, storm_index, valid_count, latitude, storm_scale = args[:7]
    masters, firsts, seconds = args[7:15], args[15:23], args[23:31]
    embedding, intervals, modulator, projector, combiner, feedforward, readout, vectors = masters
    micros, samples_dev, part, pieces = fields.shape
    patches = latitude.shape[0]
    units = micros * samples_dev
    share, width = projector.shape[0], projector.shape[1] // 3
    place = lax.axis_index("seq")
    device = lax.axis_index(ALL)
    sample_start = lax.axis_index(("dp", "fsdp")) * samples_dev
    ring = [(index, 1 - index) for index in range(2)]
    alone = units // 2 if ways == 2 else 0
    shared = units - ways * alone
    have = alone + shared

    everywhere = jnp.arange(patches, dtype=jnp.int32)
    mask = (everywhere[None, None, :] >= patches - valid_count[:, :, None]).astype(f32)
    levels = jnp.arange(storm_scale.shape[0], dtype=jnp.int32)
    storms = jnp.sum(jnp.where(storm_index[:, :, None] == levels, storm_scale, 0.0), -1)
    row_weights = latitude[None, None, :] * storms[:, :, None] * mask
    total_weight = pieces * jnp.sum(row_weights)

    def local(values):
        cut = lax.dynamic_slice_in_dim(values, sample_start, samples_dev, 1)
        cut = cut.reshape((units,) + values.shape[2:])
        mine = [lax.dynamic_slice_in_dim(cut, place * alone, alone, 0)] if alone else []
        return jnp.concatenate(mine + [cut[ways * alone :]], 0)

    kinds = local(interval)
    weights_unit = jnp.roll(local(row_weights), -place * part, 1)
    weights_rows = jnp.concatenate(
        [weights_unit[:alone].reshape(-1), weights_unit[alone:, :part].reshape(-1)]
    )
    weight_rows = jnp.stack([weights_rows, weights_rows * (2.0 / total_weight)], 1)

    def widen(values):
        flat = values.reshape(units, part, pieces)
        return jnp.pad(flat, ((0, 0), (0, 0), (0, WIDE - pieces)))

    own, goal = widen(fields), widen(targets)
    if alone:
        away = (1 - place) * alone
        cut = lambda values, start: lax.dynamic_slice_in_dim(values, start, alone, 0)
        sent = jnp.concatenate([cut(own, away), own[2 * alone :]], 0)
        came = lax.ppermute(sent, "seq", ring)
        goal_came = lax.ppermute(cut(goal, away), "seq", ring)
        whole = jnp.concatenate([cut(own, place * alone), came[:alone]], 1)
        goal_whole = jnp.concatenate([cut(goal, place * alone), goal_came], 1)
        rows = [whole, own[2 * alone :], came[alone:]]
        goals = [goal_whole, goal[2 * alone :]]
    elif ways == 1:
        rows, goals = [own], [goal]
    else:
        everyone = lax.all_gather(own, "seq", axis=1, tiled=True)
        rows = [own, jnp.roll(everyone, -place * part, 1)[:, part:]]
        goals = [goal]
    flatten = lambda parts: jnp.concatenate([piece.reshape(-1, WIDE) for piece in parts], 0)
    all_rows, goal_rows = flatten(rows), flatten(goals)
    asking = (alone * ways + shared) * part

    def unit_of(block):
        whole_blocks = alone * patches // block
        own_blocks = shared * part // block
        other = max((patches - part) // block, 1)

        def at(i):
            late = alone + (i - whole_blocks) // (part // block)
            later = alone + (i - whole_blocks - own_blocks) // other
            late = jnp.where(i < whole_blocks + own_blocks, late, later)
            return jnp.where(i < whole_blocks, i // (patches // block), late)

        return at

    low = [master.astype(bf16) for master in masters]
    step_vec = low[1].astype(f32)
    active = jax.nn.silu(step_vec)
    active_low = active.astype(bf16)
    table = contract(active_low, low[2], 1, 0)
    spread_vectors = lax.dynamic_update_slice(
        jnp.zeros((7, width), f32), low[7].astype(f32), (0, device * share)
    )
    to_wide = lambda values: jnp.pad(values, ((0, 0), (0, WIDE - pieces)))
    (embed, project, read), carried = links.start(
        (to_wide(low[0].T), low[3], to_wide(low[6])),
        jnp.concatenate([table.reshape(3 * 6 * width // 128, 128), spread_vectors.reshape(-1, 128)]),
    )
    nothing = carried[0, 0] * 0.0
    carried = carried.reshape(-1)
    table = carried[: table.size].reshape(DTK, 6, width)
    all_vectors = carried[table.size :].reshape(7, width)
    table = table + all_vectors[None, :6]
    chosen = sum(jnp.where(kinds[:, None, None] == kind, table[kind], 0.0) for kind in range(DTK))
    gain = jnp.broadcast_to(all_vectors[6], (have, 1, width))
    mod = jnp.concatenate([chosen, gain, jnp.zeros((have, 1, width), f32)], 1)

    gather = lambda values: lax.all_gather(values, ALL, axis=0, tiled=True)
    late = (combiner, feedforward[0], feedforward[1])
    combine, first, second = [gather((shard + nothing).astype(bf16)) for shard in late]

    block = largest(512, part)
    stream, hidden_a, mixed = entry(all_rows, embed, project, mod, block, asking, unit_of(block))

    calls = []
    for unit in range(have):
        if unit < alone:
            start = unit * patches
            calls.append((patches, mixed, (start, start, 1, 2)))
        else:
            start = alone * patches + (unit - alone) * part
            behind = asking + (unit - alone) * (patches - part)
            if shared == 1 and start % patches == 0:
                calls.append((part, mixed, (start, start, 1, 2)))
            else:
                joined = jnp.concatenate(
                    [
                        mixed[start : start + part, width:],
                        mixed[behind : behind + patches - part, width:],
                    ],
                    0,
                )
                calls.append((part, joined, (start, 0, 0, 1)))
    saved = []
    for count, memory, where in calls:
        block = largest(1024, count, where[0] if where[0] else count)
        saved.append(attend(mixed, memory, where, block, block, count, patches, width))
    attended_rows = jnp.concatenate([out for out, kept, inverse in saved], 0)

    block = largest(256, part)
    (
        hidden_b, activated, grad_two, grad_inner, final, grad_read, grad_one, grad_attended,
        grad_stream, sums, losses,
    ) = middle(
        attended_rows, stream, goal_rows, weight_rows, mod, combine, first, second, read, block,
        unit_of(block),
    )
    units_mid = [unit_of(block)(jnp.int32(i)) for i in range(sums.shape[0])]
    loss_local = jnp.sum(losses[:, 0, :])

    summed = lambda left, right: contract(left, right, 0, 0).astype(bf16)
    grad_first, grad_second = summed(hidden_b, grad_inner), summed(grad_two, activated)
    grad_combine, grad_readout = summed(attended_rows, grad_one), summed(final, grad_read)
    rest = jnp.concatenate([grad_combine, grad_readout, jnp.zeros((width, WIDE // 3), bf16)], 1)
    rides = [((grad_first, grad_second), ((0, 0), (1, 0)), grad_first.shape[1])]
    rides += [((rest,), ((0, 0), (0, rest.shape[1] // 2)), rest.shape[1] // 2)]
    shapes = ((asking, width), (have * patches, width), (have * patches, width))
    into, done = (), []
    for unit, ((count, memory, where), (out, kept, inverse)) in enumerate(zip(calls, saved)):
        block = kept.shape[4]
        ride = NoRide()
        if unit < len(rides):
            steps = width // (2 * HD) * (count // block)
            ride = links.ride(*rides[unit], steps, 3 + unit)
        into, ridden = attend_back(
            mixed, memory, grad_attended, out, kept, inverse, where + (where[0], unit * patches),
            block, min(block, 256), into, shapes, ride,
        )
        done.append(ridden)
    shard_first = links.scatter(grad_first, done[0][:1])
    shard_second = links.scatter(grad_second, done[0][1:])
    shard_rest = links.scatter(rest, done[1])
    shard_combine, shard_read = shard_rest[:, :width], shard_rest[:, width : width + WIDE]
    if not (alone and shared <= 1):
        own_part = lambda values, unit, low_row, high_row: values[
            unit * patches + low_row : unit * patches + high_row
        ]
        into = (into[0],) + tuple(
            jnp.concatenate(
                [values[: alone * patches]]
                + [own_part(values, unit, 0, part) for unit in range(alone, have)]
                + [own_part(values, unit, part, patches) for unit in range(alone, have)],
                0,
            )
            for values in into[1:]
        )
    grad_project = jnp.concatenate(
        [summed(hidden_a[:asking], into[0])] + [summed(hidden_a, values) for values in into[1:]], 1
    )
    block = largest(512, part)
    lane = grad_project.shape[1] // 2
    ride = links.ride((grad_project,), ((0, 0), (0, lane)), lane, stream.shape[0] // block, 5)
    (grad_zero, sums_a), ridden = leave(
        into, stream, grad_stream, project, mod, block, unit_of(block), ride
    )
    shard_project = links.scatter(grad_project, ridden)
    units_out = [unit_of(block)(jnp.int32(i)) for i in range(sums_a.shape[0])]
    grad_embed = summed(grad_zero, all_rows)

    by_block = jnp.concatenate([sums, sums_a], 0)
    kind_block = kinds[jnp.stack(units_mid + units_out)]
    grad_table = jnp.stack(
        [
            jnp.sum(jnp.where((kind_block == kind)[:, None, None], by_block, 0.0), 0)
            for kind in range(DTK)
        ]
    )
    loss_row = jnp.full((1, 128), loss_local)
    small = jnp.concatenate([grad_table[:, :7].reshape(-1, 128), loss_row])
    shard_embed, carried = links.end(grad_embed, small)
    loss_total = carried[-1, 0]
    grad_table = carried[:-1].reshape(DTK, 7, width)
    grad_mod = grad_table[:, :6].reshape(DTK, 6 * width)
    shard_vectors = lax.dynamic_slice_in_dim(jnp.sum(grad_table, 0), device * share, share, 1)
    active_wide = active_low.astype(f32)
    shard_modulator = sum(
        active_wide[kind][:, None] * grad_mod[kind][None, :] for kind in range(DTK)
    )
    grad_active = jnp.stack(
        [jnp.sum(low[2].astype(f32) * grad_mod[kind][None, :], 1) for kind in range(DTK)]
    )
    unused, silu_back = jax.vjp(jax.nn.silu, step_vec)
    shard_intervals = silu_back(grad_active)[0]

    shards = (
        shard_embed[:, :pieces].T,
        shard_intervals,
        shard_modulator,
        shard_project,
        shard_combine,
        jnp.stack([shard_first, shard_second]),
        shard_read[:, :pieces],
        shard_vectors,
    )
    squares = sum(jnp.sum(grad * grad) for grad in shards)
    squares = links.total(jnp.full((8, 128), squares))[0, 0]
    norm = jnp.sqrt(squares)
    factor = clip_norm / jnp.maximum(norm, clip_norm)
    results = [
        adam(master, first_moment, second_moment, grad, factor, rate)
        for master, first_moment, second_moment, grad, rate in zip(
            masters, firsts, seconds, shards, step_rates()
        )
    ]
    return tuple(result[index] for index in range(3) for result in results) + (
        loss_total,
        total_weight,
        norm,
    )


def solution(mesh):
    data = P(None, ("dp", "fsdp"), "seq", None)
    columns, rows = P(None, ALL), P(ALL, None)
    weights = (columns, columns, rows, rows, rows, P(None, ALL, None), rows, columns)
    return jax.shard_map(
        functools.partial(body, tuple(mesh.shape[axis] for axis in ALL)),
        mesh=mesh,
        in_specs=(data, data) + (P(),) * 5 + weights * 3,
        out_specs=weights * 3 + (P(),) * 3,
        check_vma=False,
    )
```

```python
import functools

import jax
import jax.numpy as jnp
from jax import lax
from jax.experimental import pallas as pl
from jax.experimental.pallas import tpu as pltpu
from jax.sharding import PartitionSpec as P

D = 1024
HD = 64
PIN = 276
WIDE = 384
DTK = 3
STEP = 10
PATCHES = 2048
ALL = ("dp", "seq", "fsdp")

beta_one = 0.9
beta_two = 0.999
decay = 0.01
epsilon = 1e-08
clip_norm = 0.005
norm_eps = 1e-06
bf16 = jnp.bfloat16
f32 = jnp.float32
LN2 = 0.6931471805599453
QUERY_SCALE = 0.125 / LN2
VMEM_BYTES = 60 * 2**20
ERF = (
    0.7978822138768258,
    0.03634467259297056,
    -4.4877727054425946e-05,
    -5.036405881894902e-05,
    3.0986869577148946e-06,
    -6.638614747540505e-08,
)
ERF_END = 21.16
TILE = 1024


def step_rates():
    factor = 1.5
    return (
        factor / PIN**0.5,
        factor,
        factor / D**0.5,
        factor / D**0.5,
        factor / max(64 * D // PATCHES, 16) ** 0.5,
        factor / (2 * D) ** 0.5,
        factor / D**0.5,
        factor,
    )


def contract(left, right, left_dim, right_dim):
    return lax.dot_general(
        left, right, (((left_dim,), (right_dim,)), ((), ())), preferred_element_type=f32
    )


def layer_norm(values):
    center = values - jnp.mean(values, -1, keepdims=True)
    inverse = lax.rsqrt(jnp.mean(center * center, -1, keepdims=True) + norm_eps)
    return (center * inverse, inverse)


def norm_back(upstream, normed, inverse):
    return inverse * (
        upstream
        - jnp.mean(upstream, -1, keepdims=True)
        - normed * jnp.mean(upstream * normed, -1, keepdims=True)
    )


def column_sum(values):
    return jnp.sum(values, 0, keepdims=True)


def gelu_pair(inner):
    square = inner * inner
    bounded = jnp.minimum(square, ERF_END)
    series = jnp.full_like(inner, ERF[-1])
    for coefficient in ERF[-2::-1]:
        series = series * bounded + coefficient
    normal = 0.5 + 0.5 * jnp.tanh(inner * series)
    density = jnp.exp2(square * (-0.5 / LN2)) * 0.3989422804014327
    return (inner * normal, normal + inner * density)


def resident(shape):
    return pl.BlockSpec(shape, lambda *place: (0,) * len(shape), pipeline_mode=pl.Buffered(1))


MESH = pl.DeviceIdType.MESH


def where_am_i():
    both = lax.axis_index("fsdp")
    return (lax.axis_index("dp"), lax.axis_index("seq"), both // 2, both % 2)


def neighbour(digit, away=1):
    z, x, y, core = where_am_i()
    if digit == 0:
        return {"dp": (z + away) % 4}
    if digit == 1:
        return {"seq": 1 - x}
    return {"fsdp": (1 - y) * 2 + core if digit == 2 else y * 2 + 1 - core}


def greet():
    barrier = pltpu.get_barrier_semaphore()
    partners = [neighbour(1), neighbour(2), neighbour(3)] + [neighbour(0, d) for d in (1, 2, 3)]
    for partner in partners:
        pl.semaphore_signal(barrier, inc=1, device_id=partner, device_id_type=MESH)
    pl.semaphore_wait(barrier, len(partners))


class Summing:
    steps = ((3, 1), (1, 1), (2, 1), (0, 1), (0, 2))

    def __init__(self, running, came, sent, got):
        self.running, self.came, self.sent, self.got = running, came, sent, got
        self.copies = []

    def start(self):
        index = len(self.copies)
        digit, bit = self.steps[index]
        if digit == 0:
            z = where_am_i()[0]
            partner = {"dp": z + bit - 2 * bit * ((z // bit) % 2)}
        else:
            partner = neighbour(digit)
        copy = pltpu.make_async_remote_copy(
            src_ref=self.running.at[index],
            dst_ref=self.came.at[index],
            send_sem=self.sent.at[index],
            recv_sem=self.got.at[index],
            device_id=partner,
            device_id_type=MESH,
        )
        copy.start()
        self.copies.append(copy)

    def end(self):
        index = len(self.copies) - 1
        self.copies[index].wait()
        self.running[index + 1] = self.running[index] + self.came[index]


def summing_scratch(shape):
    return [
        pltpu.VMEM((6,) + shape, f32),
        pltpu.VMEM((5,) + shape, f32),
        pltpu.SemaphoreType.DMA((5,)),
        pltpu.SemaphoreType.DMA((5,)),
    ]


def small_sum_kernel(values, out, over_fsdp, over_seq, over_dp, sents, gots):
    axes = (("fsdp", 4, over_fsdp), ("seq", 2, over_seq), ("dp", 4, over_dp))
    partner = lambda axis, size, away: {axis: (lax.axis_index(axis) + away) % size}
    barrier = pltpu.get_barrier_semaphore()
    for axis, size, slots in axes:
        for away in range(1, size):
            pl.semaphore_signal(
                barrier, inc=1, device_id=partner(axis, size, away), device_id_type=MESH
            )
    pl.semaphore_wait(barrier, sum(size - 1 for axis, size, slots in axes))
    running = values[...]
    for stage, (axis, size, slots) in enumerate(axes):
        me = lax.axis_index(axis)
        slots[me] = running
        copies = [
            pltpu.make_async_remote_copy(
                src_ref=slots.at[me],
                dst_ref=slots.at[me],
                send_sem=sents.at[stage, away - 1],
                recv_sem=gots.at[stage, away - 1],
                device_id=partner(axis, size, away),
                device_id_type=MESH,
            )
            for away in range(1, size)
        ]
        for copy in copies:
            copy.start()
        for copy in copies:
            copy.wait()
        running = slots[0]
        for index in range(1, size):
            running = running + slots[index]
    out[...] = running


def small_sum(values):
    slots = lambda size: pltpu.VMEM((size,) + values.shape, f32)
    return pl.pallas_call(
        small_sum_kernel,
        out_shape=jax.ShapeDtypeStruct(values.shape, f32),
        in_specs=[pl.BlockSpec(memory_space=pltpu.VMEM)],
        out_specs=pl.BlockSpec(memory_space=pltpu.VMEM),
        scratch_shapes=[
            slots(4),
            slots(2),
            slots(4),
            pltpu.SemaphoreType.DMA((3, 3)),
            pltpu.SemaphoreType.DMA((3, 3)),
        ],
        compiler_params=pltpu.CompilerParams(collective_id=2, has_side_effects=True),
        name="small_sum",
    )(values)


def spread_kernel(chunks, arrays, *refs):
    sources, values, targets, out = refs[:arrays], refs[arrays], refs[arrays + 1 : -10], refs[-10]
    running, came, sent, got, own_sem, z_sent, z_got, far_sent, far_got = refs[-9:]
    z, x, y, core = where_am_i()
    running[0] = values[...]
    greet()
    total = Summing(running, came, sent, got)
    total.start()
    own = []
    for index in range(arrays):
        copy = pltpu.make_async_copy(
            sources[index], targets[index].at[z, x, y, core], own_sem.at[index]
        )
        copy.start()
        own.append(copy)
    along = {}
    for chunk, (which, start, size, order) in enumerate(chunks):
        columns = pl.ds(start, size)
        for away in (1, 2, 3):
            copy = pltpu.make_async_remote_copy(
                src_ref=sources[which].at[:, columns],
                dst_ref=targets[which].at[z, x, y, core, :, columns],
                send_sem=z_sent.at[chunk, away - 1],
                recv_sem=z_got.at[chunk, away - 1],
                device_id=neighbour(0, away),
                device_id_type=MESH,
            )
            copy.start()
            along[chunk, away] = copy
    for copy in own:
        copy.wait()
    far = {}
    every = slice(None)
    for time in range(len(chunks) + 2):
        for stage in range(3):
            chunk = time - stage
            if not 0 <= chunk < len(chunks):
                continue
            which, start, size, order = chunks[chunk]
            if stage == 0:
                for away in (1, 2, 3):
                    along[chunk, away].wait_recv()
            else:
                far[chunk, stage - 1].wait_recv()
            at = [every, x, y, core]
            for digit in order[:stage]:
                at[digit] = every
            block = targets[which].at[(*at, every, pl.ds(start, size))]
            copy = pltpu.make_async_remote_copy(
                src_ref=block,
                dst_ref=block,
                send_sem=far_sent.at[chunk, stage],
                recv_sem=far_got.at[chunk, stage],
                device_id=neighbour(order[stage]),
                device_id_type=MESH,
            )
            copy.start()
            far[chunk, stage] = copy
        if time < 5:
            total.end()
            if time < 4:
                total.start()
    out[...] = running[5]
    for chunk in range(len(chunks)):
        far[chunk, 2].wait_recv()
        for away in (1, 2, 3):
            along[chunk, away].wait_send()
        for stage in range(3):
            far[chunk, stage].wait_send()


def spread_start(shards, values):
    share = shards[0].shape[0]
    orders = ((1, 2, 3), (2, 1, 3))
    chunks = []
    for which, shard in enumerate(shards):
        size = min(512, shard.shape[1])
        for start in range(0, shard.shape[1], size):
            chunks.append((which, start, size, orders[len(chunks) % 2]))
    count = len(chunks)
    grid = (4, 2, 2, 2, share)
    anywhere = pl.BlockSpec(memory_space=pl.ANY)
    near = pl.BlockSpec(memory_space=pltpu.VMEM)
    results = pl.pallas_call(
        functools.partial(spread_kernel, chunks, len(shards)),
        out_shape=[jax.ShapeDtypeStruct(grid + (shard.shape[1],), bf16) for shard in shards]
        + [jax.ShapeDtypeStruct(values.shape, f32)],
        in_specs=[anywhere] * len(shards) + [near],
        out_specs=[anywhere] * len(shards) + [near],
        scratch_shapes=summing_scratch(values.shape)
        + [pltpu.SemaphoreType.DMA((len(shards),))]
        + [pltpu.SemaphoreType.DMA((count, 3))] * 4,
        compiler_params=pltpu.CompilerParams(collective_id=0, has_side_effects=True),
        name="spread_start",
    )(*shards, values)
    return [whole.reshape(32 * share, whole.shape[-1]) for whole in results[:-1]], results[-1]


def fold_kernel(chunks, last, values, out_last, out, running, came, sent, got,
                part, part_one, part_two, got_core, got_one, got_two, got_z, sents, gots):
    place = where_am_i()
    z, core = place[0], place[3]
    running[0] = values[...]
    greet()
    total = Summing(running, came, sent, got)
    copies = {}
    every = slice(None)

    def send(chunk, stage, source, target, partner):
        copy = pltpu.make_async_remote_copy(
            src_ref=source,
            dst_ref=target,
            send_sem=sents.at[chunk, stage],
            recv_sem=gots.at[chunk, stage],
            device_id=partner,
            device_id_type=MESH,
        )
        copy.start()
        copies[chunk, stage] = copy

    def sum_of(left, right):
        return (left.astype(f32) + right.astype(f32)).astype(bf16)

    for chunk, (start, size, order) in enumerate(chunks):
        block = last.at[:, :, :, 1 - core, :, pl.ds(start, size)]
        send(chunk, 0, block, got_core.at[chunk], neighbour(3))
    total.start()
    for time in range(len(chunks) + 3):
        for stage in range(1, 5):
            chunk = time - stage + 1
            if not 0 <= chunk < len(chunks):
                continue
            start, size, order = chunks[chunk]
            columns = pl.ds(start, size)
            near, far = order
            if stage == 1:
                copies[chunk, 0].wait_recv()
                part[chunk] = sum_of(last[:, :, :, core, :, columns], got_core[chunk])
                at = [every, every, every]
                at[near] = 1 - place[near]
                send(chunk, 1, part.at[(chunk, *at)], got_one.at[chunk], neighbour(near))
            elif stage == 2:
                copies[chunk, 1].wait_recv()
                at = [every, every, every]
                at[near] = place[near]
                part_one[chunk] = sum_of(part[(chunk, *at)], got_one[chunk])
                send(
                    chunk, 2, part_one.at[chunk, :, 1 - place[far]], got_two.at[chunk], neighbour(far)
                )
            elif stage == 3:
                copies[chunk, 2].wait_recv()
                part_two[chunk] = sum_of(part_one[chunk, :, place[far]], got_two[chunk])
                for away in (1, 2, 3):
                    source = part_two.at[chunk, (z + away) % 4]
                    send(chunk, 2 + away, source, got_z.at[chunk, away - 1], neighbour(0, away))
            else:
                whole = part_two[chunk, z].astype(f32)
                for away in (1, 2, 3):
                    copies[chunk, 2 + away].wait_recv()
                    whole = whole + got_z[chunk, away - 1].astype(f32)
                out_last[:, columns] = whole
        if time < 5:
            total.end()
            if time < 4:
                total.start()
    for step in range(len(chunks) + 3, 5):
        total.end()
        if step < 4:
            total.start()
    out[...] = running[5]
    for chunk in range(len(chunks)):
        for stage in range(6):
            copies[chunk, stage].wait_send()


def fold_end(last, values):
    rows, wide = last.shape
    share = rows // 32
    size = 128
    orders = ((1, 2), (2, 1))
    chunks = [(start, size, orders[(start // size) % 2]) for start in range(0, wide, size)]
    count = len(chunks)
    near = pl.BlockSpec(memory_space=pltpu.VMEM)
    return pl.pallas_call(
        functools.partial(fold_kernel, chunks),
        out_shape=[
            jax.ShapeDtypeStruct((share, wide), f32),
            jax.ShapeDtypeStruct(values.shape, f32),
        ],
        in_specs=[near, near],
        out_specs=[near, near],
        scratch_shapes=summing_scratch(values.shape)
        + [
            pltpu.VMEM((count, 4, 2, 2, share, size), bf16),
            pltpu.VMEM((count, 4, 2, share, size), bf16),
            pltpu.VMEM((count, 4, share, size), bf16),
            pltpu.VMEM((count, 4, 2, 2, share, size), bf16),
            pltpu.VMEM((count, 4, 2, share, size), bf16),
            pltpu.VMEM((count, 4, share, size), bf16),
            pltpu.VMEM((count, 3, share, size), bf16),
            pltpu.SemaphoreType.DMA((count, 6)),
            pltpu.SemaphoreType.DMA((count, 6)),
        ],
        compiler_params=pltpu.CompilerParams(
            collective_id=1, has_side_effects=True, vmem_limit_bytes=VMEM_BYTES
        ),
        name="fold_end",
    )(last.reshape(4, 2, 2, 2, share, wide), values)


class Ride:
    def __init__(self, arrays, lanes, columns, steps, collective):
        rows = arrays[0].shape[0]
        self.share = rows // 32
        self.arrays = [array.reshape(4, 2, 2, 2, self.share, array.shape[1]) for array in arrays]
        self.lanes, self.columns, self.steps, self.collective = lanes, columns, steps, collective
        self.size = 128 if lanes else arrays[0].shape[1] // 2
        while columns % self.size or columns // self.size + 4 > steps:
            self.size += 128
        self.chunks = columns // self.size

    def in_specs(self):
        return [pl.BlockSpec(memory_space=pl.ANY)] * len(self.arrays)

    def out_specs(self):
        return [pl.BlockSpec((self.share, self.columns), lambda *place: (0, 0))] * 2

    def out_shape(self):
        return [jax.ShapeDtypeStruct((self.share, self.columns), f32)] * 2

    def scratch(self):
        tail = (self.share, self.size)
        whole, half, quarter = (4, 2, 2) + tail, (4, 2) + tail, (4,) + tail
        every = (2, self.chunks)
        return [
            pltpu.VMEM((2, 2) + whole, bf16),
            pltpu.VMEM(every + whole, bf16),
            pltpu.VMEM(every + half, bf16),
            pltpu.VMEM(every + quarter, bf16),
            pltpu.VMEM(every + (3,) + tail, bf16),
            pltpu.VMEM((2, 2) + whole, bf16),
            pltpu.VMEM((2, 2) + half, bf16),
            pltpu.VMEM((2, 2) + quarter, bf16),
            pltpu.SemaphoreType.DMA((2, 2)),
            pltpu.SemaphoreType.DMA(every + (6,)),
            pltpu.SemaphoreType.DMA(every + (6,)),
        ]

    def step(self, time, sources, outs, scratch):
        own, got_core, got_one, got_two, got_z, part, part_one, part_two, own_sem, sents, gots = scratch
        place = where_am_i()
        z, core = place[0], place[3]
        count, size = self.chunks, self.size
        every = slice(None)

        def sum_of(left, right):
            return (left.astype(f32) + right.astype(f32)).astype(bf16)

        def block_of(lane, chunk, array, which):
            if self.lanes:
                array, base = self.lanes[lane]
                columns = pl.ds(pl.multiple_of(base + chunk * size, 128), size)
            else:
                columns = pl.ds(lane * size, size)
            return sources[array].at[:, :, :, which, :, columns]

        def copy_of(lane, chunk, stage, array=0):
            near, far = ((1, 2), (2, 1))[lane]
            slot = chunk % 2
            if stage == 0:
                source = block_of(lane, chunk, array, 1 - core)
                target, partner = got_core.at[lane, chunk], neighbour(3)
            elif stage == 1:
                at = [every, every, every]
                at[near] = 1 - place[near]
                source, target = part.at[(lane, slot, *at)], got_one.at[lane, chunk]
                partner = neighbour(near)
            elif stage == 2:
                source = part_one.at[lane, slot, :, 1 - place[far]]
                target, partner = got_two.at[lane, chunk], neighbour(far)
            else:
                away = stage - 2
                source = part_two.at[lane, slot, (z + away) % 4]
                target, partner = got_z.at[lane, chunk, away - 1], neighbour(0, away)
            return pltpu.make_async_remote_copy(
                src_ref=source,
                dst_ref=target,
                send_sem=sents.at[lane, chunk, stage],
                recv_sem=gots.at[lane, chunk, stage],
                device_id=partner,
                device_id_type=MESH,
            )

        def own_copy(lane, chunk, array=0):
            source = block_of(lane, chunk, array, core)
            slot = chunk % 2
            return pltpu.make_async_copy(source, own.at[lane, slot], own_sem.at[lane, slot])

        @pl.when(time == 0)
        def _():
            greet()

        for lane in range(2):
            near, far = ((1, 2), (2, 1))[lane]

            for array in range(1 if self.lanes else len(sources)):

                @pl.when((time < count) if self.lanes else (time == array))
                def _():
                    copy_of(lane, time, 0, array).start()
                    own_copy(lane, time, array).start()

            @pl.when((time >= 1) & (time < count + 1))
            def _():
                chunk = time - 1
                own_copy(lane, chunk).wait()
                copy_of(lane, chunk, 0).wait()

                @pl.when(chunk >= 2)
                def _():
                    copy_of(lane, chunk - 2, 1).wait_send()

                part[lane, chunk % 2] = sum_of(own[lane, chunk % 2], got_core[lane, chunk])
                copy_of(lane, chunk, 1).start()

            @pl.when((time >= 2) & (time < count + 2))
            def _():
                chunk = time - 2
                copy_of(lane, chunk, 1).wait_recv()

                @pl.when(chunk >= 2)
                def _():
                    copy_of(lane, chunk - 2, 2).wait_send()

                at = [every, every, every]
                at[near] = place[near]
                mine = part[(lane, chunk % 2, *at)]
                part_one[lane, chunk % 2] = sum_of(mine, got_one[lane, chunk])
                copy_of(lane, chunk, 2).start()

            @pl.when((time >= 3) & (time < count + 3))
            def _():
                chunk = time - 3
                copy_of(lane, chunk, 2).wait_recv()

                @pl.when(chunk >= 2)
                def _():
                    for away in (1, 2, 3):
                        copy_of(lane, chunk - 2, 2 + away).wait_send()

                mine = part_one[lane, chunk % 2, :, place[far]]
                part_two[lane, chunk % 2] = sum_of(mine, got_two[lane, chunk])
                for away in (1, 2, 3):
                    copy_of(lane, chunk, 2 + away).start()

            @pl.when((time >= 4) & (time < count + 4))
            def _():
                chunk = time - 4
                whole = part_two[lane, chunk % 2, z].astype(f32)
                for away in (1, 2, 3):
                    copy_of(lane, chunk, 2 + away).wait_recv()
                    whole = whole + got_z[lane, chunk, away - 1].astype(f32)
                outs[lane][:, pl.ds(pl.multiple_of(chunk * size, 128), size)] = whole

        @pl.when(time == self.steps - 1)
        def _():
            for lane in range(2):
                for chunk in range(max(count - 2, 0), count):
                    for stage in range(1, 6):
                        copy_of(lane, chunk, stage).wait_send()


class NoRide:
    arrays = ()
    collective = None
    in_specs = out_specs = out_shape = scratch = lambda self: []

    def step(self, *unused):
        pass


class Links:
    def __init__(self, sizes):
        self.plain = sizes != (4, 2, 4)

    def start(self, shards, values):
        if not self.plain:
            return spread_start(shards, values)
        gather = lambda shard: lax.all_gather(shard, ALL, axis=0, tiled=True)
        return [gather(shard) for shard in shards], lax.psum(values, ALL)

    def ride(self, arrays, lanes, columns, steps, collective):
        return NoRide() if self.plain else Ride(arrays, lanes, columns, steps, collective)

    def scatter(self, values, done):
        if not self.plain:
            return jnp.concatenate(done, 1)
        return lax.psum_scatter(values, ALL, scatter_dimension=0, tiled=True).astype(f32)

    def end(self, last, values):
        if not self.plain:
            return fold_end(last, values)
        total = lax.psum_scatter(last, ALL, scatter_dimension=0, tiled=True).astype(f32)
        return total, lax.psum(values, ALL)

    def total(self, values):
        return lax.psum(values, ALL) if self.plain else small_sum(values)


def entry_kernel(query_blocks, field, embed, weight, mod, stream, hidden, mixed):
    width = embed.shape[0]
    stream_zero = contract(field[...], embed[...], 1, 1)
    stream[...] = stream_zero
    normed, unused = layer_norm(stream_zero)
    low = (normed * (1.0 + mod[1:2, :]) + mod[0:1, :]).astype(bf16)
    hidden[...] = low
    for part in (1, 2):
        columns = pl.ds(part * width, width)
        mixed[:, columns] = contract(low, weight[:, columns], 1, 0).astype(bf16)

    @pl.when(pl.program_id(0) < query_blocks)
    def _():
        queries = contract(low, weight[:, 0:width], 1, 0)
        mixed[:, 0:width] = (queries * QUERY_SCALE).astype(bf16)


def entry(fields, embed, weight, mod, block, query_blocks, unit_of, place_of, rows, into):
    count, pieces = fields.shape
    width = embed.shape[0]
    given = len(into)
    placed = lambda columns: pl.BlockSpec((block, columns), lambda i: (place_of(i), 0))

    def kernel(*refs):
        entry_kernel(query_blocks, *(refs[:4] + refs[4 + given :]))

    return pl.pallas_call(
        kernel,
        grid=(count // block,),
        in_specs=[
            pl.BlockSpec((block, pieces), lambda i: (i, 0)),
            resident(embed.shape),
            resident(weight.shape),
            pl.BlockSpec((None,) + mod.shape[1:], lambda i: (unit_of(i), 0, 0)),
        ]
        + [pl.BlockSpec(memory_space=pl.ANY)] * given,
        out_specs=[placed(width), placed(width), placed(3 * width)],
        out_shape=[
            jax.ShapeDtypeStruct((rows, width), f32),
            jax.ShapeDtypeStruct((rows, width), bf16),
            jax.ShapeDtypeStruct((rows, 3 * width), bf16),
        ],
        input_output_aliases={4 + index: index for index in range(given)},
        cost_estimate=pl.CostEstimate(
            flops=8 * count * width * width, bytes_accessed=12 * count * width, transcendentals=0
        ),
        compiler_params=pltpu.CompilerParams(vmem_limit_bytes=VMEM_BYTES),
        name="entry",
    )(fields, embed, weight, mod, *into)


def crossed():
    row = lax.broadcasted_iota(jnp.int32, (2 * HD, 2 * HD), 0) < HD
    column = lax.broadcasted_iota(jnp.int32, (2 * HD, 2 * HD), 1) < HD
    return jnp.where(row != column, 1.0, 0.0).astype(bf16)


def attend_kernel(sub, query, key, value, out, kept, inverse, value_t, key_one, stats):
    block, keys = query.shape[0], key.shape[0]
    zero, one = jnp.zeros((), bf16), jnp.ones((), bf16)

    @pl.when(pl.program_id(1) == 0)
    def _():
        turned = jnp.transpose(value[...])
        first_rows = lax.broadcasted_iota(jnp.int32, (2 * HD, keys), 0) < HD
        value_t[0] = jnp.where(first_rows, turned, one)
        value_t[1] = jnp.where(first_rows, one, turned)
        first_lanes = lax.broadcasted_iota(jnp.int32, (keys, 2 * HD), 1) < HD
        both = key[...]
        key_one[0] = jnp.where(first_lanes, both, one)
        key_one[1] = jnp.where(first_lanes, one, both)
        wide = both.astype(f32)
        mean = jnp.mean(wide, 0, keepdims=True)
        spread = ((wide - mean) * (wide - mean)).astype(bf16)
        stats[0:1] = mean
        far = jnp.max(contract(spread, crossed(), 1, 0), 0, keepdims=True)
        stats[1:2] = 0.5 * jnp.sqrt(far)

    lanes = lax.broadcasted_iota(jnp.int32, (sub, 2 * HD), 1)
    wide = query[...].astype(f32)
    length = jnp.sqrt(contract((wide * wide).astype(bf16), crossed(), 1, 0))
    reach = length * stats[1:2]
    shifts = (-contract((wide * stats[0:1]).astype(bf16), crossed(), 1, 0) - reach).astype(bf16)
    near = jnp.max(reach) <= 60.0
    upper = lax.broadcasted_iota(jnp.int32, (2 * HD, sub), 0) < HD

    def run(exact):
        for part in range(block // sub):
            rows = pl.ds(part * sub, sub)
            results = []
            for head in range(2):
                mine = (lanes < HD) if head == 0 else (lanes >= HD)
                if exact:
                    moved = jnp.where(mine, query[rows, :], zero)
                    scores = contract(key_one[head], moved, 1, 1)
                    scores = scores - jnp.max(scores, 0, keepdims=True)
                else:
                    free = HD if head == 0 else 0
                    rest = jnp.where(lanes == free, shifts[part * sub : part * sub + sub], zero)
                    moved = jnp.where(mine, query[rows, :], rest)
                    scores = contract(key_one[head], moved, 1, 1)
                weights = jnp.exp2(scores).astype(bf16)
                kept[head, :, rows] = weights
                results.append(contract(value_t[head], weights, 1, 0))
            total = jnp.where(
                upper, pltpu.roll(results[0], HD, 0), pltpu.roll(results[1], HD, 0)
            )
            above = 1.0 / total
            mean = jnp.where(upper, results[0], results[1]) * above
            out[rows, :] = jnp.transpose(mean).astype(bf16)
            inverse[0:1, rows] = above[0:1]
            inverse[1:2, rows] = above[HD : HD + 1]

    @pl.when(near)
    def _():
        run(False)

    @pl.when(jnp.logical_not(near))
    def _():
        run(True)


def attend(queries, memory, places, block, sub, count, keys, width, into, rows):
    pairs = width // (2 * HD)
    query_at, key_at, key_column, value_column = places
    given = len(into)

    def kernel(*refs):
        attend_kernel(sub, *(refs[:3] + refs[3 + given :]))

    return pl.pallas_call(
        kernel,
        grid=(pairs, count // block),
        in_specs=[
            pl.BlockSpec((block, 2 * HD), lambda h, i: (query_at // block + i, h)),
            pl.BlockSpec((keys, 2 * HD), lambda h, i: (key_at // keys, key_column * pairs + h)),
            pl.BlockSpec((keys, 2 * HD), lambda h, i: (key_at // keys, value_column * pairs + h)),
        ]
        + [pl.BlockSpec(memory_space=pl.ANY)] * given,
        out_specs=[
            pl.BlockSpec((block, 2 * HD), lambda h, i: (query_at // block + i, h)),
            pl.BlockSpec((None, None, 2, keys, block), lambda h, i: (h, i, 0, 0, 0)),
            pl.BlockSpec((None, 2, block), lambda h, i: (h, 0, i)),
        ],
        out_shape=[
            jax.ShapeDtypeStruct((rows, width), bf16),
            jax.ShapeDtypeStruct((pairs, count // block, 2, keys, block), bf16),
            jax.ShapeDtypeStruct((pairs, 2, count), f32),
        ],
        scratch_shapes=[
            pltpu.VMEM((2, 2 * HD, keys), bf16),
            pltpu.VMEM((2, keys, 2 * HD), bf16),
            pltpu.VMEM((8, 2 * HD), f32),
        ],
        cost_estimate=pl.CostEstimate(
            flops=20 * count * keys * width, bytes_accessed=2 * count * keys, transcendentals=0
        ),
        compiler_params=pltpu.CompilerParams(vmem_limit_bytes=VMEM_BYTES),
        input_output_aliases={3: 0} if given else {},
        name="attend",
    )(queries, memory, memory, *into)


def attend_back_kernel(
    sub, query, key, value, grad, out, kept, inverse,
    grad_query, grad_key, grad_value, key_t, value_one, key_sum, value_sum,
):
    block, keys = query.shape[0], key.shape[0]
    step, steps = pl.program_id(1), pl.num_programs(1)
    zero = jnp.zeros((), bf16)

    @pl.when(step == 0)
    def _():
        first_rows = lax.broadcasted_iota(jnp.int32, (2 * HD, keys), 0) < HD
        turned = jnp.transpose(key[...])
        key_t[0] = jnp.where(first_rows, turned, zero)
        key_t[1] = jnp.where(first_rows, zero, turned)
        first_lanes = lax.broadcasted_iota(jnp.int32, (keys, 2 * HD), 1) < HD
        minus = jnp.full((), -1.0, bf16)
        value_one[0] = jnp.where(first_lanes, value[...], minus)
        value_one[1] = jnp.where(first_lanes, minus, value[...])
        key_sum[...] = jnp.zeros_like(key_sum)
        value_sum[...] = jnp.zeros_like(value_sum)

    lanes = lax.broadcasted_iota(jnp.int32, (sub, 2 * HD), 1)
    places = lax.broadcasted_iota(jnp.int32, (2 * HD, sub), 0)
    upper = places < HD
    for part in range(block // sub):
        rows = pl.ds(part * sub, sub)
        above = jnp.where(upper, inverse[0:1, rows], inverse[1:2, rows])
        scaled = (jnp.transpose(grad[rows, :].astype(f32)) * above).astype(bf16)
        product = scaled.astype(f32) * jnp.transpose(out[rows, :].astype(f32))
        natural = jnp.transpose(scaled)
        queries = query[rows, :]
        turned = None
        for head in range(2):
            delta = jnp.sum(product[HD * head : HD * head + HD], 0, keepdims=True)
            high = delta.astype(bf16)
            rest = (delta - high.astype(f32)).astype(bf16)
            free = HD if head == 0 else 0
            mine = upper if head == 0 else jnp.logical_not(upper)
            extra = jnp.where(places == free, high, jnp.where(places == free + 1, rest, zero))
            grad_probs = contract(value_one[head], jnp.where(mine, scaled, extra), 1, 0)
            weights = kept[head, :, rows]
            grad_scores = grad_probs.astype(bf16) * weights
            own = (lanes < HD) if head == 0 else (lanes >= HD)
            value_sum[...] += contract(weights, jnp.where(own, natural, zero), 1, 0)
            key_sum[...] += contract(grad_scores, jnp.where(own, queries, zero), 1, 0)
            term = contract(key_t[head], grad_scores, 1, 0)
            turned = term if turned is None else turned + term
        grad_query[rows, :] = (jnp.transpose(turned) * 0.125).astype(bf16)

    @pl.when(step == steps - 1)
    def _():
        grad_key[...] = (key_sum[...] * LN2).astype(bf16)
        grad_value[...] = value_sum[...].astype(bf16)


def attend_back(queries, memory, grads, out, kept, inverse, places, block, sub, into, shapes, ride):
    query_at, key_at, key_column, value_column, grad_query_at, grad_key_at = places
    count, keys = kept.shape[1] * kept.shape[4], kept.shape[3]
    pairs = out.shape[1] // (2 * HD)
    two = 2 * HD
    steps = count // block
    given, riding = len(into), len(ride.arrays)

    def kernel(*refs):
        ins, refs = refs[:7], refs[7 + given :]
        sources, refs = refs[:riding], refs[riding:]
        outs, refs = refs[:3], refs[3:]
        sums, refs = refs[: 2 * bool(riding)], refs[2 * bool(riding) :]
        ride.step(pl.program_id(0) * steps + pl.program_id(1), sources, sums, refs[4:])
        attend_back_kernel(sub, *ins, *outs, *refs[:4])

    work = pairs * count * keys * two
    results = pl.pallas_call(
        kernel,
        grid=(pairs, steps),
        in_specs=[
            pl.BlockSpec((block, two), lambda h, i: (query_at // block + i, h)),
            pl.BlockSpec((keys, two), lambda h, i: (key_at // keys, key_column * pairs + h)),
            pl.BlockSpec((keys, two), lambda h, i: (key_at // keys, value_column * pairs + h)),
            pl.BlockSpec((block, two), lambda h, i: (query_at // block + i, h)),
            pl.BlockSpec((block, two), lambda h, i: (query_at // block + i, h)),
            pl.BlockSpec((None, None, 2, keys, block), lambda h, i: (h, i, 0, 0, 0)),
            pl.BlockSpec((None, 2, block), lambda h, i: (h, 0, i)),
        ]
        + [pl.BlockSpec(memory_space=pl.ANY)] * given
        + ride.in_specs(),
        out_specs=[
            pl.BlockSpec((block, two), lambda h, i: (grad_query_at // block + i, h)),
            pl.BlockSpec((keys, two), lambda h, i: (grad_key_at // keys, h)),
            pl.BlockSpec((keys, two), lambda h, i: (grad_key_at // keys, h)),
        ]
        + ride.out_specs(),
        out_shape=[jax.ShapeDtypeStruct(shape, bf16) for shape in shapes] + ride.out_shape(),
        scratch_shapes=[
            pltpu.VMEM((2, two, keys), bf16),
            pltpu.VMEM((2, keys, two), bf16),
            pltpu.VMEM((keys, two), f32),
            pltpu.VMEM((keys, two), f32),
        ]
        + ride.scratch(),
        input_output_aliases={7 + index: index for index in range(given)},
        cost_estimate=pl.CostEstimate(flops=32 * work, bytes_accessed=4 * work // HD, transcendentals=0),
        compiler_params=pltpu.CompilerParams(
            vmem_limit_bytes=VMEM_BYTES,
            collective_id=ride.collective,
            has_side_effects=riding > 0,
        ),
        name="attend_back",
    )(queries, memory, memory, grads, out, kept, inverse, *into, *ride.arrays)
    return results[:3], results[3:]


def middle_kernel(
    parts, attended, stream, target, weight_rows, mod, combine, first, second, read,
    hidden, active, grad_two, grad_inner, final, grad_read, grad_one, grad_attended, grad_stream,
    sums, losses, slopes,
):
    block = attended.shape[0]
    width, spread = first.shape
    size_tile = min(TILE, spread)
    tiles = [pl.ds(start, size_tile) for start in range(0, spread, size_tile)]
    gate_a, shift_b, scale_b = mod[2:3, :], mod[3:4, :], mod[4:5, :]
    gate_b, gain = mod[5:6, :], mod[6:7, :]

    def run(rows, found):
        branch_a = contract(attended[rows, :], combine[...], 1, 0)
        yield
        stream_one = stream[rows, :] + gate_a * branch_a
        norm_b, inverse_b = layer_norm(stream_one)
        low = (norm_b * (1.0 + scale_b) + shift_b).astype(bf16)
        hidden[rows, :] = low
        yield
        branch_b = None
        ahead = contract(low, first[:, tiles[0]], 1, 0)
        for index, tile in enumerate(tiles):
            inner = ahead
            if index + 1 < len(tiles):
                ahead = contract(low, first[:, tiles[index + 1]], 1, 0)
            yield
            value, slope = gelu_pair(inner)
            value = value.astype(bf16)
            active[rows, tile] = value
            slopes[rows, tile] = slope.astype(bf16)
            term = contract(value, second[:, tile], 1, 1)
            branch_b = term if branch_b is None else branch_b + term
            yield
        norm_c, inverse_c = layer_norm(stream_one + gate_b * branch_b)
        last = (norm_c * gain).astype(bf16)
        final[rows, :] = last
        yield
        diff = contract(last, read[...], 1, 0) - target[rows, :].astype(f32)
        found[0] = column_sum(weight_rows[rows, 0:1] * diff * diff)
        grad_low = (weight_rows[rows, 1:2] * diff).astype(bf16)
        grad_read[rows, :] = grad_low
        grad_final = contract(grad_low, read[...], 1, 1)
        yield
        found[6] = column_sum(grad_final * norm_c)
        grad = norm_back(grad_final * gain, norm_c, inverse_c)
        found[5] = column_sum(grad * branch_b)
        back = (grad * gate_b).astype(bf16)
        grad_two[rows, :] = back
        yield
        grad_hidden = None
        ahead = contract(back, second[:, tiles[0]], 1, 0)
        for index, tile in enumerate(tiles):
            inner = ahead
            if index + 1 < len(tiles):
                ahead = contract(back, second[:, tiles[index + 1]], 1, 0)
            yield
            inner = (inner * slopes[rows, tile].astype(f32)).astype(bf16)
            grad_inner[rows, tile] = inner
            term = contract(inner, first[:, tile], 1, 1)
            grad_hidden = term if grad_hidden is None else grad_hidden + term
            yield
        found[3] = column_sum(grad_hidden)
        found[4] = column_sum(grad_hidden * norm_b)
        grad = grad + norm_back(grad_hidden * (1.0 + scale_b), norm_b, inverse_b)
        grad_stream[rows, :] = grad
        found[2] = column_sum(grad * branch_a)
        back = (grad * gate_a).astype(bf16)
        grad_one[rows, :] = back
        yield
        grad_attended[rows, :] = contract(back, combine[...], 1, 1).astype(bf16)

    size = block // parts
    found = [{} for part in range(parts)]
    runs = [run(pl.ds(part * size, size), found[part]) for part in range(parts)]
    while runs:
        runs = [one for one in runs if next(one, runs) is not runs]
    losses[...] = jnp.broadcast_to(sum(one[0] for one in found), losses.shape)
    for row in (2, 3, 4, 5, 6):
        sums[row : row + 1, :] = sum(one[row] for one in found)
    sums[0:2, :] = jnp.zeros((2, width), f32)
    sums[7:8, :] = jnp.zeros((1, width), f32)


def middle(attended, stream, target, weight_rows, mod, combine, first, second, read, block, unit_of):
    rows, width = attended.shape
    spread, pieces = first.shape[1], read.shape[1]
    blocks = rows // block
    by_row = lambda columns: pl.BlockSpec((block, columns), lambda i: (i, 0))
    shape = lambda columns, kind: jax.ShapeDtypeStruct((rows, columns), kind)
    outs = (
        (width, bf16), (spread, bf16), (width, bf16), (spread, bf16), (width, bf16), (pieces, bf16),
        (width, bf16), (width, bf16), (width, f32),
    )
    return pl.pallas_call(
        functools.partial(middle_kernel, 1),
        grid=(blocks,),
        in_specs=[
            by_row(width),
            by_row(width),
            by_row(pieces),
            by_row(2),
            pl.BlockSpec((None,) + mod.shape[1:], lambda i: (unit_of(i), 0, 0)),
            resident(combine.shape),
            resident(first.shape),
            resident(second.shape),
            resident(read.shape),
        ],
        out_specs=[by_row(columns) for columns, kind in outs]
        + [
            pl.BlockSpec((None, 8, width), lambda i: (i, 0, 0)),
            pl.BlockSpec((None, 8, pieces), lambda i: (i, 0, 0)),
        ],
        out_shape=[shape(columns, kind) for columns, kind in outs]
        + [
            jax.ShapeDtypeStruct((blocks, 8, width), f32),
            jax.ShapeDtypeStruct((blocks, 8, pieces), f32),
        ],
        scratch_shapes=[pltpu.VMEM((block, spread), bf16)],
        cost_estimate=pl.CostEstimate(
            flops=60 * rows * width * width, bytes_accessed=40 * rows * width, transcendentals=0
        ),
        compiler_params=pltpu.CompilerParams(vmem_limit_bytes=VMEM_BYTES),
        name="middle",
    )(attended, stream, target, weight_rows, mod, combine, first, second, read)


def leave_kernel(query_blocks, grad_query, grad_key, grad_value, stream, grad_stream, weight, mod, out, sums, held):
    width = stream.shape[1]
    asks = pl.program_id(0) < query_blocks
    columns = lambda kind: pl.ds(kind * width, width)
    held[...] = contract(grad_key[...], weight[:, columns(1)], 1, 1)
    held[...] += contract(grad_value[...], weight[:, columns(2)], 1, 1)

    @pl.when(asks)
    def _():
        held[...] += contract(grad_query[...], weight[:, columns(0)], 1, 1)

    normed, inverse = layer_norm(stream[...])
    grad_hidden = held[...]
    sums[0:1, :] = column_sum(grad_hidden)
    sums[1:2, :] = column_sum(grad_hidden * normed)
    sums[2:8, :] = jnp.zeros((6, width), f32)
    grad = norm_back(grad_hidden * (1.0 + mod[1:2, :]), normed, inverse)
    grad = grad + jnp.where(asks, grad_stream[...], 0.0)
    out[...] = grad.astype(bf16)


def leave(grads, stream, grad_stream, weight, mod, block, unit_of, ride):
    rows, width = stream.shape
    asking = grads[0].shape[0] // block
    blocks, riding = rows // block, len(ride.arrays)
    by_row = pl.BlockSpec((block, width), lambda i: (i, 0))
    asked = pl.BlockSpec((block, width), lambda i: (jnp.minimum(i, asking - 1), 0))

    def kernel(*refs):
        ins, refs = refs[:7], refs[7:]
        sources, refs = refs[:riding], refs[riding:]
        outs, refs = refs[:2], refs[2:]
        shards, refs = refs[: 2 * bool(riding)], refs[2 * bool(riding) :]
        ride.step(pl.program_id(0), sources, shards, refs[1:])
        leave_kernel(asking, *ins, *outs, refs[0])

    results = pl.pallas_call(
        kernel,
        grid=(blocks,),
        in_specs=[
            asked,
            by_row,
            by_row,
            by_row,
            asked,
            resident(weight.shape),
            pl.BlockSpec((None,) + mod.shape[1:], lambda i: (unit_of(i), 0, 0)),
        ]
        + ride.in_specs(),
        out_specs=[by_row, pl.BlockSpec((None, 8, width), lambda i: (i, 0, 0))] + ride.out_specs(),
        out_shape=[
            jax.ShapeDtypeStruct((rows, width), bf16),
            jax.ShapeDtypeStruct((blocks, 8, width), f32),
        ]
        + ride.out_shape(),
        scratch_shapes=[pltpu.VMEM((block, width), f32)] + ride.scratch(),
        cost_estimate=pl.CostEstimate(
            flops=7 * rows * width * width, bytes_accessed=16 * rows * width, transcendentals=0
        ),
        compiler_params=pltpu.CompilerParams(
            vmem_limit_bytes=VMEM_BYTES,
            collective_id=ride.collective,
            has_side_effects=riding > 0,
        ),
        name="leave",
    )(*grads, stream, grad_stream, weight, mod, *ride.arrays)
    return results[:2], results[2:]


def adam(master, first, second, grad, factor, step_rate):
    grad = grad * factor
    first_new = beta_one * first + (1.0 - beta_one) * grad
    second_new = beta_two * second + (1.0 - beta_two) * grad * grad
    corrected = (
        first_new
        / (1.0 - beta_one**STEP)
        / (jnp.sqrt(second_new / (1.0 - beta_two**STEP)) + epsilon)
    )
    return (master - step_rate * (corrected + decay * master), first_new, second_new)


def largest(limit, *sizes):
    block = limit
    while any(size % block for size in sizes):
        block //= 2
    return block


def body(sizes, *args):
    ways = sizes[1]
    links = Links(sizes)
    fields, targets, interval, storm_index, valid_count, latitude, storm_scale = args[:7]
    masters, firsts, seconds = args[7:15], args[15:23], args[23:31]
    embedding, intervals, modulator, projector, combiner, feedforward, readout, vectors = masters
    micros, samples_dev, part, pieces = fields.shape
    patches = latitude.shape[0]
    units = micros * samples_dev
    share, width = projector.shape[0], projector.shape[1] // 3
    place = lax.axis_index("seq")
    device = lax.axis_index(ALL)
    sample_start = lax.axis_index(("dp", "fsdp")) * samples_dev
    ring = [(index, 1 - index) for index in range(2)]
    alone = units // 2 if ways == 2 else 0
    shared = units - ways * alone
    have = alone + shared

    def local(values):
        cut = lax.dynamic_slice_in_dim(values, sample_start, samples_dev, 1)
        cut = cut.reshape((units,) + values.shape[2:])
        mine = [lax.dynamic_slice_in_dim(cut, place * alone, alone, 0)] if alone else []
        return jnp.concatenate(mine + [cut[ways * alone :]], 0)

    kinds = local(interval)

    def widen(values):
        flat = values.reshape(units, part, pieces)
        return jnp.pad(flat, ((0, 0), (0, 0), (0, WIDE - pieces)))

    def flatten(parts):
        return jnp.concatenate([piece.reshape(-1, WIDE) for piece in parts], 0)

    def pick(values, start):
        return lax.dynamic_slice_in_dim(values, start, alone, 0)

    own = widen(fields)
    if alone:
        sent = jnp.concatenate([pick(own, (1 - place) * alone), own[2 * alone :]], 0)
        came = lax.ppermute(sent, "seq", ring)
        own = jnp.concatenate([pick(own, place * alone), own[2 * alone :]], 0)
        others = flatten([came])
        all_rows = [own[:alone], came[:alone]]
        all_rows = flatten([jnp.concatenate(all_rows, 1), own[alone:], came[alone:]])
        own = flatten([own])
    else:
        if ways > 1:
            everyone = lax.all_gather(own, "seq", axis=1, tiled=True)
            own = flatten([own, jnp.roll(everyone, -place * part, 1)[:, part:]])
        own = all_rows = own.reshape(-1, WIDE)

    def spread_goals(goal):
        if not alone:
            return flatten([goal])
        came = lax.ppermute(pick(goal, (1 - place) * alone), "seq", ring)
        whole = jnp.concatenate([pick(goal, place * alone), came], 1)
        return flatten([whole, goal[2 * alone :]])

    def weigh(latitude):
        everywhere = jnp.arange(patches, dtype=jnp.int32)
        mask = (everywhere[None, None, :] >= patches - valid_count[:, :, None]).astype(f32)
        levels = jnp.arange(storm_scale.shape[0], dtype=jnp.int32)
        storms = jnp.sum(jnp.where(storm_index[:, :, None] == levels, storm_scale, 0.0), -1)
        row_weights = latitude[None, None, :] * storms[:, :, None] * mask
        total = pieces * jnp.sum(row_weights)
        by_unit = jnp.roll(local(row_weights), -place * part, 1)
        flat = jnp.concatenate([by_unit[:alone].reshape(-1), by_unit[alone:, :part].reshape(-1)])
        return total, jnp.stack([flat, flat * (2.0 / total)], 1)

    asking = (alone * ways + shared) * part

    def unit_of(block):
        whole_blocks = alone * patches // block
        own_blocks = shared * part // block
        other = max((patches - part) // block, 1)

        def at(i):
            late = alone + (i - whole_blocks) // (part // block)
            later = alone + (i - whole_blocks - own_blocks) // other
            late = jnp.where(i < whole_blocks + own_blocks, late, later)
            return jnp.where(i < whole_blocks, i // (patches // block), late)

        return at

    low = [master.astype(bf16) for master in masters]
    step_vec = low[1].astype(f32)
    active = jax.nn.silu(step_vec)
    active_low = active.astype(bf16)
    table = contract(active_low, low[2], 1, 0)
    spread_vectors = lax.dynamic_update_slice(
        jnp.zeros((7, width), f32), low[7].astype(f32), (0, device * share)
    )
    to_wide = lambda values: jnp.pad(values, ((0, 0), (0, WIDE - pieces)))
    (embed, project, read), carried = links.start(
        (to_wide(low[0].T), low[3], to_wide(low[6])),
        jnp.concatenate([table.reshape(3 * 6 * width // 128, 128), spread_vectors.reshape(-1, 128)]),
    )
    nothing = carried[0, 0] * 0.0
    carried = carried.reshape(-1)
    table = carried[: table.size].reshape(DTK, 6, width)
    all_vectors = carried[table.size :].reshape(7, width)
    table = table + all_vectors[None, :6]
    chosen = sum(jnp.where(kinds[:, None, None] == kind, table[kind], 0.0) for kind in range(DTK))
    gain = jnp.broadcast_to(all_vectors[6], (have, 1, width))
    mod = jnp.concatenate([chosen, gain, jnp.zeros((have, 1, width), f32)], 1)

    gather = lambda values: lax.all_gather(values, ALL, axis=0, tiled=True)
    late = (combiner, feedforward[0], feedforward[1])
    combine, first, second = [gather((shard + nothing).astype(bf16)) for shard in late]

    block = largest(512, part)
    rows_all = have * patches
    if alone:
        short, long = part // block, patches // block

        def placer(first_of_shared, shift):
            def at(i):
                unit = i // short
                late = first_of_shared // block + (unit - alone) * short
                return jnp.where(unit < alone, unit * long + shift, late) + i % short

            return at

        by_unit = lambda i: i // short
        stream, hidden_a, mixed = entry(
            own, embed, project, mod, block, have * short, by_unit, placer(alone * patches, 0), rows_all, ()
        )
        stream, hidden_a, mixed = entry(
            others, embed, project, mod, block, alone * short, by_unit, placer(asking, short), rows_all,
            (stream, hidden_a, mixed),
        )
    else:
        stream, hidden_a, mixed = entry(
            own, embed, project, mod, block, asking // block, unit_of(block), lambda i: i, rows_all, ()
        )
    mixed, targets, latitude = lax.optimization_barrier((mixed, targets, latitude))
    goal_rows = spread_goals(widen(targets))
    total_weight, weight_rows = weigh(latitude)

    calls = []
    for unit in range(have):
        if unit < alone:
            start = unit * patches
            calls.append((patches, mixed, (start, start, 1, 2)))
        else:
            start = alone * patches + (unit - alone) * part
            behind = asking + (unit - alone) * (patches - part)
            if shared == 1 and start % patches == 0:
                calls.append((part, mixed, (start, start, 1, 2)))
            else:
                joined = jnp.concatenate(
                    [
                        mixed[start : start + part, width:],
                        mixed[behind : behind + patches - part, width:],
                    ],
                    0,
                )
                calls.append((part, joined, (start, 0, 0, 1)))
    attended_rows, saved = (), []
    for count, memory, where in calls:
        block = largest(1024, count, where[0] if where[0] else count)
        attended_rows, kept, inverse = attend(
            mixed, memory, where, block, block, count, patches, width, attended_rows, asking
        )
        attended_rows = (attended_rows,)
        saved.append((kept, inverse))
    attended_rows = attended_rows[0]

    block = largest(256, part)
    (
        hidden_b, activated, grad_two, grad_inner, final, grad_read, grad_one, grad_attended,
        grad_stream, sums, losses,
    ) = middle(
        attended_rows, stream, goal_rows, weight_rows, mod, combine, first, second, read, block,
        unit_of(block),
    )
    units_mid = [unit_of(block)(jnp.int32(i)) for i in range(sums.shape[0])]
    loss_local = jnp.sum(losses[:, 0, :])

    summed = lambda left, right: contract(left, right, 0, 0).astype(bf16)
    grad_first, grad_second = summed(hidden_b, grad_inner), summed(grad_two, activated)
    grad_combine, grad_readout = summed(attended_rows, grad_one), summed(final, grad_read)
    rest = jnp.concatenate([grad_combine, grad_readout, jnp.zeros((width, WIDE // 3), bf16)], 1)
    rides = [((grad_first, grad_second), ((0, 0), (1, 0)), grad_first.shape[1])]
    rides += [((rest,), ((0, 0), (0, rest.shape[1] // 2)), rest.shape[1] // 2)]
    shapes = ((asking, width), (have * patches, width), (have * patches, width))
    into, done = (), []
    for unit, ((count, memory, where), (kept, inverse)) in enumerate(zip(calls, saved)):
        block = kept.shape[4]
        ride = NoRide()
        if unit < len(rides):
            steps = width // (2 * HD) * (count // block)
            ride = links.ride(*rides[unit], steps, 3 + unit)
        into, ridden = attend_back(
            mixed, memory, grad_attended, attended_rows, kept, inverse, where + (where[0], unit * patches),
            block, min(block, 256), into, shapes, ride,
        )
        done.append(ridden)
    shard_first = links.scatter(grad_first, done[0][:1])
    shard_second = links.scatter(grad_second, done[0][1:])
    shard_rest = links.scatter(rest, done[1])
    shard_combine, shard_read = shard_rest[:, :width], shard_rest[:, width : width + WIDE]
    if not (alone and shared <= 1):
        own_part = lambda values, unit, low_row, high_row: values[
            unit * patches + low_row : unit * patches + high_row
        ]
        into = (into[0],) + tuple(
            jnp.concatenate(
                [values[: alone * patches]]
                + [own_part(values, unit, 0, part) for unit in range(alone, have)]
                + [own_part(values, unit, part, patches) for unit in range(alone, have)],
                0,
            )
            for values in into[1:]
        )
    grad_project = [summed(hidden_a[:asking], into[0])] + [summed(hidden_a, part) for part in into[1:]]
    block = largest(512, part)
    ride = links.ride(grad_project, None, 3 * width // 2, stream.shape[0] // block, 5)
    (grad_zero, sums_a), ridden = leave(
        into, stream, grad_stream, project, mod, block, unit_of(block), ride
    )
    if links.plain:
        shard_project = links.scatter(jnp.concatenate(grad_project, 1), ridden)
    else:
        by_lane = jnp.stack([lane.reshape(share, 3, width // 2) for lane in ridden], 2)
        shard_project = by_lane.reshape(share, 3 * width)
    units_out = [unit_of(block)(jnp.int32(i)) for i in range(sums_a.shape[0])]
    grad_embed = summed(grad_zero, all_rows)

    by_block = jnp.concatenate([sums, sums_a], 0)
    kind_block = kinds[jnp.stack(units_mid + units_out)]
    grad_table = jnp.stack(
        [
            jnp.sum(jnp.where((kind_block == kind)[:, None, None], by_block, 0.0), 0)
            for kind in range(DTK)
        ]
    )
    loss_row = jnp.full((1, 128), loss_local)
    small = jnp.concatenate([grad_table[:, :7].reshape(-1, 128), loss_row])
    shard_embed, carried = links.end(grad_embed, small)
    loss_total = carried[-1, 0]
    grad_table = carried[:-1].reshape(DTK, 7, width)
    grad_mod = grad_table[:, :6].reshape(DTK, 6 * width)
    shard_vectors = lax.dynamic_slice_in_dim(jnp.sum(grad_table, 0), device * share, share, 1)
    active_wide = active_low.astype(f32)
    shard_modulator = sum(
        active_wide[kind][:, None] * grad_mod[kind][None, :] for kind in range(DTK)
    )
    grad_active = jnp.stack(
        [jnp.sum(low[2].astype(f32) * grad_mod[kind][None, :], 1) for kind in range(DTK)]
    )
    unused, silu_back = jax.vjp(jax.nn.silu, step_vec)
    shard_intervals = silu_back(grad_active)[0]

    shards = (
        shard_embed[:, :pieces].T,
        shard_intervals,
        shard_modulator,
        shard_project,
        shard_combine,
        jnp.stack([shard_first, shard_second]),
        shard_read[:, :pieces],
        shard_vectors,
    )
    squares = sum(jnp.sum(grad * grad) for grad in shards)
    squares = links.total(jnp.full((8, 128), squares))[0, 0]
    norm = jnp.sqrt(squares)
    factor = clip_norm / jnp.maximum(norm, clip_norm)
    results = [
        adam(master, first_moment, second_moment, grad, factor, rate)
        for master, first_moment, second_moment, grad, rate in zip(
            masters, firsts, seconds, shards, step_rates()
        )
    ]
    return tuple(result[index] for index in range(3) for result in results) + (
        loss_total,
        total_weight,
        norm,
    )


def solution(mesh):
    data = P(None, ("dp", "fsdp"), "seq", None)
    columns, rows = P(None, ALL), P(ALL, None)
    weights = (columns, columns, rows, rows, rows, P(None, ALL, None), rows, columns)
    return jax.shard_map(
        functools.partial(body, tuple(mesh.shape[axis] for axis in ALL)),
        mesh=mesh,
        in_specs=(data, data) + (P(),) * 5 + weights * 3,
        out_specs=weights * 3 + (P(),) * 3,
        check_vma=False,
    )
```

```python
import functools

import jax
import jax.numpy as jnp
from jax import lax
from jax.experimental import pallas as pl
from jax.experimental.pallas import tpu as pltpu
from jax.sharding import PartitionSpec as P

D = 1024
HD = 64
PIN = 276
WIDE = 384
DTK = 3
STEP = 10
PATCHES = 2048
ALL = ("dp", "seq", "fsdp")

beta_one = 0.9
beta_two = 0.999
decay = 0.01
epsilon = 1e-08
clip_norm = 0.005
norm_eps = 1e-06
bf16 = jnp.bfloat16
f32 = jnp.float32
LN2 = 0.6931471805599453
QUERY_SCALE = 0.125 / LN2
VMEM_BYTES = 60 * 2**20
ERF = (
    0.7978822138768258,
    0.03634467259297056,
    -4.4877727054425946e-05,
    -5.036405881894902e-05,
    3.0986869577148946e-06,
    -6.638614747540505e-08,
)
ERF_END = 21.16
CHUNK = 512
TILE = 1024


def step_rates():
    factor = 1.5
    return (
        factor / PIN**0.5,
        factor,
        factor / D**0.5,
        factor / D**0.5,
        factor / max(64 * D // PATCHES, 16) ** 0.5,
        factor / (2 * D) ** 0.5,
        factor / D**0.5,
        factor,
    )


def contract(left, right, left_dim, right_dim):
    return lax.dot_general(
        left, right, (((left_dim,), (right_dim,)), ((), ())), preferred_element_type=f32
    )


def layer_norm(values):
    center = values - jnp.mean(values, -1, keepdims=True)
    inverse = lax.rsqrt(jnp.mean(center * center, -1, keepdims=True) + norm_eps)
    return (center * inverse, inverse)


def norm_back(upstream, normed, inverse):
    return inverse * (
        upstream
        - jnp.mean(upstream, -1, keepdims=True)
        - normed * jnp.mean(upstream * normed, -1, keepdims=True)
    )


def column_sum(values):
    return jnp.sum(values, 0, keepdims=True)


def gelu_pair(inner):
    square = inner * inner
    bounded = jnp.minimum(square, ERF_END)
    series = jnp.full_like(inner, ERF[-1])
    for coefficient in ERF[-2::-1]:
        series = series * bounded + coefficient
    normal = 0.5 + 0.5 * jnp.tanh(inner * series)
    density = jnp.exp2(square * (-0.5 / LN2)) * 0.3989422804014327
    return (inner * normal, normal + inner * density)


def halves_of(rows):
    size = rows // 2 if rows >= 512 else rows
    return [pl.ds(start, size) for start in range(0, rows, size)]


def resident(shape):
    return pl.BlockSpec(shape, lambda *place: (0,) * len(shape), pipeline_mode=pl.Buffered(1))


MESH = pl.DeviceIdType.MESH


def where_am_i():
    both = lax.axis_index("fsdp")
    return (lax.axis_index("dp"), lax.axis_index("seq"), both // 2, both % 2)


def neighbour(digit, away=1):
    z, x, y, core = where_am_i()
    if digit == 0:
        return {"dp": (z + away) % 4}
    if digit == 1:
        return {"seq": 1 - x}
    return {"fsdp": (1 - y) * 2 + core if digit == 2 else y * 2 + 1 - core}


def greet():
    barrier = pltpu.get_barrier_semaphore()
    partners = [neighbour(1), neighbour(2), neighbour(3)] + [neighbour(0, d) for d in (1, 2, 3)]
    for partner in partners:
        pl.semaphore_signal(barrier, inc=1, device_id=partner, device_id_type=MESH)
    pl.semaphore_wait(barrier, len(partners))


class Summing:
    steps = ((3, 1), (1, 1), (2, 1), (0, 1), (0, 2))

    def __init__(self, running, came, sent, got):
        self.running, self.came, self.sent, self.got = running, came, sent, got
        self.copies = []

    def start(self):
        index = len(self.copies)
        digit, bit = self.steps[index]
        if digit == 0:
            z = where_am_i()[0]
            partner = {"dp": z + bit - 2 * bit * ((z // bit) % 2)}
        else:
            partner = neighbour(digit)
        copy = pltpu.make_async_remote_copy(
            src_ref=self.running.at[index],
            dst_ref=self.came.at[index],
            send_sem=self.sent.at[index],
            recv_sem=self.got.at[index],
            device_id=partner,
            device_id_type=MESH,
        )
        copy.start()
        self.copies.append(copy)

    def end(self):
        index = len(self.copies) - 1
        self.copies[index].wait()
        self.running[index + 1] = self.running[index] + self.came[index]


def summing_scratch(shape):
    return [
        pltpu.VMEM((6,) + shape, f32),
        pltpu.VMEM((5,) + shape, f32),
        pltpu.SemaphoreType.DMA((5,)),
        pltpu.SemaphoreType.DMA((5,)),
    ]


def small_sum_kernel(values, out, over_fsdp, over_seq, over_dp, sents, gots):
    axes = (("fsdp", 4, over_fsdp), ("seq", 2, over_seq), ("dp", 4, over_dp))
    partner = lambda axis, size, away: {axis: (lax.axis_index(axis) + away) % size}
    barrier = pltpu.get_barrier_semaphore()
    for axis, size, slots in axes:
        for away in range(1, size):
            pl.semaphore_signal(
                barrier, inc=1, device_id=partner(axis, size, away), device_id_type=MESH
            )
    pl.semaphore_wait(barrier, sum(size - 1 for axis, size, slots in axes))
    running = values[...]
    for stage, (axis, size, slots) in enumerate(axes):
        me = lax.axis_index(axis)
        slots[me] = running
        copies = [
            pltpu.make_async_remote_copy(
                src_ref=slots.at[me],
                dst_ref=slots.at[me],
                send_sem=sents.at[stage, away - 1],
                recv_sem=gots.at[stage, away - 1],
                device_id=partner(axis, size, away),
                device_id_type=MESH,
            )
            for away in range(1, size)
        ]
        for copy in copies:
            copy.start()
        for copy in copies:
            copy.wait()
        running = slots[0]
        for index in range(1, size):
            running = running + slots[index]
    out[...] = running


def small_sum(values):
    slots = lambda size: pltpu.VMEM((size,) + values.shape, f32)
    return pl.pallas_call(
        small_sum_kernel,
        out_shape=jax.ShapeDtypeStruct(values.shape, f32),
        in_specs=[pl.BlockSpec(memory_space=pltpu.VMEM)],
        out_specs=pl.BlockSpec(memory_space=pltpu.VMEM),
        scratch_shapes=[
            slots(4),
            slots(2),
            slots(4),
            pltpu.SemaphoreType.DMA((3, 3)),
            pltpu.SemaphoreType.DMA((3, 3)),
        ],
        compiler_params=pltpu.CompilerParams(collective_id=2, has_side_effects=True),
        name="small_sum",
    )(values)


def spread_kernel(chunks, arrays, *refs):
    sources, values, targets, out = refs[:arrays], refs[arrays], refs[arrays + 1 : -10], refs[-10]
    running, came, sent, got, own_sem, z_sent, z_got, far_sent, far_got = refs[-9:]
    z, x, y, core = where_am_i()
    running[0] = values[...]
    greet()
    total = Summing(running, came, sent, got)
    total.start()
    own = []
    for index in range(arrays):
        copy = pltpu.make_async_copy(
            sources[index], targets[index].at[z, x, y, core], own_sem.at[index]
        )
        copy.start()
        own.append(copy)
    along = {}
    for chunk, (which, start, size, order) in enumerate(chunks):
        columns = pl.ds(start, size)
        for away in (1, 2, 3):
            copy = pltpu.make_async_remote_copy(
                src_ref=sources[which].at[:, columns],
                dst_ref=targets[which].at[z, x, y, core, :, columns],
                send_sem=z_sent.at[chunk, away - 1],
                recv_sem=z_got.at[chunk, away - 1],
                device_id=neighbour(0, away),
                device_id_type=MESH,
            )
            copy.start()
            along[chunk, away] = copy
    for copy in own:
        copy.wait()
    far = {}
    every = slice(None)
    for time in range(len(chunks) + 2):
        for stage in range(3):
            chunk = time - stage
            if not 0 <= chunk < len(chunks):
                continue
            which, start, size, order = chunks[chunk]
            if stage == 0:
                for away in (1, 2, 3):
                    along[chunk, away].wait_recv()
            else:
                far[chunk, stage - 1].wait_recv()
            at = [every, x, y, core]
            for digit in order[:stage]:
                at[digit] = every
            block = targets[which].at[(*at, every, pl.ds(start, size))]
            copy = pltpu.make_async_remote_copy(
                src_ref=block,
                dst_ref=block,
                send_sem=far_sent.at[chunk, stage],
                recv_sem=far_got.at[chunk, stage],
                device_id=neighbour(order[stage]),
                device_id_type=MESH,
            )
            copy.start()
            far[chunk, stage] = copy
        if time < 5:
            total.end()
            if time < 4:
                total.start()
    out[...] = running[5]
    for chunk in range(len(chunks)):
        far[chunk, 2].wait_recv()
        for away in (1, 2, 3):
            along[chunk, away].wait_send()
        for stage in range(3):
            far[chunk, stage].wait_send()


def spread_start(shards, values):
    share = shards[0].shape[0]
    orders = ((1, 2, 3), (2, 1, 3))
    chunks = []
    for which, shard in enumerate(shards):
        size = min(CHUNK, shard.shape[1])
        for start in range(0, shard.shape[1], size):
            chunks.append((which, start, size, orders[len(chunks) % 2]))
    count = len(chunks)
    grid = (4, 2, 2, 2, share)
    anywhere = pl.BlockSpec(memory_space=pl.ANY)
    near = pl.BlockSpec(memory_space=pltpu.VMEM)
    results = pl.pallas_call(
        functools.partial(spread_kernel, chunks, len(shards)),
        out_shape=[jax.ShapeDtypeStruct(grid + (shard.shape[1],), bf16) for shard in shards]
        + [jax.ShapeDtypeStruct(values.shape, f32)],
        in_specs=[anywhere] * len(shards) + [near],
        out_specs=[anywhere] * len(shards) + [near],
        scratch_shapes=summing_scratch(values.shape)
        + [pltpu.SemaphoreType.DMA((len(shards),))]
        + [pltpu.SemaphoreType.DMA((count, 3))] * 4,
        compiler_params=pltpu.CompilerParams(collective_id=0, has_side_effects=True),
        name="spread_start",
    )(*shards, values)
    return [whole.reshape(32 * share, whole.shape[-1]) for whole in results[:-1]], results[-1]


def fold_kernel(chunks, last, values, out_last, out, running, came, sent, got,
                part, part_one, part_two, got_core, got_one, got_two, got_z, sents, gots):
    place = where_am_i()
    z, core = place[0], place[3]
    running[0] = values[...]
    greet()
    total = Summing(running, came, sent, got)
    copies = {}
    every = slice(None)

    def send(chunk, stage, source, target, partner):
        copy = pltpu.make_async_remote_copy(
            src_ref=source,
            dst_ref=target,
            send_sem=sents.at[chunk, stage],
            recv_sem=gots.at[chunk, stage],
            device_id=partner,
            device_id_type=MESH,
        )
        copy.start()
        copies[chunk, stage] = copy

    def sum_of(left, right):
        return (left.astype(f32) + right.astype(f32)).astype(bf16)

    for chunk, (start, size, order) in enumerate(chunks):
        block = last.at[:, :, :, 1 - core, :, pl.ds(start, size)]
        send(chunk, 0, block, got_core.at[chunk], neighbour(3))
    total.start()
    for time in range(len(chunks) + 3):
        for stage in range(1, 5):
            chunk = time - stage + 1
            if not 0 <= chunk < len(chunks):
                continue
            start, size, order = chunks[chunk]
            columns = pl.ds(start, size)
            near, far = order
            if stage == 1:
                copies[chunk, 0].wait_recv()
                part[chunk] = sum_of(last[:, :, :, core, :, columns], got_core[chunk])
                at = [every, every, every]
                at[near] = 1 - place[near]
                send(chunk, 1, part.at[(chunk, *at)], got_one.at[chunk], neighbour(near))
            elif stage == 2:
                copies[chunk, 1].wait_recv()
                at = [every, every, every]
                at[near] = place[near]
                part_one[chunk] = sum_of(part[(chunk, *at)], got_one[chunk])
                send(
                    chunk, 2, part_one.at[chunk, :, 1 - place[far]], got_two.at[chunk], neighbour(far)
                )
            elif stage == 3:
                copies[chunk, 2].wait_recv()
                part_two[chunk] = sum_of(part_one[chunk, :, place[far]], got_two[chunk])
                for away in (1, 2, 3):
                    source = part_two.at[chunk, (z + away) % 4]
                    send(chunk, 2 + away, source, got_z.at[chunk, away - 1], neighbour(0, away))
            else:
                whole = part_two[chunk, z].astype(f32)
                for away in (1, 2, 3):
                    copies[chunk, 2 + away].wait_recv()
                    whole = whole + got_z[chunk, away - 1].astype(f32)
                out_last[:, columns] = whole
        if time < 5:
            total.end()
            if time < 4:
                total.start()
    for step in range(len(chunks) + 3, 5):
        total.end()
        if step < 4:
            total.start()
    out[...] = running[5]
    for chunk in range(len(chunks)):
        for stage in range(6):
            copies[chunk, stage].wait_send()


def fold_end(last, values):
    rows, wide = last.shape
    share = rows // 32
    size = 128
    orders = ((1, 2), (2, 1))
    chunks = [(start, size, orders[(start // size) % 2]) for start in range(0, wide, size)]
    count = len(chunks)
    near = pl.BlockSpec(memory_space=pltpu.VMEM)
    return pl.pallas_call(
        functools.partial(fold_kernel, chunks),
        out_shape=[
            jax.ShapeDtypeStruct((share, wide), f32),
            jax.ShapeDtypeStruct(values.shape, f32),
        ],
        in_specs=[near, near],
        out_specs=[near, near],
        scratch_shapes=summing_scratch(values.shape)
        + [
            pltpu.VMEM((count, 4, 2, 2, share, size), bf16),
            pltpu.VMEM((count, 4, 2, share, size), bf16),
            pltpu.VMEM((count, 4, share, size), bf16),
            pltpu.VMEM((count, 4, 2, 2, share, size), bf16),
            pltpu.VMEM((count, 4, 2, share, size), bf16),
            pltpu.VMEM((count, 4, share, size), bf16),
            pltpu.VMEM((count, 3, share, size), bf16),
            pltpu.SemaphoreType.DMA((count, 6)),
            pltpu.SemaphoreType.DMA((count, 6)),
        ],
        compiler_params=pltpu.CompilerParams(
            collective_id=1, has_side_effects=True, vmem_limit_bytes=VMEM_BYTES
        ),
        name="fold_end",
    )(last.reshape(4, 2, 2, 2, share, wide), values)


class Ride:
    def __init__(self, arrays, lanes, columns, steps, collective):
        rows = arrays[0].shape[0]
        self.share = rows // 32
        self.arrays = [array.reshape(4, 2, 2, 2, self.share, array.shape[1]) for array in arrays]
        self.lanes, self.columns, self.steps, self.collective = lanes, columns, steps, collective
        self.size = 128 if lanes else arrays[0].shape[1] // 2
        while columns % self.size or columns // self.size + 4 > steps:
            self.size += 128
        self.chunks = columns // self.size

    def in_specs(self):
        return [pl.BlockSpec(memory_space=pl.ANY)] * len(self.arrays)

    def out_specs(self):
        return [pl.BlockSpec((self.share, self.columns), lambda *place: (0, 0))] * 2

    def out_shape(self):
        return [jax.ShapeDtypeStruct((self.share, self.columns), f32)] * 2

    def scratch(self):
        tail = (self.share, self.size)
        whole, half, quarter = (4, 2, 2) + tail, (4, 2) + tail, (4,) + tail
        every = (2, self.chunks)
        return [
            pltpu.VMEM((2, 2) + whole, bf16),
            pltpu.VMEM(every + whole, bf16),
            pltpu.VMEM(every + half, bf16),
            pltpu.VMEM(every + quarter, bf16),
            pltpu.VMEM(every + (3,) + tail, bf16),
            pltpu.VMEM((2, 2) + whole, bf16),
            pltpu.VMEM((2, 2) + half, bf16),
            pltpu.VMEM((2, 2) + quarter, bf16),
            pltpu.SemaphoreType.DMA((2, 2)),
            pltpu.SemaphoreType.DMA(every + (6,)),
            pltpu.SemaphoreType.DMA(every + (6,)),
        ]

    def step(self, time, sources, outs, scratch):
        own, got_core, got_one, got_two, got_z, part, part_one, part_two, own_sem, sents, gots = scratch
        place = where_am_i()
        z, core = place[0], place[3]
        count, size = self.chunks, self.size
        every = slice(None)

        def sum_of(left, right):
            return (left.astype(f32) + right.astype(f32)).astype(bf16)

        def block_of(lane, chunk, array, which):
            if self.lanes:
                array, base = self.lanes[lane]
                columns = pl.ds(pl.multiple_of(base + chunk * size, 128), size)
            else:
                columns = pl.ds(lane * size, size)
            return sources[array].at[:, :, :, which, :, columns]

        def copy_of(lane, chunk, stage, array=0):
            near, far = ((1, 2), (2, 1))[lane]
            slot = chunk % 2
            if stage == 0:
                source = block_of(lane, chunk, array, 1 - core)
                target, partner = got_core.at[lane, chunk], neighbour(3)
            elif stage == 1:
                at = [every, every, every]
                at[near] = 1 - place[near]
                source, target = part.at[(lane, slot, *at)], got_one.at[lane, chunk]
                partner = neighbour(near)
            elif stage == 2:
                source = part_one.at[lane, slot, :, 1 - place[far]]
                target, partner = got_two.at[lane, chunk], neighbour(far)
            else:
                away = stage - 2
                source = part_two.at[lane, slot, (z + away) % 4]
                target, partner = got_z.at[lane, chunk, away - 1], neighbour(0, away)
            return pltpu.make_async_remote_copy(
                src_ref=source,
                dst_ref=target,
                send_sem=sents.at[lane, chunk, stage],
                recv_sem=gots.at[lane, chunk, stage],
                device_id=partner,
                device_id_type=MESH,
            )

        def own_copy(lane, chunk, array=0):
            source = block_of(lane, chunk, array, core)
            slot = chunk % 2
            return pltpu.make_async_copy(source, own.at[lane, slot], own_sem.at[lane, slot])

        @pl.when(time == 0)
        def _():
            greet()

        for lane in range(2):
            near, far = ((1, 2), (2, 1))[lane]

            for array in range(1 if self.lanes else len(sources)):

                @pl.when((time < count) if self.lanes else (time == array))
                def _():
                    copy_of(lane, time, 0, array).start()
                    own_copy(lane, time, array).start()

            @pl.when((time >= 1) & (time < count + 1))
            def _():
                chunk = time - 1
                own_copy(lane, chunk).wait()
                copy_of(lane, chunk, 0).wait()

                @pl.when(chunk >= 2)
                def _():
                    copy_of(lane, chunk - 2, 1).wait_send()

                part[lane, chunk % 2] = sum_of(own[lane, chunk % 2], got_core[lane, chunk])
                copy_of(lane, chunk, 1).start()

            @pl.when((time >= 2) & (time < count + 2))
            def _():
                chunk = time - 2
                copy_of(lane, chunk, 1).wait_recv()

                @pl.when(chunk >= 2)
                def _():
                    copy_of(lane, chunk - 2, 2).wait_send()

                at = [every, every, every]
                at[near] = place[near]
                mine = part[(lane, chunk % 2, *at)]
                part_one[lane, chunk % 2] = sum_of(mine, got_one[lane, chunk])
                copy_of(lane, chunk, 2).start()

            @pl.when((time >= 3) & (time < count + 3))
            def _():
                chunk = time - 3
                copy_of(lane, chunk, 2).wait_recv()

                @pl.when(chunk >= 2)
                def _():
                    for away in (1, 2, 3):
                        copy_of(lane, chunk - 2, 2 + away).wait_send()

                mine = part_one[lane, chunk % 2, :, place[far]]
                part_two[lane, chunk % 2] = sum_of(mine, got_two[lane, chunk])
                for away in (1, 2, 3):
                    copy_of(lane, chunk, 2 + away).start()

            @pl.when((time >= 4) & (time < count + 4))
            def _():
                chunk = time - 4
                whole = part_two[lane, chunk % 2, z].astype(f32)
                for away in (1, 2, 3):
                    copy_of(lane, chunk, 2 + away).wait_recv()
                    whole = whole + got_z[lane, chunk, away - 1].astype(f32)
                outs[lane][:, pl.ds(pl.multiple_of(chunk * size, 128), size)] = whole

        @pl.when(time == self.steps - 1)
        def _():
            for lane in range(2):
                for chunk in range(max(count - 2, 0), count):
                    for stage in range(1, 6):
                        copy_of(lane, chunk, stage).wait_send()


class NoRide:
    arrays = ()
    collective = None
    in_specs = out_specs = out_shape = scratch = lambda self: []

    def step(self, *unused):
        pass


class Links:
    def __init__(self, sizes):
        self.plain = sizes != (4, 2, 4)

    def start(self, shards, values):
        if not self.plain:
            return spread_start(shards, values)
        gather = lambda shard: lax.all_gather(shard, ALL, axis=0, tiled=True)
        return [gather(shard) for shard in shards], lax.psum(values, ALL)

    def ride(self, arrays, lanes, columns, steps, collective):
        return NoRide() if self.plain else Ride(arrays, lanes, columns, steps, collective)

    def scatter(self, values, done):
        if not self.plain:
            return jnp.concatenate(done, 1)
        return lax.psum_scatter(values, ALL, scatter_dimension=0, tiled=True).astype(f32)

    def end(self, last, values):
        if not self.plain:
            return fold_end(last, values)
        total = lax.psum_scatter(last, ALL, scatter_dimension=0, tiled=True).astype(f32)
        return total, lax.psum(values, ALL)

    def total(self, values):
        return lax.psum(values, ALL) if self.plain else small_sum(values)


def entry_kernel(query_blocks, field, embed, weight, mod, stream, hidden, mixed):
    width = embed.shape[0]
    halves = halves_of(field.shape[0])
    starts = [contract(field[rows, :], embed[...], 1, 1) for rows in halves]
    lows = []
    for rows, stream_zero in zip(halves, starts):
        stream[rows, :] = stream_zero
        normed, unused = layer_norm(stream_zero)
        lows.append((normed * (1.0 + mod[1:2, :]) + mod[0:1, :]).astype(bf16))
        hidden[rows, :] = lows[-1]
        for part in (1, 2):
            columns = pl.ds(part * width, width)
            mixed[rows, columns] = contract(lows[-1], weight[:, columns], 1, 0).astype(bf16)

    @pl.when(pl.program_id(0) < query_blocks)
    def _():
        queries = contract(hidden[...], weight[:, 0:width], 1, 0)
        mixed[:, 0:width] = (queries * QUERY_SCALE).astype(bf16)


def entry(fields, embed, weight, mod, block, query_blocks, unit_of, place_of, rows, into):
    count, pieces = fields.shape
    width = embed.shape[0]
    given = len(into)
    placed = lambda columns: pl.BlockSpec((block, columns), lambda i: (place_of(i), 0))

    def kernel(*refs):
        entry_kernel(query_blocks, *(refs[:4] + refs[4 + given :]))

    return pl.pallas_call(
        kernel,
        grid=(count // block,),
        in_specs=[
            pl.BlockSpec((block, pieces), lambda i: (i, 0)),
            resident(embed.shape),
            resident(weight.shape),
            pl.BlockSpec((None,) + mod.shape[1:], lambda i: (unit_of(i), 0, 0)),
        ]
        + [pl.BlockSpec(memory_space=pl.ANY)] * given,
        out_specs=[placed(width), placed(width), placed(3 * width)],
        out_shape=[
            jax.ShapeDtypeStruct((rows, width), f32),
            jax.ShapeDtypeStruct((rows, width), bf16),
            jax.ShapeDtypeStruct((rows, 3 * width), bf16),
        ],
        input_output_aliases={4 + index: index for index in range(given)},
        cost_estimate=pl.CostEstimate(
            flops=8 * count * width * width, bytes_accessed=12 * count * width, transcendentals=0
        ),
        compiler_params=pltpu.CompilerParams(vmem_limit_bytes=VMEM_BYTES),
        name="entry",
    )(fields, embed, weight, mod, *into)


def crossed():
    row = lax.broadcasted_iota(jnp.int32, (2 * HD, 2 * HD), 0) < HD
    column = lax.broadcasted_iota(jnp.int32, (2 * HD, 2 * HD), 1) < HD
    return jnp.where(row != column, 1.0, 0.0).astype(bf16)


def attend_kernel(sub, query, key, value, out, kept, inverse, value_t, key_one, stats):
    block, keys = query.shape[0], key.shape[0]
    zero, one = jnp.zeros((), bf16), jnp.ones((), bf16)

    @pl.when(pl.program_id(1) == 0)
    def _():
        turned = jnp.transpose(value[...])
        first_rows = lax.broadcasted_iota(jnp.int32, (2 * HD, keys), 0) < HD
        value_t[0] = jnp.where(first_rows, turned, one)
        value_t[1] = jnp.where(first_rows, one, turned)
        first_lanes = lax.broadcasted_iota(jnp.int32, (keys, 2 * HD), 1) < HD
        both = key[...]
        key_one[0] = jnp.where(first_lanes, both, one)
        key_one[1] = jnp.where(first_lanes, one, both)
        wide = both.astype(f32)
        mean = jnp.mean(wide, 0, keepdims=True)
        spread = ((wide - mean) * (wide - mean)).astype(bf16)
        stats[0:1] = mean
        far = jnp.max(contract(spread, crossed(), 1, 0), 0, keepdims=True)
        stats[1:2] = 0.5 * jnp.sqrt(far)

    lanes = lax.broadcasted_iota(jnp.int32, (sub, 2 * HD), 1)
    wide = query[...].astype(f32)
    length = jnp.sqrt(contract((wide * wide).astype(bf16), crossed(), 1, 0))
    reach = length * stats[1:2]
    shifts = (-contract((wide * stats[0:1]).astype(bf16), crossed(), 1, 0) - reach).astype(bf16)
    near = jnp.max(reach) <= 60.0
    upper = lax.broadcasted_iota(jnp.int32, (2 * HD, sub), 0) < HD

    def run(exact):
        for part in range(block // sub):
            rows = pl.ds(part * sub, sub)
            results = []
            for head in range(2):
                mine = (lanes < HD) if head == 0 else (lanes >= HD)
                if exact:
                    moved = jnp.where(mine, query[rows, :], zero)
                    scores = contract(key_one[head], moved, 1, 1)
                    scores = scores - jnp.max(scores, 0, keepdims=True)
                else:
                    free = HD if head == 0 else 0
                    rest = jnp.where(lanes == free, shifts[part * sub : part * sub + sub], zero)
                    moved = jnp.where(mine, query[rows, :], rest)
                    scores = contract(key_one[head], moved, 1, 1)
                weights = jnp.exp2(scores).astype(bf16)
                kept[head, :, rows] = weights
                results.append(contract(value_t[head], weights, 1, 0))
            total = jnp.where(
                upper, pltpu.roll(results[0], HD, 0), pltpu.roll(results[1], HD, 0)
            )
            above = 1.0 / total
            mean = jnp.where(upper, results[0], results[1]) * above
            out[rows, :] = jnp.transpose(mean).astype(bf16)
            inverse[0:1, rows] = above[0:1]
            inverse[1:2, rows] = above[HD : HD + 1]

    @pl.when(near)
    def _():
        run(False)

    @pl.when(jnp.logical_not(near))
    def _():
        run(True)


def attend(queries, memory, places, block, sub, count, keys, width, into, rows):
    pairs = width // (2 * HD)
    query_at, key_at, key_column, value_column = places
    given = len(into)

    def kernel(*refs):
        attend_kernel(sub, *(refs[:3] + refs[3 + given :]))

    return pl.pallas_call(
        kernel,
        grid=(pairs, count // block),
        in_specs=[
            pl.BlockSpec((block, 2 * HD), lambda h, i: (query_at // block + i, h)),
            pl.BlockSpec((keys, 2 * HD), lambda h, i: (key_at // keys, key_column * pairs + h)),
            pl.BlockSpec((keys, 2 * HD), lambda h, i: (key_at // keys, value_column * pairs + h)),
        ]
        + [pl.BlockSpec(memory_space=pl.ANY)] * given,
        out_specs=[
            pl.BlockSpec((block, 2 * HD), lambda h, i: (query_at // block + i, h)),
            pl.BlockSpec((None, None, 2, keys, block), lambda h, i: (h, i, 0, 0, 0)),
            pl.BlockSpec((None, 2, block), lambda h, i: (h, 0, i)),
        ],
        out_shape=[
            jax.ShapeDtypeStruct((rows, width), bf16),
            jax.ShapeDtypeStruct((pairs, count // block, 2, keys, block), bf16),
            jax.ShapeDtypeStruct((pairs, 2, count), f32),
        ],
        scratch_shapes=[
            pltpu.VMEM((2, 2 * HD, keys), bf16),
            pltpu.VMEM((2, keys, 2 * HD), bf16),
            pltpu.VMEM((8, 2 * HD), f32),
        ],
        cost_estimate=pl.CostEstimate(
            flops=20 * count * keys * width, bytes_accessed=2 * count * keys, transcendentals=0
        ),
        compiler_params=pltpu.CompilerParams(vmem_limit_bytes=VMEM_BYTES),
        input_output_aliases={3: 0} if given else {},
        name="attend",
    )(queries, memory, memory, *into)


def attend_back_kernel(
    sub, query, key, value, grad, out, kept, inverse,
    grad_query, grad_key, grad_value, key_t, value_one, key_sum, value_sum,
):
    block, keys = query.shape[0], key.shape[0]
    step, steps = pl.program_id(1), pl.num_programs(1)
    zero = jnp.zeros((), bf16)

    @pl.when(step == 0)
    def _():
        first_rows = lax.broadcasted_iota(jnp.int32, (2 * HD, keys), 0) < HD
        turned = jnp.transpose(key[...])
        key_t[0] = jnp.where(first_rows, turned, zero)
        key_t[1] = jnp.where(first_rows, zero, turned)
        first_lanes = lax.broadcasted_iota(jnp.int32, (keys, 2 * HD), 1) < HD
        minus = jnp.full((), -1.0, bf16)
        value_one[0] = jnp.where(first_lanes, value[...], minus)
        value_one[1] = jnp.where(first_lanes, minus, value[...])
        key_sum[...] = jnp.zeros_like(key_sum)
        value_sum[...] = jnp.zeros_like(value_sum)

    lanes = lax.broadcasted_iota(jnp.int32, (sub, 2 * HD), 1)
    places = lax.broadcasted_iota(jnp.int32, (2 * HD, sub), 0)
    upper = places < HD
    for part in range(block // sub):
        rows = pl.ds(part * sub, sub)
        above = jnp.where(upper, inverse[0:1, rows], inverse[1:2, rows])
        scaled = (jnp.transpose(grad[rows, :].astype(f32)) * above).astype(bf16)
        product = scaled.astype(f32) * jnp.transpose(out[rows, :].astype(f32))
        natural = jnp.transpose(scaled)
        queries = query[rows, :]
        turned = None
        for head in range(2):
            delta = jnp.sum(product[HD * head : HD * head + HD], 0, keepdims=True)
            high = delta.astype(bf16)
            rest = (delta - high.astype(f32)).astype(bf16)
            free = HD if head == 0 else 0
            mine = upper if head == 0 else jnp.logical_not(upper)
            extra = jnp.where(places == free, high, jnp.where(places == free + 1, rest, zero))
            grad_probs = contract(value_one[head], jnp.where(mine, scaled, extra), 1, 0)
            weights = kept[head, :, rows]
            grad_scores = grad_probs.astype(bf16) * weights
            own = (lanes < HD) if head == 0 else (lanes >= HD)
            value_sum[...] += contract(weights, jnp.where(own, natural, zero), 1, 0)
            key_sum[...] += contract(grad_scores, jnp.where(own, queries, zero), 1, 0)
            term = contract(key_t[head], grad_scores, 1, 0)
            turned = term if turned is None else turned + term
        grad_query[rows, :] = (jnp.transpose(turned) * 0.125).astype(bf16)

    @pl.when(step == steps - 1)
    def _():
        grad_key[...] = (key_sum[...] * LN2).astype(bf16)
        grad_value[...] = value_sum[...].astype(bf16)


def attend_back(queries, memory, grads, out, kept, inverse, places, block, sub, into, shapes, ride):
    query_at, key_at, key_column, value_column, grad_query_at, grad_key_at = places
    count, keys = kept.shape[1] * kept.shape[4], kept.shape[3]
    pairs = out.shape[1] // (2 * HD)
    two = 2 * HD
    steps = count // block
    given, riding = len(into), len(ride.arrays)

    def kernel(*refs):
        ins, refs = refs[:7], refs[7 + given :]
        sources, refs = refs[:riding], refs[riding:]
        outs, refs = refs[:3], refs[3:]
        sums, refs = refs[: 2 * bool(riding)], refs[2 * bool(riding) :]
        ride.step(pl.program_id(0) * steps + pl.program_id(1), sources, sums, refs[4:])
        attend_back_kernel(sub, *ins, *outs, *refs[:4])

    work = pairs * count * keys * two
    results = pl.pallas_call(
        kernel,
        grid=(pairs, steps),
        in_specs=[
            pl.BlockSpec((block, two), lambda h, i: (query_at // block + i, h)),
            pl.BlockSpec((keys, two), lambda h, i: (key_at // keys, key_column * pairs + h)),
            pl.BlockSpec((keys, two), lambda h, i: (key_at // keys, value_column * pairs + h)),
            pl.BlockSpec((block, two), lambda h, i: (query_at // block + i, h)),
            pl.BlockSpec((block, two), lambda h, i: (query_at // block + i, h)),
            pl.BlockSpec((None, None, 2, keys, block), lambda h, i: (h, i, 0, 0, 0)),
            pl.BlockSpec((None, 2, block), lambda h, i: (h, 0, i)),
        ]
        + [pl.BlockSpec(memory_space=pl.ANY)] * given
        + ride.in_specs(),
        out_specs=[
            pl.BlockSpec((block, two), lambda h, i: (grad_query_at // block + i, h)),
            pl.BlockSpec((keys, two), lambda h, i: (grad_key_at // keys, h)),
            pl.BlockSpec((keys, two), lambda h, i: (grad_key_at // keys, h)),
        ]
        + ride.out_specs(),
        out_shape=[jax.ShapeDtypeStruct(shape, bf16) for shape in shapes] + ride.out_shape(),
        scratch_shapes=[
            pltpu.VMEM((2, two, keys), bf16),
            pltpu.VMEM((2, keys, two), bf16),
            pltpu.VMEM((keys, two), f32),
            pltpu.VMEM((keys, two), f32),
        ]
        + ride.scratch(),
        input_output_aliases={7 + index: index for index in range(given)},
        cost_estimate=pl.CostEstimate(flops=32 * work, bytes_accessed=4 * work // HD, transcendentals=0),
        compiler_params=pltpu.CompilerParams(
            vmem_limit_bytes=VMEM_BYTES,
            collective_id=ride.collective,
            has_side_effects=riding > 0,
        ),
        name="attend_back",
    )(queries, memory, memory, grads, out, kept, inverse, *into, *ride.arrays)
    return results[:3], results[3:]


def middle_kernel(
    parts, attended, stream, target, weight_rows, mod, combine, first, second, read,
    hidden, active, grad_two, grad_inner, final, grad_read, grad_one, grad_attended, grad_stream,
    sums, losses, slopes,
):
    block = attended.shape[0]
    width, spread = first.shape
    size_tile = min(TILE, spread)
    tiles = [pl.ds(start, size_tile) for start in range(0, spread, size_tile)]
    gate_a, shift_b, scale_b = mod[2:3, :], mod[3:4, :], mod[4:5, :]
    gate_b, gain = mod[5:6, :], mod[6:7, :]

    def run(rows, found):
        branch_a = contract(attended[rows, :], combine[...], 1, 0)
        yield
        stream_one = stream[rows, :] + gate_a * branch_a
        norm_b, inverse_b = layer_norm(stream_one)
        low = (norm_b * (1.0 + scale_b) + shift_b).astype(bf16)
        hidden[rows, :] = low
        yield
        branch_b = None
        ahead = contract(low, first[:, tiles[0]], 1, 0)
        for index, tile in enumerate(tiles):
            inner = ahead
            if index + 1 < len(tiles):
                ahead = contract(low, first[:, tiles[index + 1]], 1, 0)
            yield
            value, slope = gelu_pair(inner)
            value = value.astype(bf16)
            active[rows, tile] = value
            slopes[rows, tile] = slope.astype(bf16)
            term = contract(value, second[:, tile], 1, 1)
            branch_b = term if branch_b is None else branch_b + term
            yield
        norm_c, inverse_c = layer_norm(stream_one + gate_b * branch_b)
        last = (norm_c * gain).astype(bf16)
        final[rows, :] = last
        yield
        diff = contract(last, read[...], 1, 0) - target[rows, :].astype(f32)
        found[0] = column_sum(weight_rows[rows, 0:1] * diff * diff)
        grad_low = (weight_rows[rows, 1:2] * diff).astype(bf16)
        grad_read[rows, :] = grad_low
        grad_final = contract(grad_low, read[...], 1, 1)
        yield
        found[6] = column_sum(grad_final * norm_c)
        grad = norm_back(grad_final * gain, norm_c, inverse_c)
        found[5] = column_sum(grad * branch_b)
        back = (grad * gate_b).astype(bf16)
        grad_two[rows, :] = back
        yield
        grad_hidden = None
        ahead = contract(back, second[:, tiles[0]], 1, 0)
        for index, tile in enumerate(tiles):
            inner = ahead
            if index + 1 < len(tiles):
                ahead = contract(back, second[:, tiles[index + 1]], 1, 0)
            yield
            inner = (inner * slopes[rows, tile].astype(f32)).astype(bf16)
            grad_inner[rows, tile] = inner
            term = contract(inner, first[:, tile], 1, 1)
            grad_hidden = term if grad_hidden is None else grad_hidden + term
            yield
        found[3] = column_sum(grad_hidden)
        found[4] = column_sum(grad_hidden * norm_b)
        grad = grad + norm_back(grad_hidden * (1.0 + scale_b), norm_b, inverse_b)
        grad_stream[rows, :] = grad
        found[2] = column_sum(grad * branch_a)
        back = (grad * gate_a).astype(bf16)
        grad_one[rows, :] = back
        yield
        grad_attended[rows, :] = contract(back, combine[...], 1, 1).astype(bf16)

    size = block // parts
    found = [{} for part in range(parts)]
    runs = [run(pl.ds(part * size, size), found[part]) for part in range(parts)]
    while runs:
        runs = [one for one in runs if next(one, runs) is not runs]
    losses[...] = jnp.broadcast_to(sum(one[0] for one in found), losses.shape)
    for row in (2, 3, 4, 5, 6):
        sums[row : row + 1, :] = sum(one[row] for one in found)
    sums[0:2, :] = jnp.zeros((2, width), f32)
    sums[7:8, :] = jnp.zeros((1, width), f32)


def middle(attended, stream, target, weight_rows, mod, combine, first, second, read, block, unit_of):
    rows, width = attended.shape
    spread, pieces = first.shape[1], read.shape[1]
    blocks = rows // block
    by_row = lambda columns: pl.BlockSpec((block, columns), lambda i: (i, 0))
    shape = lambda columns, kind: jax.ShapeDtypeStruct((rows, columns), kind)
    outs = (
        (width, bf16), (spread, bf16), (width, bf16), (spread, bf16), (width, bf16), (pieces, bf16),
        (width, bf16), (width, bf16), (width, f32),
    )
    return pl.pallas_call(
        functools.partial(middle_kernel, 1),
        grid=(blocks,),
        in_specs=[
            by_row(width),
            by_row(width),
            by_row(pieces),
            by_row(2),
            pl.BlockSpec((None,) + mod.shape[1:], lambda i: (unit_of(i), 0, 0)),
            resident(combine.shape),
            resident(first.shape),
            resident(second.shape),
            resident(read.shape),
        ],
        out_specs=[by_row(columns) for columns, kind in outs]
        + [
            pl.BlockSpec((None, 8, width), lambda i: (i, 0, 0)),
            pl.BlockSpec((None, 8, pieces), lambda i: (i, 0, 0)),
        ],
        out_shape=[shape(columns, kind) for columns, kind in outs]
        + [
            jax.ShapeDtypeStruct((blocks, 8, width), f32),
            jax.ShapeDtypeStruct((blocks, 8, pieces), f32),
        ],
        scratch_shapes=[pltpu.VMEM((block, spread), bf16)],
        cost_estimate=pl.CostEstimate(
            flops=60 * rows * width * width, bytes_accessed=40 * rows * width, transcendentals=0
        ),
        compiler_params=pltpu.CompilerParams(vmem_limit_bytes=VMEM_BYTES),
        name="middle",
    )(attended, stream, target, weight_rows, mod, combine, first, second, read)


def leave_kernel(query_blocks, grad_query, grad_key, grad_value, stream, grad_stream, weight, mod, out, sums, held):
    width = stream.shape[1]
    asks = pl.program_id(0) < query_blocks
    columns = lambda kind: pl.ds(kind * width, width)

    @pl.when(asks)
    def _():
        held[...] = contract(grad_query[...], weight[:, columns(0)], 1, 1)

    @pl.when(jnp.logical_not(asks))
    def _():
        held[...] = jnp.zeros_like(held)

    halves = halves_of(stream.shape[0])
    hidden = []
    for rows in halves:
        total = held[rows, :] + contract(grad_key[rows, :], weight[:, columns(1)], 1, 1)
        hidden.append(total + contract(grad_value[rows, :], weight[:, columns(2)], 1, 1))
    plain, scaled = [], []
    for rows, grad_hidden in zip(halves, hidden):
        normed, inverse = layer_norm(stream[rows, :])
        plain.append(column_sum(grad_hidden))
        scaled.append(column_sum(grad_hidden * normed))
        grad = norm_back(grad_hidden * (1.0 + mod[1:2, :]), normed, inverse)
        grad = grad + jnp.where(asks, grad_stream[rows, :], 0.0)
        out[rows, :] = grad.astype(bf16)
    sums[0:1, :] = sum(plain)
    sums[1:2, :] = sum(scaled)
    sums[2:8, :] = jnp.zeros((6, width), f32)


def leave(grads, stream, grad_stream, weight, mod, block, unit_of, ride):
    rows, width = stream.shape
    asking = grads[0].shape[0] // block
    blocks, riding = rows // block, len(ride.arrays)
    by_row = pl.BlockSpec((block, width), lambda i: (i, 0))
    asked = pl.BlockSpec((block, width), lambda i: (jnp.minimum(i, asking - 1), 0))

    def kernel(*refs):
        ins, refs = refs[:7], refs[7:]
        sources, refs = refs[:riding], refs[riding:]
        outs, refs = refs[:2], refs[2:]
        shards, refs = refs[: 2 * bool(riding)], refs[2 * bool(riding) :]
        ride.step(pl.program_id(0), sources, shards, refs[1:])
        leave_kernel(asking, *ins, *outs, refs[0])

    results = pl.pallas_call(
        kernel,
        grid=(blocks,),
        in_specs=[
            asked,
            by_row,
            by_row,
            by_row,
            asked,
            resident(weight.shape),
            pl.BlockSpec((None,) + mod.shape[1:], lambda i: (unit_of(i), 0, 0)),
        ]
        + ride.in_specs(),
        out_specs=[by_row, pl.BlockSpec((None, 8, width), lambda i: (i, 0, 0))] + ride.out_specs(),
        out_shape=[
            jax.ShapeDtypeStruct((rows, width), bf16),
            jax.ShapeDtypeStruct((blocks, 8, width), f32),
        ]
        + ride.out_shape(),
        scratch_shapes=[pltpu.VMEM((block, width), f32)] + ride.scratch(),
        cost_estimate=pl.CostEstimate(
            flops=7 * rows * width * width, bytes_accessed=16 * rows * width, transcendentals=0
        ),
        compiler_params=pltpu.CompilerParams(
            vmem_limit_bytes=VMEM_BYTES,
            collective_id=ride.collective,
            has_side_effects=riding > 0,
        ),
        name="leave",
    )(*grads, stream, grad_stream, weight, mod, *ride.arrays)
    return results[:2], results[2:]


def adam(master, first, second, grad, factor, step_rate):
    grad = grad * factor
    first_new = beta_one * first + (1.0 - beta_one) * grad
    second_new = beta_two * second + (1.0 - beta_two) * grad * grad
    corrected = (
        first_new
        / (1.0 - beta_one**STEP)
        / (jnp.sqrt(second_new / (1.0 - beta_two**STEP)) + epsilon)
    )
    return (master - step_rate * (corrected + decay * master), first_new, second_new)


def largest(limit, *sizes):
    block = limit
    while any(size % block for size in sizes):
        block //= 2
    return block


def body(sizes, *args):
    ways = sizes[1]
    links = Links(sizes)
    fields, targets, interval, storm_index, valid_count, latitude, storm_scale = args[:7]
    masters, firsts, seconds = args[7:15], args[15:23], args[23:31]
    embedding, intervals, modulator, projector, combiner, feedforward, readout, vectors = masters
    micros, samples_dev, part, pieces = fields.shape
    patches = latitude.shape[0]
    units = micros * samples_dev
    share, width = projector.shape[0], projector.shape[1] // 3
    place = lax.axis_index("seq")
    device = lax.axis_index(ALL)
    sample_start = lax.axis_index(("dp", "fsdp")) * samples_dev
    ring = [(index, 1 - index) for index in range(2)]
    alone = units // 2 if ways == 2 else 0
    shared = units - ways * alone
    have = alone + shared

    def local(values):
        cut = lax.dynamic_slice_in_dim(values, sample_start, samples_dev, 1)
        cut = cut.reshape((units,) + values.shape[2:])
        mine = [lax.dynamic_slice_in_dim(cut, place * alone, alone, 0)] if alone else []
        return jnp.concatenate(mine + [cut[ways * alone :]], 0)

    kinds = local(interval)

    def widen(values):
        flat = values.reshape(units, part, pieces)
        return jnp.pad(flat, ((0, 0), (0, 0), (0, WIDE - pieces)))

    def flatten(parts):
        return jnp.concatenate([piece.reshape(-1, WIDE) for piece in parts], 0)

    def pick(values, start):
        return lax.dynamic_slice_in_dim(values, start, alone, 0)

    own = widen(fields)
    if alone:
        sent = jnp.concatenate([pick(own, (1 - place) * alone), own[2 * alone :]], 0)
        came = lax.ppermute(sent, "seq", ring)
        own = jnp.concatenate([pick(own, place * alone), own[2 * alone :]], 0)
        others = flatten([came])
        all_rows = [own[:alone], came[:alone]]
        all_rows = flatten([jnp.concatenate(all_rows, 1), own[alone:], came[alone:]])
        own = flatten([own])
    else:
        if ways > 1:
            everyone = lax.all_gather(own, "seq", axis=1, tiled=True)
            own = flatten([own, jnp.roll(everyone, -place * part, 1)[:, part:]])
        own = all_rows = own.reshape(-1, WIDE)

    def spread_goals(goal):
        if not alone:
            return flatten([goal])
        came = lax.ppermute(pick(goal, (1 - place) * alone), "seq", ring)
        whole = jnp.concatenate([pick(goal, place * alone), came], 1)
        return flatten([whole, goal[2 * alone :]])

    def weigh(latitude):
        everywhere = jnp.arange(patches, dtype=jnp.int32)
        mask = (everywhere[None, None, :] >= patches - valid_count[:, :, None]).astype(f32)
        levels = jnp.arange(storm_scale.shape[0], dtype=jnp.int32)
        storms = jnp.sum(jnp.where(storm_index[:, :, None] == levels, storm_scale, 0.0), -1)
        row_weights = latitude[None, None, :] * storms[:, :, None] * mask
        total = pieces * jnp.sum(row_weights)
        by_unit = jnp.roll(local(row_weights), -place * part, 1)
        flat = jnp.concatenate([by_unit[:alone].reshape(-1), by_unit[alone:, :part].reshape(-1)])
        return total, jnp.stack([flat, flat * (2.0 / total)], 1)

    asking = (alone * ways + shared) * part

    def unit_of(block):
        whole_blocks = alone * patches // block
        own_blocks = shared * part // block
        other = max((patches - part) // block, 1)

        def at(i):
            late = alone + (i - whole_blocks) // (part // block)
            later = alone + (i - whole_blocks - own_blocks) // other
            late = jnp.where(i < whole_blocks + own_blocks, late, later)
            return jnp.where(i < whole_blocks, i // (patches // block), late)

        return at

    low = [master.astype(bf16) for master in masters]
    step_vec = low[1].astype(f32)
    active = jax.nn.silu(step_vec)
    active_low = active.astype(bf16)
    table = contract(active_low, low[2], 1, 0)
    spread_vectors = lax.dynamic_update_slice(
        jnp.zeros((7, width), f32), low[7].astype(f32), (0, device * share)
    )
    to_wide = lambda values: jnp.pad(values, ((0, 0), (0, WIDE - pieces)))
    (embed, project, read), carried = links.start(
        (to_wide(low[0].T), low[3], to_wide(low[6])),
        jnp.concatenate([table.reshape(3 * 6 * width // 128, 128), spread_vectors.reshape(-1, 128)]),
    )
    nothing = carried[0, 0] * 0.0
    carried = carried.reshape(-1)
    table = carried[: table.size].reshape(DTK, 6, width)
    all_vectors = carried[table.size :].reshape(7, width)
    table = table + all_vectors[None, :6]
    chosen = sum(jnp.where(kinds[:, None, None] == kind, table[kind], 0.0) for kind in range(DTK))
    gain = jnp.broadcast_to(all_vectors[6], (have, 1, width))
    mod = jnp.concatenate([chosen, gain, jnp.zeros((have, 1, width), f32)], 1)

    gather = lambda values: lax.all_gather(values, ALL, axis=0, tiled=True)
    combine = gather(low[4])
    late = (feedforward[0], feedforward[1])
    first, second = [gather((shard + nothing).astype(bf16)) for shard in late]

    block = largest(512, part)
    rows_all = have * patches
    if alone:
        short, long = part // block, patches // block

        def placer(first_of_shared, shift):
            def at(i):
                unit = i // short
                late = first_of_shared // block + (unit - alone) * short
                return jnp.where(unit < alone, unit * long + shift, late) + i % short

            return at

        by_unit = lambda i: i // short
        stream, hidden_a, mixed = entry(
            own, embed, project, mod, block, have * short, by_unit, placer(alone * patches, 0), rows_all, ()
        )
        stream, hidden_a, mixed = entry(
            others, embed, project, mod, block, alone * short, by_unit, placer(asking, short), rows_all,
            (stream, hidden_a, mixed),
        )
    else:
        stream, hidden_a, mixed = entry(
            own, embed, project, mod, block, asking // block, unit_of(block), lambda i: i, rows_all, ()
        )
    mixed, targets, latitude = lax.optimization_barrier((mixed, targets, latitude))
    goal_rows = spread_goals(widen(targets))
    total_weight, weight_rows = weigh(latitude)

    calls = []
    for unit in range(have):
        if unit < alone:
            start = unit * patches
            calls.append((patches, mixed, (start, start, 1, 2)))
        else:
            start = alone * patches + (unit - alone) * part
            behind = asking + (unit - alone) * (patches - part)
            if shared == 1 and start % patches == 0:
                calls.append((part, mixed, (start, start, 1, 2)))
            else:
                joined = jnp.concatenate(
                    [
                        mixed[start : start + part, width:],
                        mixed[behind : behind + patches - part, width:],
                    ],
                    0,
                )
                calls.append((part, joined, (start, 0, 0, 1)))
    attended_rows, saved = (), []
    for count, memory, where in calls:
        block = largest(1024, count, where[0] if where[0] else count)
        attended_rows, kept, inverse = attend(
            mixed, memory, where, block, block, count, patches, width, attended_rows, asking
        )
        attended_rows = (attended_rows,)
        saved.append((kept, inverse))
    attended_rows = attended_rows[0]

    block = largest(256, part)
    (
        hidden_b, activated, grad_two, grad_inner, final, grad_read, grad_one, grad_attended,
        grad_stream, sums, losses,
    ) = middle(
        attended_rows, stream, goal_rows, weight_rows, mod, combine, first, second, read, block,
        unit_of(block),
    )
    units_mid = [unit_of(block)(jnp.int32(i)) for i in range(sums.shape[0])]
    loss_local = jnp.sum(losses[:, 0, :])

    summed = lambda left, right: contract(left, right, 0, 0).astype(bf16)
    grad_first, grad_second = summed(hidden_b, grad_inner), summed(grad_two, activated)
    grad_combine, grad_readout = summed(attended_rows, grad_one), summed(final, grad_read)
    rest = jnp.concatenate([grad_combine, grad_readout, jnp.zeros((width, WIDE // 3), bf16)], 1)
    rides = [((grad_first, grad_second), ((0, 0), (1, 0)), grad_first.shape[1])]
    rides += [((rest,), ((0, 0), (0, rest.shape[1] // 2)), rest.shape[1] // 2)]
    shapes = ((asking, width), (have * patches, width), (have * patches, width))
    into, done = (), []
    for unit, ((count, memory, where), (kept, inverse)) in enumerate(zip(calls, saved)):
        block = kept.shape[4]
        ride = NoRide()
        if unit < len(rides):
            steps = width // (2 * HD) * (count // block)
            ride = links.ride(*rides[unit], steps, 3 + unit)
        into, ridden = attend_back(
            mixed, memory, grad_attended, attended_rows, kept, inverse, where + (where[0], unit * patches),
            block, min(block, 256), into, shapes, ride,
        )
        done.append(ridden)
    shard_first = links.scatter(grad_first, done[0][:1])
    shard_second = links.scatter(grad_second, done[0][1:])
    shard_rest = links.scatter(rest, done[1])
    shard_combine, shard_read = shard_rest[:, :width], shard_rest[:, width : width + WIDE]
    if not (alone and shared <= 1):
        own_part = lambda values, unit, low_row, high_row: values[
            unit * patches + low_row : unit * patches + high_row
        ]
        into = (into[0],) + tuple(
            jnp.concatenate(
                [values[: alone * patches]]
                + [own_part(values, unit, 0, part) for unit in range(alone, have)]
                + [own_part(values, unit, part, patches) for unit in range(alone, have)],
                0,
            )
            for values in into[1:]
        )
    grad_project = [summed(hidden_a[:asking], into[0])] + [summed(hidden_a, part) for part in into[1:]]
    block = largest(512, part)
    ride = links.ride(grad_project, None, 3 * width // 2, stream.shape[0] // block, 5)
    (grad_zero, sums_a), ridden = leave(
        into, stream, grad_stream, project, mod, block, unit_of(block), ride
    )
    if links.plain:
        shard_project = links.scatter(jnp.concatenate(grad_project, 1), ridden)
    else:
        by_lane = jnp.stack([lane.reshape(share, 3, width // 2) for lane in ridden], 2)
        shard_project = by_lane.reshape(share, 3 * width)
    units_out = [unit_of(block)(jnp.int32(i)) for i in range(sums_a.shape[0])]
    grad_embed = summed(grad_zero, all_rows)

    by_block = jnp.concatenate([sums, sums_a], 0)
    kind_block = kinds[jnp.stack(units_mid + units_out)]
    grad_table = jnp.stack(
        [
            jnp.sum(jnp.where((kind_block == kind)[:, None, None], by_block, 0.0), 0)
            for kind in range(DTK)
        ]
    )
    loss_row = jnp.full((1, 128), loss_local)
    small = jnp.concatenate([grad_table[:, :7].reshape(-1, 128), loss_row])
    shard_embed, carried = links.end(grad_embed, small)
    loss_total = carried[-1, 0]
    grad_table = carried[:-1].reshape(DTK, 7, width)
    grad_mod = grad_table[:, :6].reshape(DTK, 6 * width)
    shard_vectors = lax.dynamic_slice_in_dim(jnp.sum(grad_table, 0), device * share, share, 1)
    active_wide = active_low.astype(f32)
    shard_modulator = sum(
        active_wide[kind][:, None] * grad_mod[kind][None, :] for kind in range(DTK)
    )
    grad_active = jnp.stack(
        [jnp.sum(low[2].astype(f32) * grad_mod[kind][None, :], 1) for kind in range(DTK)]
    )
    unused, silu_back = jax.vjp(jax.nn.silu, step_vec)
    shard_intervals = silu_back(grad_active)[0]

    shards = (
        shard_embed[:, :pieces].T,
        shard_intervals,
        shard_modulator,
        shard_project,
        shard_combine,
        jnp.stack([shard_first, shard_second]),
        shard_read[:, :pieces],
        shard_vectors,
    )
    squares = sum(jnp.sum(grad * grad) for grad in shards)
    squares = links.total(jnp.full((8, 128), squares))[0, 0]
    norm = jnp.sqrt(squares)
    factor = clip_norm / jnp.maximum(norm, clip_norm)
    results = [
        adam(master, first_moment, second_moment, grad, factor, rate)
        for master, first_moment, second_moment, grad, rate in zip(
            masters, firsts, seconds, shards, step_rates()
        )
    ]
    return tuple(result[index] for index in range(3) for result in results) + (
        loss_total,
        total_weight,
        norm,
    )


def solution(mesh):
    data = P(None, ("dp", "fsdp"), "seq", None)
    columns, rows = P(None, ALL), P(ALL, None)
    weights = (columns, columns, rows, rows, rows, P(None, ALL, None), rows, columns)
    return jax.shard_map(
        functools.partial(body, tuple(mesh.shape[axis] for axis in ALL)),
        mesh=mesh,
        in_specs=(data, data) + (P(),) * 5 + weights * 3,
        out_specs=weights * 3 + (P(),) * 3,
        check_vma=False,
    )
```
